32 devices in a mesh: wide: 4 (over y, x), narrow: 8 (over z, core).
Axes of the slice: x: 2, y: 2, z: 4, core: 2. Of those that a mesh axis runs over, the one named last changes fastest.
Arguments:
- tokens: bfloat16 [32, 1024, 768], P(('wide', 'narrow')), may hold values from -6 to 6
- split_point: int32 [32], P(('wide', 'narrow')), may hold values from 128 to 896
- cotangent: bfloat16 [32, 1024, 768], P(('wide', 'narrow')), may hold values from -6 to 6
- norm_gain: float32 [2, 2, 768], replicated, may hold values from 0.5 to 1.5
- norm_shift: float32 [2, 2, 768], replicated, may hold values from -1.75 to 1.75
- in_weight: bfloat16 [2, 768, 2304], P(None, None, ('wide', 'narrow')), may hold values from -0.21875 to 0.21875
- in_bias: float32 [2, 2304], replicated, may hold values from -3 to 3
- short_taps: float32 [2, 3, 2304], replicated, may hold values from -3.5 to 3.5
- cond_taps: float32 [2, 3, 768], replicated, may hold values from -3.5 to 3.5
- decay_rate: float32 [2, 768], replicated, may hold values from 0.001 to 0.05
- freq_in: float32 [2, 64, 64], replicated, may hold values from -0.75 to 0.75
- freq_bias: float32 [2, 64], replicated, may hold values from -3.140625 to 3.140625
- freq_out: float32 [2, 64, 768], replicated, may hold values from -0.75 to 0.75
- out_weight: bfloat16 [2, 768, 768], P(None, ('wide', 'narrow')), may hold values from -0.4375 to 0.4375
- out_bias: float32 [2, 768], replicated, may hold values from -1.75 to 1.75
- up_weight: bfloat16 [2, 768, 6144], P(None, None, ('wide', 'narrow')), may hold values from -0.21875 to 0.21875
- down_weight: bfloat16 [2, 3072, 768], P(None, ('wide', 'narrow')), may hold values from -0.109375 to 0.109375
- down_bias: float32 [2, 768], replicated, may hold values from -1.75 to 1.75
Outputs:
- layer_outputs: float32 [2, 32, 1024, 768], P(None, ('wide', 'narrow'))
- token_grad: float32 [32, 1024, 768], P(('wide', 'narrow'))
- norm_gain_grad: float32 [2, 2, 768], replicated
- norm_shift_grad: float32 [2, 2, 768], replicated
- in_weight_grad: float32 [2, 768, 2304], P(None, None, ('wide', 'narrow'))
- in_bias_grad: float32 [2, 2304], replicated
- short_taps_grad: float32 [2, 3, 2304], replicated
- cond_taps_grad: float32 [2, 3, 768], replicated
- decay_rate_grad: float32 [2, 768], replicated
- freq_in_grad: float32 [2, 64, 64], replicated
- freq_bias_grad: float32 [2, 64], replicated
- freq_out_grad: float32 [2, 64, 768], replicated
- out_weight_grad: float32 [2, 768, 768], P(None, ('wide', 'narrow'))
- out_bias_grad: float32 [2, 768], replicated
- up_weight_grad: float32 [2, 768, 6144], P(None, None, ('wide', 'narrow'))
- down_weight_grad: float32 [2, 3072, 768], P(None, ('wide', 'narrow'))
- down_bias_grad: float32 [2, 768], replicated
The draws below stay inside these ranges and needn't reach their ends.
Inputs may be any that keep to these rules, and one draw needn't show every extreme that they name: Each pair has two nonempty segments split at split_point.
All inputs are finite; a program needn't handle non-finite values.
Results may differ from the reference program's by a relative error of at most 0.012.
Values may be sent and summed in bfloat16 or wider, within the bound.
No kernel may reach another device: no remote copies, remote signals or barrier semaphores. Data moves between devices by JAX's collectives and lax.ppermute only.
A program may use at most 576 MiB of HBM per device.

```python
import math
import jax
import jax.numpy as jnp
from jax import lax

D = 768
FF = 3072
FE = 64
FH = 64
LEN = 1024
LAYERS = 2
PAIRS = 32


def place_ends(result, key, low, largest):
    extent = result.shape
    index_at = [jax.random.randint(jax.random.fold_in(key, axis), (), 0, extent[axis]) for axis in range(len(extent))]
    result = result.at[tuple(index_at)].set(low)
    longest = extent.index(max(extent))
    index_at[longest] = (index_at[longest] + 1) % extent[longest]
    return result.at[tuple(index_at)].set(largest)


def shard_levels(own_key, extent, split, smallest, top_value):
    factor_of = 1.0
    for dim, shards_of in split:
        draws = jax.random.uniform(jax.random.fold_in(jax.random.fold_in(own_key, 6), dim), (shards_of,), jnp.float32, smallest / len(split), top_value / len(split))
        factor_of = factor_of * jnp.repeat(jnp.exp(draws), extent[dim] // shards_of).reshape((-1,) + (1,) * (len(extent) - 1 - dim))
    return factor_of


def normal_values(stream_key, shape, spread, limit, split=(), held_as=jnp.bfloat16):
    array = jax.random.normal(stream_key, shape, jnp.float32) * spread
    if len(split) > 0:
        array = shard_levels(stream_key, shape, split, -0.22, 0.18) * array
    return jnp.clip(array, min=-limit, max=limit).astype(held_as)


def setup_inputs(seed: int = 0) -> dict:
    key_list = jax.random.split(jax.random.key(seed), 19)
    tokens = normal_values(key_list[0], (PAIRS, LEN, D), 1.0, 6.0, ((0, 32),))
    split_point = place_ends(jax.random.randint(key_list[1], (PAIRS,), LEN // 8, LEN - LEN // 8 + 1), jax.random.fold_in(key_list[1], 1), LEN // 8, (LEN - LEN // 8 + 1) - 1).astype(jnp.int32)
    cotangent = normal_values(key_list[2], (PAIRS, LEN, D), 1.0, 6.0, ((0, 32),))
    norm_gain = jnp.clip(1.0 + 0.1 * jax.random.normal(key_list[3], (LAYERS, 2, D), jnp.float32), 0.5, 1.5)
    norm_shift = normal_values(key_list[4], (LAYERS, 2, D), 0.3, 1.75, (), jnp.float32)
    in_weight = normal_values(key_list[5], (LAYERS, D, 3 * D), D ** -0.5, 0.21875, ((2, 32),))
    in_bias = normal_values(key_list[6], (LAYERS, 3 * D), 0.5, 3.0, (), jnp.float32)
    short_taps = normal_values(key_list[7], (LAYERS, 3, 3 * D), 0.6, 3.5, (), jnp.float32)
    cond_taps = normal_values(key_list[8], (LAYERS, 3, D), 0.6, 3.5, (), jnp.float32)
    decay_rate = jnp.clip(jnp.exp(jax.random.uniform(key_list[9], (LAYERS, D), jnp.float32, math.log(0.001), math.log(0.05))), 0.001, 0.05)
    freq_in = normal_values(key_list[10], (LAYERS, FE, FH), FE ** -0.5, 0.75, (), jnp.float32)
    freq_bias = jnp.clip(jax.random.uniform(key_list[11], (LAYERS, FH), jnp.float32, -3.140625, 3.140625), -3.140625, 3.140625)
    freq_out = normal_values(key_list[12], (LAYERS, FH, D), FH ** -0.5, 0.75, (), jnp.float32)
    out_weight = normal_values(key_list[13], (LAYERS, D, D), (D // 4) ** -0.5, 0.4375, ((1, 32),))
    out_bias = normal_values(key_list[14], (LAYERS, D), 0.3, 1.75, (), jnp.float32)
    up_weight = normal_values(key_list[15], (LAYERS, D, 2 * FF), D ** -0.5, 0.21875, ((2, 32),))
    down_weight = normal_values(key_list[16], (LAYERS, FF, D), FF ** -0.5, 0.109375, ((1, 32),))
    down_bias = normal_values(key_list[17], (LAYERS, D), 0.3, 1.75, (), jnp.float32)
    return {"tokens": tokens, "split_point": split_point, "cotangent": cotangent, "norm_gain": norm_gain, "norm_shift": norm_shift, "in_weight": in_weight, "in_bias": in_bias, "short_taps": short_taps, "cond_taps": cond_taps, "decay_rate": decay_rate, "freq_in": freq_in, "freq_bias": freq_bias, "freq_out": freq_out, "out_weight": out_weight, "out_bias": out_bias, "up_weight": up_weight, "down_weight": down_weight, "down_bias": down_bias}


epsilon = 1e-05
highest = lax.Precision.HIGHEST

@jax.custom_vjp
def low(v):
    return lax.optimization_barrier(v.astype(jnp.bfloat16)).astype(jnp.float32)

@jax.custom_vjp
def low_back(v):
    return v

def low_keep(v):
    return (low(v), None)

def low_pass(kept, grad):
    return (grad,)

def back_keep(v):
    return (v, None)

def back_low(kept, grad):
    return (low(grad),)
low.defvjp(low_keep, low_pass)
low_back.defvjp(back_keep, back_low)

def norm_rows(values, gain, shift):
    average = lax.optimization_barrier(jnp.mean(values, axis=-1, keepdims=True))
    centered = values - average
    variance = lax.optimization_barrier(jnp.mean(centered * centered, axis=-1, keepdims=True))
    return centered * lax.rsqrt(variance + epsilon) * gain + shift

def gated_unit(values):
    midpoint = values.shape[-1] // 2
    return jax.nn.gelu(values[..., :midpoint], approximate=True) * values[..., midpoint:]

def short_conv(values, tap_weights, segment):
    length = values.shape[-2]
    accumulated = tap_weights[0] * values
    for offset in (1, 2):
        moved = jnp.pad(values, ((0, 0), (offset, 0), (0, 0)))[:, :length, :]
        before = jnp.pad(segment, ((0, 0), (offset, 0)), constant_values=-1)[:, :length]
        same_doc = (before == segment).astype(values.dtype)[..., None]
        accumulated = accumulated + tap_weights[offset] * moved * same_doc
    return accumulated

def filter_kernel(length, decay, freq_in, freq_bias, freq_out):
    feature_half = freq_in.shape[0] // 2
    positions = jnp.arange(length, dtype=jnp.float32)[:, None]
    harmonics = jnp.arange(1, feature_half + 1, dtype=jnp.float32)[None, :]
    angles = positions * harmonics * (2.0 * math.pi / length)
    features = jnp.concatenate([jnp.sin(angles), jnp.cos(angles)], axis=1)
    inner = jnp.sin(jnp.dot(features, freq_in, precision=highest) + freq_bias)
    profile = jnp.dot(inner, freq_out, precision=highest)
    window = jnp.exp(-positions * decay[None, :]) * jnp.sqrt(2.0 * decay)[None, :]
    return profile * window

def fft_conv(kernel, signal):
    length = kernel.shape[0]
    padded_len = 2 * length
    kernel_spec = jnp.fft.rfft(kernel, n=padded_len, axis=0)
    signal_spec = jnp.fft.rfft(signal, n=padded_len, axis=-2)
    return jnp.fft.irfft(signal_spec * kernel_spec, n=padded_len, axis=-2)[..., :length, :]

def mixer(projected, segment, in_bias, short_taps, cond_taps, decay, freq_in, freq_bias, freq_out, convolve):
    channels = projected.shape[-1] // 3
    length = projected.shape[-2]
    shortened = short_conv(projected + in_bias, short_taps, segment)
    query = shortened[..., :channels]
    key_part = shortened[..., channels:2 * channels]
    value_part = shortened[..., 2 * channels:]
    condition = short_conv(value_part, cond_taps, segment)
    channel_scale = jnp.sqrt(lax.optimization_barrier(jnp.mean(condition * condition, axis=-2, keepdims=True)) + epsilon)
    kernel = filter_kernel(length, decay, freq_in, freq_bias, freq_out)
    front_mask = (segment == 0).astype(projected.dtype)[..., None]
    back_mask = 1.0 - front_mask
    product = key_part * value_part
    convolved = convolve(kernel, jnp.stack([product * front_mask, product * back_mask]))
    return query * channel_scale * (convolved[0] * front_mask + convolved[1] * back_mask)

def layer_forward(state, segment, gain, shift, w_in, b_in, taps, cond, decay, f_in, f_bias, f_out, w_out, b_out, w_up, w_down, b_down):
    normed = low(norm_rows(state, gain[0], shift[0]))
    projected = low_back(jnp.einsum('pld,de->ple', normed, w_in, precision=highest))
    mixed = low(mixer(projected, segment, b_in, taps, cond, decay, f_in, f_bias, f_out, fft_conv))
    middle = state + low_back(jnp.einsum('pld,de->ple', mixed, w_out, precision=highest)) + b_out
    second = low(norm_rows(middle, gain[1], shift[1]))
    hidden_in = low_back(jnp.einsum('pld,df->plf', second, w_up, precision=highest))
    hidden = low(gated_unit(hidden_in))
    return middle + low_back(jnp.einsum('plf,fd->pld', hidden, w_down, precision=highest)) + b_down

def reference(tokens, split_point, cotangent, norm_gain, norm_shift, in_weight, in_bias, short_taps, cond_taps, decay_rate, freq_in, freq_bias, freq_out, out_weight, out_bias, up_weight, down_weight, down_bias):
    params = tuple((member.astype(jnp.float32) for member in (norm_gain, norm_shift, in_weight, in_bias, short_taps, cond_taps, decay_rate, freq_in, freq_bias, freq_out, out_weight, out_bias, up_weight, down_weight, down_bias)))
    group_size = math.gcd(PAIRS, 4)
    rounds = PAIRS // group_size
    inputs_all = tokens.astype(jnp.float32).reshape(rounds, group_size, LEN, D)
    splits_all = split_point.reshape(rounds, group_size)
    cotan_all = cotangent.astype(jnp.float32).reshape(rounds, group_size, LEN, D)

    def forward(state, segment, weights):
        results = []
        for layer_index in range(LAYERS):
            state = layer_forward(state, segment, *[member[layer_index] for member in weights])
            results.append(state)
        return jnp.stack(results)

    def accumulate(totals, sliced):
        state, splits, cotan = sliced
        segment = (jnp.arange(LEN, dtype=jnp.int32)[None, :] >= splits[:, None]).astype(jnp.int32)
        results, pullback = jax.vjp(lambda inputs, weights: forward(inputs, segment, weights), state, params)
        seeds = jnp.concatenate([jnp.zeros((LAYERS - 1,) + cotan.shape, cotan.dtype), cotan[None]], axis=0)
        grad_inputs, grad_params = pullback(seeds)
        totals = jax.tree.map(lambda left, right: left + right, totals, grad_params)
        return (totals, (results, grad_inputs))
    start_totals = jax.tree.map(jnp.zeros_like, params)
    totals, (results, grad_inputs) = lax.scan(accumulate, start_totals, (inputs_all, splits_all, cotan_all))
    layer_outputs = results.transpose(1, 0, 2, 3, 4).reshape(LAYERS, PAIRS, LEN, D)
    token_grad = grad_inputs.reshape(PAIRS, LEN, D)
    return (layer_outputs, token_grad, totals[0], totals[1], totals[2], totals[3], totals[4], totals[5], totals[6], totals[7], totals[8], totals[9], totals[10], totals[11], totals[12], totals[13], totals[14])
```

```python
import functools
import math

import jax
import jax.numpy as jnp
import numpy as np
from jax import lax
from jax.experimental import pallas as pl
from jax.experimental.pallas import tpu as pltpu
from jax.sharding import PartitionSpec as P

epsilon = 1e-05
f32 = jnp.float32
bf16 = jnp.bfloat16
AXES = ("wide", "narrow")
BLK = 256
BINS = 2 * BLK
CB = 256
PAD = 8
VMEM = 60 * 2**20
NN = (((1,), (0,)), ((), ()))
NT = (((1,), (1,)), ((), ()))
TN = (((0,), (0,)), ((), ()))
GELU_A = math.sqrt(2.0 / math.pi)
GELU_B = 0.044715


def dot(left, right, dims):
    return lax.dot_general(left, right, dims, preferred_element_type=f32)


def split_low(table):
    high = table.astype(jnp.bfloat16)
    low = (table - high.astype(np.float32)).astype(jnp.bfloat16)
    return np.concatenate([high, high, low], axis=1)


def spectrum_tables():
    t = np.arange(BLK, dtype=np.float64)[None, :]
    k = np.arange(BLK, dtype=np.float64)[:, None]
    angle = 2.0 * np.pi * ((k * t) % BINS) / BINS
    forward = np.concatenate([np.cos(angle), -np.sin(angle)], axis=0)
    forward[BLK] = np.where(np.arange(BLK) % 2 == 0, 1.0, -1.0)
    weight = np.full((BINS, 1), 2.0 / BINS)
    weight[0] = 1.0 / BINS
    weight[BLK] = 1.0 / BINS
    inverse = (forward * weight).T
    return forward.astype(np.float32), inverse.astype(np.float32)


FORWARD, INVERSE = spectrum_tables()


def transform(table, values):
    return dot(table, values.astype(bf16), NN)


def transform_fine(table, values):
    high = values.astype(bf16)
    low = (values - high.astype(f32)).astype(bf16)
    return dot(table, jnp.concatenate([high, low, high], axis=0), NN)


def fold(values):
    rows, cols = values.shape
    return jnp.sum(values.reshape(rows // 8, 8, cols), axis=0)


def loop_rows(total, step, body, init):
    def run(index, carry):
        return body(pl.multiple_of(index * step, step), carry)

    return lax.fori_loop(0, total // step, run, init)


def row_mask(start, rows, cols):
    return start + lax.broadcasted_iota(jnp.int32, (rows, cols), 0)


def earlier(ref, lead, start, rows, cols, split):
    ext = ref[lead + (pl.ds(start, rows + PAD), slice(None))]
    t = row_mask(start, rows, cols)
    one = jnp.where(t != split, pltpu.roll(ext, 1, 0)[PAD:], 0.0)
    two = jnp.where((t != split) & (t != split + 1), pltpu.roll(ext, 2, 0)[PAD:], 0.0)
    return ext[PAD:], one, two


def later(ref, lead, start, rows, cols, split):
    ext = ref[lead + (pl.ds(start, rows + PAD), slice(None))]
    total = rows + PAD
    t = row_mask(start, rows, cols)
    one = jnp.where(t + 1 != split, pltpu.roll(ext, total - 1, 0)[:rows], 0.0)
    two = jnp.where(
        (t + 2 != split) & (t + 1 != split), pltpu.roll(ext, total - 2, 0)[:rows], 0.0
    )
    return ext[:rows], one, two


def norm_parts(values):
    average = jnp.mean(values, axis=-1, keepdims=True)
    centered = values - average
    variance = jnp.mean(centered * centered, axis=-1, keepdims=True)
    rstd = lax.rsqrt(variance + epsilon)
    return centered * rstd, rstd


def part_place(part, boundary):
    block = jnp.where(part <= boundary, part, part - 1)
    return pl.multiple_of(block * BLK, BLK)


def part_keep(part, boundary, split, start):
    t = row_mask(start, BLK, CB)
    front = jnp.where(part <= boundary, 1, 0)
    return jnp.where(t < split, 1, 0) == front


def load_part(ref, part, parts, boundary, split):
    start = part_place(part, boundary)
    return jnp.where(part_keep(part, boundary, split, start), ref[pl.ds(start, BLK), :], 0.0)


def store_part(ref, part, boundary, split, values):
    start = part_place(part, boundary)
    keep = part_keep(part, boundary, split, start)
    ref[pl.ds(start, BLK), :] = jnp.where(keep, values, ref[pl.ds(start, BLK), :])


def first_row(shape):
    return lax.broadcasted_iota(jnp.int32, shape, 0) == 0


def sum_terms(terms):
    total = terms[0]
    for term in terms[1:]:
        total = total + term
    return total


def mixer_forward_kernel(
    split_ref,
    state_ref,
    norm_ref,
    chan_ref,
    win_ref,
    khat_ref,
    fwd_ref,
    inv_ref,
    wout_ref,
    middle_ref,
    second_ref,
    normed_ref,
    biased_ref,
    conv_ref,
    scale_ref,
    val_ref,
    query_ref,
    prod_ref,
    spec_ref,
    res_ref,
):
    step = pl.program_id(0)
    length, width = state_ref.shape
    split = split_ref[0]
    boundary = split // BLK
    parts = length // BLK + 1

    @pl.when(step == 0)
    def _():
        def norm(row, carry):
            hat, _ = norm_parts(state_ref[pl.ds(row, 64), :])
            normed_ref[pl.ds(row, 64), :] = (hat * norm_ref[0:1, :] + norm_ref[1:2, :]).astype(bf16)
            return carry

        loop_rows(length, 64, norm, 0)
        val_ref[0:PAD, :] = jnp.zeros((PAD, CB), f32)

    biased_ref[:, 0:PAD, :] = jnp.zeros((3, PAD, CB), f32)
    for stream in range(3):
        biased = dot(normed_ref[...], win_ref[stream], NT) + chan_ref[stream : stream + 1, :]
        biased_ref[stream, PAD:, :] = biased

    rows = 32

    def shorten(row, carry):
        out = []
        for stream in range(3):
            now, one, two = earlier(biased_ref, (stream,), row, rows, CB, split)
            out.append(
                chan_ref[3 + stream : 4 + stream, :] * now
                + chan_ref[6 + stream : 7 + stream, :] * one
                + chan_ref[9 + stream : 10 + stream, :] * two
            )
        query_ref[pl.ds(row, rows), :] = out[0]
        val_ref[pl.ds(row + PAD, rows), :] = out[2]
        prod_ref[pl.ds(row, rows), :] = out[1] * out[2]
        return carry

    loop_rows(length, rows, shorten, 0)

    def condition(row, total):
        now, one, two = earlier(val_ref, (), row, rows, CB, split)
        cond = chan_ref[12:13, :] * now + chan_ref[13:14, :] * one + chan_ref[14:15, :] * two
        return total + fold(cond * cond)

    squares = loop_rows(length, rows, condition, jnp.zeros((8, CB), f32))
    scale = jnp.sqrt(jnp.sum(squares, axis=0, keepdims=True) * (1.0 / length) + epsilon)
    scale_ref[...] = jnp.broadcast_to(scale, (8, CB))

    for part in range(parts):
        spec_ref[part] = transform_fine(
            fwd_ref[...], load_part(prod_ref, part, parts, boundary, split)
        )

    def pairs_into(part, bound):
        low = 0 if part <= bound else bound + 1
        return [(part - source, source) for source in range(low, part + 1)]

    for bound in range(parts - 1):

        @pl.when(boundary == bound)
        def _():
            def multiply(row, carry):
                k_re = [khat_ref[m, pl.ds(row, 8), :] for m in range(parts - 1)]
                k_im = [khat_ref[m, pl.ds(row + BLK, 8), :] for m in range(parts - 1)]
                s_re = [spec_ref[v, pl.ds(row, 8), :] for v in range(parts)]
                s_im = [spec_ref[v, pl.ds(row + BLK, 8), :] for v in range(parts)]
                for part in range(parts):
                    pairs = pairs_into(part, bound)
                    res_ref[part, pl.ds(row, 8), :] = sum_terms(
                        [k_re[m] * s_re[v] - k_im[m] * s_im[v] for m, v in pairs]
                    )
                    res_ref[part, pl.ds(row + BLK, 8), :] = sum_terms(
                        [k_re[m] * s_im[v] + k_im[m] * s_re[v] for m, v in pairs]
                    )
                return carry

            loop_rows(BLK, 8, multiply, 0)
            top = first_row((8, CB))
            for part in range(parts):
                pairs = pairs_into(part, bound)
                for base in (0, BLK):
                    real = sum_terms(
                        [khat_ref[m, base : base + 8, :] * spec_ref[v, base : base + 8, :] for m, v in pairs]
                    )
                    res_ref[part, base : base + 8, :] = jnp.where(
                        top, real, res_ref[part, base : base + 8, :]
                    )

    for part in range(parts):
        store_part(conv_ref, part, boundary, split, transform_fine(inv_ref[...], res_ref[part]))

    mixed = (query_ref[...] * scale * conv_ref[...]).astype(bf16)
    update = dot(mixed, wout_ref[...], NN)

    @pl.when(step == 0)
    def _():
        middle_ref[...] = update

    @pl.when(step > 0)
    def _():
        middle_ref[...] += update

    @pl.when(step == pl.num_programs(0) - 1)
    def _():
        def finish(row, carry):
            here = pl.ds(row, 64)
            middle = state_ref[here, :] + middle_ref[here, :] + norm_ref[4:5, :]
            middle_ref[here, :] = middle
            hat, _ = norm_parts(middle)
            second_ref[here, :] = (hat * norm_ref[2:3, :] + norm_ref[3:4, :]).astype(bf16)
            return carry

        loop_rows(length, 64, finish, 0)


def whole_block(shape):
    return pl.BlockSpec(shape, lambda *index: (0,) * len(shape))


def fixed_block(shape):
    return pl.BlockSpec(shape, lambda *index: (0,) * len(shape), pipeline_mode=pl.Buffered(1))


def mixer_forward(split, state, norm_pack, chan_pack, w_in, khat, w_out):
    length, width = state.shape
    steps = width // CB
    parts = length // BLK + 1
    forward = jnp.asarray(split_low(FORWARD))
    inverse = jnp.asarray(split_low(INVERSE))
    return pl.pallas_call(
        mixer_forward_kernel,
        grid=(steps,),
        in_specs=[
            pl.BlockSpec(memory_space=pltpu.SMEM),
            fixed_block((length, width)),
            fixed_block(norm_pack.shape),
            pl.BlockSpec((16, CB), lambda i: (0, i)),
            pl.BlockSpec((3, CB, width), lambda i: (0, i, 0)),
            pl.BlockSpec((parts - 1, BINS, CB), lambda i: (0, 0, i)),
            fixed_block(forward.shape),
            fixed_block(inverse.shape),
            pl.BlockSpec((CB, width), lambda i: (i, 0)),
        ],
        out_specs=[
            whole_block((length, width)),
            whole_block((length, width)),
            whole_block((length, width)),
            pl.BlockSpec((3, length + PAD, CB), lambda i: (0, 0, i)),
            pl.BlockSpec((length, CB), lambda i: (0, i)),
            pl.BlockSpec((8, CB), lambda i: (0, i)),
        ],
        out_shape=[
            jax.ShapeDtypeStruct((length, width), f32),
            jax.ShapeDtypeStruct((length, width), bf16),
            jax.ShapeDtypeStruct((length, width), bf16),
            jax.ShapeDtypeStruct((3, length + PAD, width), f32),
            jax.ShapeDtypeStruct((length, width), f32),
            jax.ShapeDtypeStruct((8, width), f32),
        ],
        scratch_shapes=[
            pltpu.VMEM((length + PAD, CB), f32),
            pltpu.VMEM((length, CB), f32),
            pltpu.VMEM((length, CB), f32),
            pltpu.VMEM((parts, BINS, CB), f32),
            pltpu.VMEM((parts, BINS, CB), f32),
        ],
        compiler_params=pltpu.CompilerParams(vmem_limit_bytes=VMEM),
        cost_estimate=cost(20e9, 40 * 2**20),
        name="mixer_forward",
    )(split, state, norm_pack, chan_pack, w_in.reshape(3, width, width), khat, forward, inverse, w_out)


PARTS = 2


def cost(flops, moved):
    return pl.CostEstimate(flops=int(flops), bytes_accessed=int(moved), transcendentals=0)


def flat(block):
    return block.reshape(-1, block.shape[-1])


def gated_forward_kernel(
    first, second_ref, gate_w_ref, value_w_ref, down_ref, middle_ref, norm_ref, gate_ref, value_ref, out_ref
):
    step = pl.program_id(0)
    length = second_ref.shape[0]
    rows = 256
    gate_w = flat(gate_w_ref[...])
    value_w = flat(value_w_ref[...])
    down_w = flat(down_ref[...])

    @pl.when(step == 0)
    def _():
        if first:
            out_ref[...] = middle_ref[...] + norm_ref[5:6, :]
        else:
            out_ref[...] = middle_ref[...]

    for row in range(0, length, rows):
        here = slice(row, row + rows)
        gate = dot(second_ref[here, :], gate_w, NT)
        value = dot(second_ref[here, :], value_w, NT)
        gate_ref[here, :] = gate.astype(bf16)
        value_ref[here, :] = value.astype(bf16)
        bent = jnp.tanh(GELU_A * gate * (1.0 + GELU_B * gate * gate))
        hidden = (0.5 * gate * (1.0 + bent) * value).astype(bf16)
        out_ref[here, :] += dot(hidden, down_w, NN)


def pieces_of(weight, group):
    grouped = weight.reshape(-1, PARTS, group // PARTS, weight.shape[-1])
    return [grouped[:, part] for part in range(PARTS)]


def gated_forward(second, up, down, before, norm_pack, first, block=768):
    length, width = second.shape
    piece = down.shape[1]
    hidden = down.shape[0] * piece
    steps = hidden // block
    tile = (block // piece, piece, width)
    return pl.pallas_call(
        functools.partial(gated_forward_kernel, first),
        grid=(steps,),
        in_specs=[
            fixed_block((length, width)),
            pl.BlockSpec(tile, lambda i: (i, 0, 0)),
            pl.BlockSpec(tile, lambda i: (i + steps, 0, 0)),
            pl.BlockSpec(tile, lambda i: (i, 0, 0)),
            fixed_block((length, width)),
            fixed_block(norm_pack.shape),
        ],
        out_specs=[
            pl.BlockSpec((length, block), lambda i: (0, i)),
            pl.BlockSpec((length, block), lambda i: (0, i)),
            whole_block((length, width)),
        ],
        out_shape=[
            jax.ShapeDtypeStruct((length, hidden), bf16),
            jax.ShapeDtypeStruct((length, hidden), bf16),
            jax.ShapeDtypeStruct((length, width), f32),
        ],
        compiler_params=pltpu.CompilerParams(vmem_limit_bytes=VMEM),
        cost_estimate=cost(6 * length * width * hidden, 20 * 2**20),
        name="gated_forward",
    )(second, up, up, down, before, norm_pack)


def norm_backward(values, grad_out, gain):
    hat, rstd = norm_parts(values)
    grad_hat = grad_out * gain
    mean_one = jnp.mean(grad_hat, axis=-1, keepdims=True)
    mean_two = jnp.mean(grad_hat * hat, axis=-1, keepdims=True)
    return rstd * (grad_hat - mean_one - hat * mean_two), grad_out * hat


def gated_backward_kernel(
    first,
    last,
    slots,
    me_ref,
    grad_ref,
    before_ref,
    second_ref,
    middle_ref,
    norm_ref,
    gate_ref,
    value_ref,
    gate_w_ref,
    value_w_ref,
    down_ref,
    one_ref,
    two_ref,
    out_ref,
    small_ref,
    glow_ref,
    hidden_ref,
    dgate_ref,
    dvalue_ref,
    stage_ref,
    sems,
):
    step = pl.program_id(0)
    steps = pl.num_programs(0)
    length, width = grad_ref.shape
    rows = 256
    count, piece, _ = gate_w_ref.shape
    side = step % 2
    gate_w = flat(gate_w_ref[...])
    value_w = flat(value_w_ref[...])
    down_w = flat(down_ref[...])

    @pl.when(step == 0)
    def _():
        glow_ref[...] = grad_ref[...].astype(bf16)
        if first:
            out_ref[...] = jnp.zeros_like(out_ref)
        else:
            out_ref[...] = before_ref[...]

    def copies(at_step, kind, item):
        source = stage_ref.at[at_step % 2, kind, pl.ds(item * piece, piece), :]
        half = at_step * count + item
        if not slots:
            if kind == 2:
                return source, [(None, two_ref.at[half])]
            return source, [(None, one_ref.at[half + kind * steps * count])]
        if kind == 2:
            mask = half ^ me_ref[0]
            rows_at = pl.ds(2 * piece, piece)
        else:
            mask = ((half >> 1) + kind * (steps * count >> 1)) ^ me_ref[0]
            rows_at = pl.ds((half & 1) * piece, piece)
        place = mask >> 1
        core = mask & 1
        return source, [
            (core == 0, one_ref.at[place, rows_at, :]),
            (core == 1, two_ref.at[place, rows_at, :]),
        ]

    def send(kind):
        def go(item, carry):
            source, targets = copies(step, kind, item)
            for condition, target in targets:
                move = pltpu.make_async_copy(source, target, sems.at[side, kind, item])
                if condition is None:
                    move.start()
                else:
                    pl.when(condition)(move.start)
            return carry

        lax.fori_loop(0, count, go, 0)

    def drain(at_step):
        def go(item, carry):
            for kind in range(3):
                source, targets = copies(at_step, kind, item)
                pltpu.make_async_copy(
                    source, targets[0][1], sems.at[at_step % 2, kind, item]
                ).wait()
            return carry

        lax.fori_loop(0, count, go, 0)

    for row in range(0, length, rows):
        here = slice(row, row + rows)
        grad_hidden = dot(glow_ref[here, :], down_w, NT)
        gate = gate_ref[here, :].astype(f32)
        value = value_ref[here, :].astype(f32)
        square = gate * gate
        bent = jnp.tanh(GELU_A * gate * (1.0 + GELU_B * square))
        half = 0.5 * (1.0 + bent)
        unit = half * gate
        slope = half + 0.5 * gate * (1.0 - bent * bent) * (GELU_A * (1.0 + 3.0 * GELU_B * square))
        hidden_ref[here, :] = (unit * value).astype(bf16)
        dgate = (grad_hidden * value * slope).astype(bf16)
        dvalue = (grad_hidden * unit).astype(bf16)
        dgate_ref[here, :] = dgate
        dvalue_ref[here, :] = dvalue
        out_ref[here, :] += dot(dgate, gate_w, NN) + dot(dvalue, value_w, NN)

    @pl.when(step > 1)
    def _():
        drain(step - 2)

    stage_ref[side, 0] = dot(dgate_ref[...], second_ref[...], TN).astype(bf16)
    send(0)
    stage_ref[side, 1] = dot(dvalue_ref[...], second_ref[...], TN).astype(bf16)
    send(1)
    stage_ref[side, 2] = dot(hidden_ref[...], glow_ref[...], TN).astype(bf16)
    send(2)

    @pl.when(step == steps - 1)
    def _():
        if not last:
            small_ref[...] = jnp.zeros_like(small_ref)
        else:

            def finish(row, carry):
                here = pl.ds(row, 32)
                grad_out = out_ref[here, :]
                grad = grad_ref[here, :]
                change, gain_rows = norm_backward(middle_ref[here, :], grad_out, norm_ref[2:3, :])
                total = grad + change
                out_ref[here, :] = total
                return (
                    carry[0] + fold(gain_rows),
                    carry[1] + fold(grad_out),
                    carry[2] + fold(total),
                    carry[3] + fold(grad),
                )

            zero = jnp.zeros((8, width), f32)
            sums = loop_rows(length, 32, finish, (zero, zero, zero, zero))
            small_ref[...] = jnp.concatenate(
                [jnp.sum(part, axis=0, keepdims=True) for part in sums]
                + [jnp.zeros((4, width), f32)],
                axis=0,
            )

        @pl.when(steps > 1)
        def _():
            drain(step - 1)

        drain(step)


def gated_backward(
    part, me, grad, before, second, middle, norm_pack, gate, value, up, down, size, block=768
):
    length, width = second.shape
    piece = down.shape[1]
    hidden = down.shape[0] * piece
    inner = hidden // block
    count = block // piece
    tile = (count, piece, width)
    slots = size == 32
    column = pl.BlockSpec((length, block), lambda i: (0, i))
    anywhere = pl.BlockSpec(memory_space=pl.ANY)
    if slots:
        places = [jax.ShapeDtypeStruct((size // 2, 3 * piece, width), bf16)] * 2
    else:
        places = [
            jax.ShapeDtypeStruct((up.shape[0], piece, width), bf16),
            jax.ShapeDtypeStruct((down.shape[0], piece, width), bf16),
        ]
    last = part == PARTS - 1
    return pl.pallas_call(
        functools.partial(gated_backward_kernel, part == 0, last, slots),
        grid=(inner,),
        in_specs=[
            pl.BlockSpec(memory_space=pltpu.SMEM),
            fixed_block((length, width)),
            fixed_block(before.shape),
            fixed_block((length, width)),
            fixed_block((length, width)),
            fixed_block(norm_pack.shape),
            column,
            column,
            pl.BlockSpec(tile, lambda i: (i, 0, 0)),
            pl.BlockSpec(tile, lambda i: (i + inner, 0, 0)),
            pl.BlockSpec(tile, lambda i: (i, 0, 0)),
        ],
        out_specs=[anywhere, anywhere, whole_block((length, width)), whole_block((8, width))],
        out_shape=places
        + [
            jax.ShapeDtypeStruct((length, width), f32),
            jax.ShapeDtypeStruct((8, width), f32),
        ],
        scratch_shapes=[
            pltpu.VMEM((length, width), bf16),
            pltpu.VMEM((length, block), bf16),
            pltpu.VMEM((length, block), bf16),
            pltpu.VMEM((length, block), bf16),
            pltpu.VMEM((2, 3, block, width), bf16),
            pltpu.SemaphoreType.DMA((2, 3, count)),
        ],
        compiler_params=pltpu.CompilerParams(vmem_limit_bytes=VMEM),
        cost_estimate=cost(12 * length * width * hidden, 20 * 2**20),
        name="gated_backward",
    )(me, grad, before, second, middle, norm_pack, gate, value, up, up, down)


def mixer_backward_kernel(
    first,
    last,
    split_ref,
    grad_ref,
    before_ref,
    state_ref,
    normed_ref,
    norm_ref,
    chan_ref,
    biased_ref,
    conv_ref,
    scale_ref,
    khat_ref,
    fwd_ref,
    inv_ref,
    wout_ref,
    win_ref,
    win_g_ref,
    wout_g_ref,
    kern_g_ref,
    chan_g_ref,
    out_ref,
    small_ref,
    mlow_ref,
    key_ref,
    val_ref,
    prod_ref,
    dconv_ref,
    mixed_ref,
    cond_ref,
    dpad_ref,
    low_ref,
    spec_ref,
    dspec_ref,
    res_ref,
    gram_ref,
):
    step = pl.program_id(0)
    length, width = state_ref.shape
    split = split_ref[0]
    boundary = split // BLK
    parts = length // BLK + 1
    rows = 32

    @pl.when(step == 0)
    def _():
        mlow_ref[...] = grad_ref[...].astype(bf16)
        val_ref[0:PAD, :] = jnp.zeros((PAD, CB), f32)
        cond_ref[length:, :] = jnp.zeros((PAD, CB), f32)
        dpad_ref[:, length:, :] = jnp.zeros((3, PAD, CB), f32)

    dconv_ref[...] = dot(mlow_ref[...], wout_ref[...], NT)
    scale = scale_ref[0:1, :]

    def gate(row, total):
        here = pl.ds(row, rows)
        out = []
        for stream in range(3):
            now, one, two = earlier(biased_ref, (stream,), row, rows, CB, split)
            out.append(
                chan_ref[3 + stream : 4 + stream, :] * now
                + chan_ref[6 + stream : 7 + stream, :] * one
                + chan_ref[9 + stream : 10 + stream, :] * two
            )
        query, key, value = out
        key_ref[here, :] = key
        val_ref[pl.ds(row + PAD, rows), :] = value
        prod_ref[here, :] = key * value
        grad = dconv_ref[here, :]
        conv = conv_ref[here, :]
        mixed_ref[here, :] = (query * scale * conv).astype(bf16)
        dpad_ref[0, here, :] = grad * scale * conv
        through = grad * query
        dconv_ref[here, :] = through * scale
        return total + fold(through * conv)

    scale_sum = loop_rows(length, rows, gate, jnp.zeros((8, CB), f32))
    grad_scale = jnp.sum(scale_sum, axis=0, keepdims=True)
    factor = grad_scale / (scale * float(length))

    def condition(row, carry):
        now, one, two = earlier(val_ref, (), row, rows, CB, split)
        cond_ref[pl.ds(row, rows), :] = (
            chan_ref[12:13, :] * now + chan_ref[13:14, :] * one + chan_ref[14:15, :] * two
        )
        return carry

    loop_rows(length, rows, condition, 0)

    for part in range(parts):
        spec_ref[part] = transform(fwd_ref[...], load_part(prod_ref, part, parts, boundary, split))
        dspec_ref[part] = transform(fwd_ref[...], load_part(dconv_ref, part, parts, boundary, split))

    def pairs_from(source, bound):
        high = bound if source <= bound else parts - 1
        return [(part - source, part) for part in range(source, high + 1)]

    def pairs_apart(lag, bound):
        found = []
        for source in range(parts - lag):
            if (source <= bound) == (source + lag <= bound):
                found.append((source, source + lag))
        return found

    odd_sign = jnp.where(lax.broadcasted_iota(jnp.int32, (8, CB), 0) % 2 == 0, 1.0, -1.0)

    def chain(grams):
        return [
            grams[lag] + odd_sign * grams[lag + 1] if lag + 1 < parts - 1 else grams[lag]
            for lag in range(parts - 1)
        ]

    def or_zero(terms):
        return sum_terms(terms) if terms else jnp.zeros((8, CB), f32)

    for bound in range(parts - 1):

        @pl.when(boundary == bound)
        def _():
            def multiply(row, carry):
                k_re = [khat_ref[m, pl.ds(row, 8), :] for m in range(parts - 1)]
                k_im = [khat_ref[m, pl.ds(row + BLK, 8), :] for m in range(parts - 1)]
                e_re = [dspec_ref[v, pl.ds(row, 8), :] for v in range(parts)]
                e_im = [dspec_ref[v, pl.ds(row + BLK, 8), :] for v in range(parts)]
                for source in range(parts):
                    pairs = pairs_from(source, bound)
                    res_ref[source, pl.ds(row, 8), :] = sum_terms(
                        [k_re[m] * e_re[v] + k_im[m] * e_im[v] for m, v in pairs]
                    )
                    res_ref[source, pl.ds(row + BLK, 8), :] = sum_terms(
                        [k_re[m] * e_im[v] - k_im[m] * e_re[v] for m, v in pairs]
                    )
                s_re = [spec_ref[v, pl.ds(row, 8), :] for v in range(parts)]
                s_im = [spec_ref[v, pl.ds(row + BLK, 8), :] for v in range(parts)]
                real, imag = [], []
                for lag in range(parts - 1):
                    pairs = pairs_apart(lag, bound)
                    real.append(
                        or_zero([s_re[j] * e_re[i] + s_im[j] * e_im[i] for j, i in pairs])
                    )
                    imag.append(
                        or_zero([s_re[j] * e_im[i] - s_im[j] * e_re[i] for j, i in pairs])
                    )
                for lag, (one, two) in enumerate(zip(chain(real), chain(imag))):
                    gram_ref[lag, pl.ds(row, 8), :] = one
                    gram_ref[lag, pl.ds(row + BLK, 8), :] = two
                return carry

            loop_rows(BLK, 8, multiply, 0)
            top = first_row((8, CB))
            for base in (0, BLK):
                tile = slice(base, base + 8)
                for source in range(parts):
                    real = sum_terms(
                        [khat_ref[m, tile, :] * dspec_ref[v, tile, :] for m, v in pairs_from(source, bound)]
                    )
                    res_ref[source, tile, :] = jnp.where(top, real, res_ref[source, tile, :])
                grams = [
                    or_zero([spec_ref[j, tile, :] * dspec_ref[i, tile, :] for j, i in pairs_apart(lag, bound)])
                    for lag in range(parts - 1)
                ]
                for lag, real in enumerate(chain(grams)):
                    gram_ref[lag, tile, :] = jnp.where(top, real, gram_ref[lag, tile, :])

    for part in range(parts):
        store_part(prod_ref, part, boundary, split, transform(inv_ref[...], res_ref[part]))
    for lag in range(parts - 1):
        kern_g_ref[lag * BLK : (lag + 1) * BLK, :] = transform(inv_ref[...], gram_ref[lag])

    def spread(row, carry):
        here = pl.ds(row, rows)
        change = prod_ref[here, :]
        value = val_ref[pl.ds(row + PAD, rows), :]
        dpad_ref[1, here, :] = change * value
        now, one, two = later(cond_ref, (), row, rows, CB, split)
        from_cond = chan_ref[12:13, :] * now + chan_ref[13:14, :] * one + chan_ref[14:15, :] * two
        dpad_ref[2, here, :] = change * key_ref[here, :] + factor * from_cond
        return (
            carry[0] + fold(value * now),
            carry[1] + fold(value * one),
            carry[2] + fold(value * two),
        )

    zero = jnp.zeros((8, CB), f32)
    cond_sums = loop_rows(length, rows, spread, (zero, zero, zero))
    sums = [None] * 12
    for stream in range(3):

        def back(row, carry, stream=stream):
            now, one, two = later(dpad_ref, (stream,), row, rows, CB, split)
            biased = biased_ref[stream, pl.ds(row + PAD, rows), :]
            change = (
                chan_ref[3 + stream : 4 + stream, :] * now
                + chan_ref[6 + stream : 7 + stream, :] * one
                + chan_ref[9 + stream : 10 + stream, :] * two
            )
            low_ref[stream, pl.ds(row, rows), :] = change.astype(bf16)
            return (
                carry[0] + fold(change),
                carry[1] + fold(biased * now),
                carry[2] + fold(biased * one),
                carry[3] + fold(biased * two),
            )

        got = loop_rows(length, rows, back, (zero, zero, zero, zero))
        for index in range(4):
            sums[3 * index + stream] = got[index]
    chan_g_ref[...] = jnp.concatenate(
        [jnp.sum(part, axis=0, keepdims=True) for part in sums]
        + [factor * jnp.sum(part, axis=0, keepdims=True) for part in cond_sums]
        + [jnp.zeros((1, CB), f32)],
        axis=0,
    )
    wout_g_ref[...] = dot(mixed_ref[...], mlow_ref[...], TN).astype(bf16)
    for stream in range(3):
        win_g_ref[stream] = dot(low_ref[stream], normed_ref[...], TN).astype(bf16)
    update = sum_terms([dot(low_ref[stream], win_ref[stream], NN) for stream in range(3)])

    @pl.when(step == 0)
    def _():
        if first:
            out_ref[...] = update
        else:
            out_ref[...] = before_ref[...] + update

    @pl.when(step > 0)
    def _():
        out_ref[...] += update

    if not last:
        small_ref[...] = jnp.zeros_like(small_ref)
        return

    @pl.when(step == pl.num_programs(0) - 1)
    def _():
        def finish(row, carry):
            here = pl.ds(row, 32)
            grad_out = out_ref[here, :]
            change, gain_rows = norm_backward(state_ref[here, :], grad_out, norm_ref[0:1, :])
            out_ref[here, :] = grad_ref[here, :] + change
            return carry[0] + fold(gain_rows), carry[1] + fold(grad_out)

        wide_zero = jnp.zeros((8, width), f32)
        got = loop_rows(length, 32, finish, (wide_zero, wide_zero))
        small_ref[...] = jnp.concatenate(
            [jnp.sum(part, axis=0, keepdims=True) for part in got] + [jnp.zeros((6, width), f32)],
            axis=0,
        )


def mixer_backward(start, steps, split, grad, before, state, normed, norm_pack, chan_pack, biased, conv, scale, khat, w_out, w_in):
    length, width = state.shape
    last = (start + steps) * CB == width
    parts = length // BLK + 1
    forward = jnp.asarray(FORWARD, bf16)
    inverse = jnp.asarray(INVERSE, bf16)
    full = fixed_block((length, width))
    tall = pltpu.VMEM((length, CB), f32)
    tall_pad = pltpu.VMEM((length + PAD, CB), f32)
    spectrum = pltpu.VMEM((parts, BINS, CB), f32)
    return pl.pallas_call(
        functools.partial(mixer_backward_kernel, start == 0, last),
        grid=(steps,),
        in_specs=[
            pl.BlockSpec(memory_space=pltpu.SMEM),
            full,
            fixed_block(before.shape),
            full,
            full,
            fixed_block(norm_pack.shape),
            pl.BlockSpec((16, CB), lambda i: (0, i + start)),
            pl.BlockSpec((3, length + PAD, CB), lambda i: (0, 0, i + start)),
            pl.BlockSpec((length, CB), lambda i: (0, i + start)),
            pl.BlockSpec((8, CB), lambda i: (0, i + start)),
            pl.BlockSpec((parts - 1, BINS, CB), lambda i: (0, 0, i + start)),
            fixed_block(forward.shape),
            fixed_block(inverse.shape),
            pl.BlockSpec((CB, width), lambda i: (i + start, 0)),
            pl.BlockSpec((3, CB, width), lambda i: (0, i + start, 0)),
        ],
        out_specs=[
            pl.BlockSpec((3, CB, width), lambda i: (0, i, 0)),
            pl.BlockSpec((CB, width), lambda i: (i, 0)),
            pl.BlockSpec((length, CB), lambda i: (0, i)),
            pl.BlockSpec((16, CB), lambda i: (0, i)),
            whole_block((length, width)),
            whole_block((8, width)),
        ],
        out_shape=[
            jax.ShapeDtypeStruct((3, steps * CB, width), bf16),
            jax.ShapeDtypeStruct((steps * CB, width), bf16),
            jax.ShapeDtypeStruct((length, steps * CB), f32),
            jax.ShapeDtypeStruct((16, steps * CB), f32),
            jax.ShapeDtypeStruct((length, width), f32),
            jax.ShapeDtypeStruct((8, width), f32),
        ],
        scratch_shapes=[
            pltpu.VMEM((length, width), bf16),
            tall,
            tall_pad,
            tall,
            tall,
            pltpu.VMEM((length, CB), bf16),
            tall_pad,
            pltpu.VMEM((3, length + PAD, CB), f32),
            pltpu.VMEM((3, length, CB), bf16),
            spectrum,
            spectrum,
            spectrum,
            pltpu.VMEM((parts - 1, BINS, CB), f32),
        ],
        compiler_params=pltpu.CompilerParams(vmem_limit_bytes=VMEM),
        cost_estimate=cost(12e9 * steps, 14 * 2**20 * steps),
        name="mixer_backward",
    )(
        split,
        grad,
        before,
        state,
        normed,
        norm_pack,
        chan_pack,
        biased,
        conv,
        scale,
        khat,
        forward,
        inverse,
        w_out,
        w_in.reshape(3, width, width),
    )


def filter_features(length, count):
    half = count // 2
    positions = np.arange(length, dtype=np.float64)[:, None]
    harmonics = np.arange(1, half + 1, dtype=np.float64)[None, :]
    angles = 2.0 * np.pi * ((positions * harmonics) % length) / length
    return np.concatenate([np.sin(angles), np.cos(angles)], axis=1).astype(np.float32)


def highest(left, right, dims):
    return lax.dot_general(left, right, dims, precision=lax.Precision.HIGHEST)


def filter_kernel_body(inner_ref, out_ref, decay_ref, fwd_ref, kernel_ref, khat_ref):
    length = inner_ref.shape[0]
    decay = decay_ref[0:1, :]
    level = jnp.sqrt(2.0 * decay)
    sign = jnp.where(lax.broadcasted_iota(jnp.int32, (BINS, CB), 0) % 2 == 0, 1.0, -1.0)
    before = None
    for block in range(length // BLK):
        here = slice(block * BLK, (block + 1) * BLK)
        profile = lax.dot_general(
            inner_ref[here, :],
            out_ref[...],
            NN,
            precision=lax.Precision.HIGHEST,
            preferred_element_type=f32,
        )
        position = row_mask(block * BLK, BLK, CB).astype(f32)
        kernel = profile * (jnp.exp(-position * decay) * level)
        kernel_ref[here, :] = kernel
        spectrum = transform_fine(fwd_ref[...], kernel)
        khat_ref[block] = spectrum if before is None else spectrum + sign * before
        before = spectrum


def filter_forward(length, decay, freq_in, freq_bias, freq_out):
    features = jnp.asarray(filter_features(length, freq_in.shape[0]))
    phase = highest(features, freq_in, NN) + freq_bias
    inner = jnp.sin(phase)
    width = decay.shape[0]
    hidden = inner.shape[1]
    table = jnp.asarray(split_low(FORWARD))
    blocks = length // BLK
    kernel, khat = pl.pallas_call(
        filter_kernel_body,
        grid=(width // CB,),
        in_specs=[
            fixed_block((length, hidden)),
            pl.BlockSpec((hidden, CB), lambda i: (0, i)),
            pl.BlockSpec((8, CB), lambda i: (0, i)),
            fixed_block(table.shape),
        ],
        out_specs=[
            pl.BlockSpec((length, CB), lambda i: (0, i)),
            pl.BlockSpec((blocks, BINS, CB), lambda i: (0, 0, i)),
        ],
        out_shape=[
            jax.ShapeDtypeStruct((length, width), f32),
            jax.ShapeDtypeStruct((blocks, BINS, width), f32),
        ],
        compiler_params=pltpu.CompilerParams(vmem_limit_bytes=VMEM),
        cost_estimate=cost(6e9, 10 * 2**20),
        name="filter_forward",
    )(inner, freq_out, jnp.broadcast_to(decay[None], (8, width)), table)
    positions = jnp.arange(length, dtype=f32)[:, None]
    window = jnp.exp(-positions * decay[None, :]) * jnp.sqrt(2.0 * decay)[None, :]
    return khat, (features, phase, inner, window, kernel, positions)


def filter_backward(grad_kernel, kept, decay, freq_out):
    features, phase, inner, window, kernel, positions = kept
    grad_profile = grad_kernel * window
    grad_freq_out = highest(inner, grad_profile, TN)
    grad_phase = highest(grad_profile, freq_out, NT) * jnp.cos(phase)
    grad_freq_in = highest(features, grad_phase, TN)
    grad_freq_bias = jnp.sum(grad_phase, axis=0)
    grad_decay = jnp.sum(grad_kernel * kernel * (0.5 / decay[None, :] - positions), axis=0)
    return grad_decay, grad_freq_in, grad_freq_bias, grad_freq_out


def cube_orders(size):
    bits = [1 << place for place in range(1, size.bit_length() - 1)]
    if len(bits) < 2:
        return [bits + [1], bits + [1]]
    return [bits + [1], bits[:-2] + [bits[-1], bits[-2]] + [1]]


def slot_table(order, size):
    table = np.zeros(size, np.int32)
    for slot in range(size):
        mask = sum(bit for place, bit in enumerate(order) if slot >> place & 1)
        table[mask] = slot
    return table


def swap(values, bit, size):
    return lax.ppermute(values, AXES, [(index, index ^ bit) for index in range(size)])


def cube_gather(block, order, size, me):
    held = block[None]
    for bit in order:
        held = jnp.concatenate([held, swap(held, bit, size)], axis=0)
    places = jnp.asarray(slot_table(order, size))[jnp.arange(size, dtype=jnp.int32) ^ me]
    return jnp.take(held, places, axis=0)


def cube_scatter(blocks, order, size, me):
    masks = np.zeros(size, np.int32)
    masks[slot_table(order, size)] = np.arange(size)
    held = jnp.take(blocks, jnp.asarray(masks) ^ me, axis=0)
    for place in reversed(range(len(order))):
        half = 1 << place
        got = swap(held[half:], order[place], size)
        held = held[:half].astype(f32) + got.astype(f32)
        if place:
            held = held.astype(bf16)
    return held[0]


def cube_sum(values, size):
    for place in range(size.bit_length() - 1):
        values = values + swap(values, 1 << place, size)
    return values


def halves(rows):
    if rows < 32:
        return rows // 2
    return (rows // 2 + 15) // 16 * 16


def gather_rows(block, size, me):
    cut = halves(block.shape[0])
    orders = cube_orders(size)
    one = cube_gather(block[:cut], orders[0], size, me)
    two = cube_gather(block[cut:], orders[1], size, me)
    return jnp.concatenate([one, two], axis=1)


def scatter_rows(blocks, size, me):
    cut = halves(blocks.shape[1])
    orders = cube_orders(size)
    one = cube_scatter(blocks[:, :cut], orders[0], size, me)
    two = cube_scatter(blocks[:, cut:], orders[1], size, me)
    return jnp.concatenate([one, two], axis=0)


def tie(value, *others):
    return lax.optimization_barrier((value,) + others)[0]


def gather_pieces(block, start_after=(), spread_after=()):
    size = 32
    if start_after:
        block = tie(block, *start_after)
    line = jnp.stack([block] + [swap(block, bit, size) for bit in (2, 4, 6)])
    if spread_after:
        line = tie(line, *spread_after)
    along_x = swap(line, 8, size)
    along_y = swap(line, 16, size)
    corner_one = swap(along_x[:2], 16, size)
    corner_two = swap(along_y[2:], 8, size)
    places = (0, 2, 4, 6)
    held = [
        (line, places),
        (along_x, tuple(8 + place for place in places)),
        (along_y, tuple(16 + place for place in places)),
        (corner_one, (24, 26)),
        (corner_two, (28, 30)),
    ]
    pieces = []
    for piece, masks in held:
        pieces.append((piece, masks))
        pieces.append((swap(piece, 1, size), tuple(mask + 1 for mask in masks)))
    return pieces, (line,), (along_x, along_y)


def place_kernel(masks, cuts, me_ref, *refs):
    pieces = refs[: len(masks)]
    targets = refs[len(masks) : len(masks) + len(cuts)]
    held, in_sems, out_sems = refs[-3:]
    loads = []
    slot = 0
    for index, (piece, own) in enumerate(zip(pieces, masks)):
        load = pltpu.make_async_copy(piece, held.at[slot : slot + len(own)], in_sems.at[index])
        load.start()
        loads.append((load, slot, own))
        slot += len(own)
    moves = []
    for load, slot, own in loads:
        load.wait()
        for place, mask in enumerate(own):
            device = me_ref[0] ^ mask
            start = 0
            for target, rows in zip(targets, cuts):
                move = pltpu.make_async_copy(
                    held.at[slot + place, start : start + rows, :],
                    target.at[device],
                    out_sems.at[len(moves)],
                )
                move.start()
                moves.append(move)
                start += rows
    for move in moves:
        move.wait()


def place_pieces(pieces, cuts, me):
    arrays = [piece for piece, _ in pieces]
    masks = [own for _, own in pieces]
    size = sum(len(own) for own in masks)
    width = arrays[0].shape[-1]
    anywhere = pl.BlockSpec(memory_space=pl.ANY)
    return pl.pallas_call(
        functools.partial(place_kernel, masks, cuts),
        in_specs=[pl.BlockSpec(memory_space=pltpu.SMEM)] + [anywhere] * len(arrays),
        out_specs=[anywhere] * len(cuts),
        out_shape=[jax.ShapeDtypeStruct((size, rows, width), bf16) for rows in cuts],
        scratch_shapes=[
            pltpu.VMEM((size, sum(cuts), width), bf16),
            pltpu.SemaphoreType.DMA((len(masks),)),
            pltpu.SemaphoreType.DMA((size * len(cuts),)),
        ],
        compiler_params=pltpu.CompilerParams(vmem_limit_bytes=VMEM),
        cost_estimate=cost(0, 2 * sum(cuts) * size * width * 2),
        name="place_pieces",
    )(me, *arrays)


def scatter_steps(keep, send, done):
    size = 32
    shape = (4, 4) + keep.shape[1:]
    keep = keep.reshape(shape)
    got = swap(send, 1, size).reshape(shape)
    yield [send]

    def both(group):
        return keep[group].astype(f32) + got[group].astype(f32)

    corner = both(3).astype(bf16)
    from_y = swap(corner[:2], 16, size)
    from_x = swap(corner[2:], 8, size)
    yield [corner]
    to_x = both(1)
    to_x = jnp.concatenate([to_x[:2] + from_y.astype(f32), to_x[2:]], axis=0).astype(bf16)
    to_y = both(2)
    to_y = jnp.concatenate([to_y[:2], to_y[2:] + from_x.astype(f32)], axis=0).astype(bf16)
    got_x, got_y = swap(to_x, 8, size), swap(to_y, 16, size)
    yield [to_x, to_y]
    line = both(0) + got_x.astype(f32) + got_y.astype(f32)
    low = [line[place].astype(bf16) for place in (1, 2, 3)]
    came = [swap(piece, 2 * place + 2, size) for place, piece in enumerate(low)]
    yield low
    done(sum_terms([line[0]] + [piece.astype(f32) for piece in came]))


def sum_steps(values, size, done):
    for place in range(size.bit_length() - 1):
        came = swap(values, 1 << place, size)
        yield [values]
        values = values + came
    done(values)


class Flight:
    def __init__(self):
        self.running = []

    def add(self, steps):
        self.running.append(steps)

    def advance(self):
        sent = []
        still = []
        for steps in self.running:
            try:
                sent.extend(next(steps))
                still.append(steps)
            except StopIteration:
                pass
        self.running = still
        return sent

    def finish(self):
        while self.running:
            self.advance()


def body(
    size,
    tokens,
    split_point,
    cotangent,
    norm_gain,
    norm_shift,
    in_weight,
    in_bias,
    short_taps,
    cond_taps,
    decay_rate,
    freq_in,
    freq_bias,
    freq_out,
    out_weight,
    out_bias,
    up_weight,
    down_weight,
    down_bias,
):
    layers = in_weight.shape[0]
    length, width = tokens.shape[1:]
    me = lax.axis_index(AXES)
    split = split_point.astype(jnp.int32)
    state = tokens[0].astype(f32)
    in_rows = in_weight.shape[2]
    out_rows = out_weight.shape[1]

    packs = []
    for layer in range(layers):
        norm_pack = jnp.concatenate(
            [
                jnp.stack([norm_gain[layer, 0], norm_shift[layer, 0]]),
                jnp.stack([norm_gain[layer, 1], norm_shift[layer, 1]]),
                out_bias[layer][None],
                down_bias[layer][None],
                jnp.zeros((2, width), f32),
            ]
        )
        chan_pack = jnp.concatenate(
            [
                in_bias[layer].reshape(3, width),
                short_taps[layer].reshape(9, width),
                cond_taps[layer],
                jnp.zeros((1, width), f32),
            ]
        )
        packs.append((norm_pack, chan_pack))

    mine = me.astype(jnp.int32)[None]
    up_rows = up_weight.shape[2]
    down_rows = down_weight.shape[1]
    special = size == 32
    mixer_w = [None] * layers
    gated_w = [None] * layers
    lines = {}
    after_start, after_spread = (), ()
    for layer in range(layers):
        mixer_block = jnp.concatenate([in_weight[layer].T, out_weight[layer]], axis=0)
        up_own, down_own = up_weight[layer].T, down_weight[layer]
        if special:
            pieces, after_start, after_spread = gather_pieces(mixer_block, after_start, after_spread)
            lines[layer, "mixer"] = after_start + after_spread
            (mixer_rows,) = place_pieces(pieces, (in_rows + out_rows,), mine)
            gated_w[layer] = []
            halved = up_own.reshape(2, PARTS, -1, width)
            for part in range(PARTS):
                block = jnp.concatenate(
                    [halved[0, part], halved[1, part], down_own.reshape(PARTS, -1, width)[part]], axis=0
                )
                pieces, after_start, after_spread = gather_pieces(block, after_start, after_spread)
                lines[layer, part] = after_start + after_spread
                up, down = place_pieces(pieces, (up_rows // PARTS, down_rows // PARTS), mine)
                gated_w[layer].append((up.reshape(-1, down_rows // PARTS, width), down))
        else:
            mixer_rows = gather_rows(mixer_block, size, me)
            gated_rows = gather_rows(jnp.concatenate([up_own, down_own], axis=0), size, me)
            ups = pieces_of(gated_rows[:, :up_rows].reshape(-1, width), 96)
            downs = pieces_of(gated_rows[:, up_rows:].reshape(-1, width), 96)
            gated_w[layer] = list(zip(ups, downs))
        mixer_w[layer] = (
            mixer_rows[:, :in_rows].reshape(3 * width, width),
            mixer_rows[:, in_rows:].reshape(width, width),
        )

    filters = [
        filter_forward(length, decay_rate[layer], freq_in[layer], freq_bias[layer], freq_out[layer])
        for layer in range(layers)
    ]

    saved = []
    outputs = []
    for layer in range(layers):
        w_in, w_out = mixer_w[layer]
        norm_pack, chan_pack = packs[layer]
        if special:
            state = tie(state, *lines[layer, 0][:1])
        middle, second, normed, biased, conv, scale = mixer_forward(
            split, state, norm_pack, chan_pack, w_in, filters[layer][0], w_out
        )
        total = middle
        kept = []
        for part in range(PARTS):
            up, down = gated_w[layer][part]
            if special and part + 1 < PARTS:
                second = tie(second, *lines[layer, part + 1])
            elif special and layer + 1 < layers:
                second = tie(second, *lines[layer + 1, "mixer"][:1])
            gate, value, total = gated_forward(second, up, down, total, norm_pack, part == 0)
            kept.append((gate, value))
        saved.append((state, normed, biased, conv, scale, middle, second, kept))
        outputs.append(total)
        state = total

    gradient = cotangent[0].astype(f32)
    big = [[None] * 4 for _ in range(layers)]
    small = [None] * layers
    flight = Flight()
    nothing = jnp.zeros((8, width), f32)
    for layer in reversed(range(layers)):
        w_in, w_out = mixer_w[layer]
        norm_pack, chan_pack = packs[layer]
        state_in, normed, biased, conv, scale, middle, second, kept = saved[layer]
        passed = nothing
        gated_g = []
        owned = [None] * PARTS
        for part in range(PARTS):
            gate, value = kept[part]
            up, down = gated_w[layer][part]
            one, two, passed, sums_two = gated_backward(
                part,
                mine,
                tie(gradient, *flight.advance()),
                passed,
                second,
                middle,
                norm_pack,
                gate,
                value,
                up,
                down,
                size,
            )
            gated_g.append((one, two))
            if special:
                flight.add(scatter_steps(one, two, functools.partial(owned.__setitem__, part)))
        grad_middle = passed
        passed = nothing
        found = []
        splits = [3] if layer else [1, 1, 1]
        start = 0
        for steps in splits:
            *got, passed, sums_one = mixer_backward(
                start,
                steps,
                split,
                tie(grad_middle, *flight.advance()),
                passed,
                state_in,
                normed,
                norm_pack,
                chan_pack,
                biased,
                conv,
                scale,
                filters[layer][0],
                w_out,
                w_in,
            )
            found.append(got)
            start += steps
        gradient = passed
        in_g = jnp.concatenate([got[0] for got in found], axis=1)
        out_g = jnp.concatenate([got[1] for got in found], axis=0)
        kernel_g = jnp.concatenate([got[2] for got in found], axis=1)
        chan_g = jnp.concatenate([got[3] for got in found], axis=1)
        mixer_g = jnp.concatenate(
            [in_g.reshape(size, in_rows, width), out_g.reshape(size, out_rows, width)], axis=1
        )

        mixer_own = [None]
        if special:
            order = jnp.arange(size // 2, dtype=jnp.int32) * 2 ^ me
            keep, send = [
                mixer_g.at[places].get(mode="promise_in_bounds") for places in (order, order ^ 1)
            ]
            flight.add(scatter_steps(keep, send, functools.partial(mixer_own.__setitem__, 0)))
        else:
            up_g = jnp.stack([one for one, _ in gated_g], axis=1).reshape(size, -1, width)
            down_g = jnp.stack([two for _, two in gated_g], axis=1).reshape(size, -1, width)
            owned = (scatter_rows(up_g, size, me), scatter_rows(down_g, size, me))
            mixer_own[0] = scatter_rows(mixer_g, size, me)
        grad_decay, grad_freq_in, grad_freq_bias, grad_freq_out = filter_backward(
            kernel_g, filters[layer][1], decay_rate[layer], freq_out[layer]
        )
        pieces = [
            jnp.stack([sums_one[0], sums_two[0]]),
            jnp.stack([sums_one[1], sums_two[1]]),
            chan_g[0:3].reshape(3 * width),
            chan_g[3:12].reshape(3, 3 * width),
            chan_g[12:15],
            grad_decay,
            grad_freq_in,
            grad_freq_bias,
            grad_freq_out,
            sums_two[2],
            sums_two[3],
        ]
        vector = jnp.concatenate([piece.reshape(-1) for piece in pieces])
        vector = jnp.pad(vector, (0, -vector.size % 1024)).reshape(-1, 128)
        summed = [None]
        flight.add(sum_steps(vector, size, functools.partial(summed.__setitem__, 0)))
        small[layer] = (pieces, summed)
        big[layer] = (owned, mixer_own)
    flight.finish()

    for layer in range(layers):
        owned, mixer_own = big[layer]
        if special:
            piece = down_rows // PARTS
            up_own = jnp.concatenate(
                [part[at * piece : (at + 1) * piece] for at in range(2) for part in owned], axis=0
            )
            down_own = jnp.concatenate([part[2 * piece :] for part in owned], axis=0)
        else:
            up_own, down_own = owned
        big[layer] = (mixer_own[0][:in_rows].T, mixer_own[0][in_rows:], up_own.T, down_own)
        pieces, summed = small[layer]
        vector = summed[0].reshape(-1)
        taken = []
        start = 0
        for piece in pieces:
            taken.append(vector[start : start + piece.size].reshape(piece.shape))
            start += piece.size
        small[layer] = taken

    small = [jnp.stack([small[layer][index] for layer in range(layers)]) for index in range(11)]
    big = [jnp.stack([big[layer][index] for layer in range(layers)]) for index in range(4)]
    return (
        jnp.stack(outputs)[:, None],
        gradient[None],
        small[0],
        small[1],
        big[0],
        small[2],
        small[3],
        small[4],
        small[5],
        small[6],
        small[7],
        small[8],
        big[1],
        small[9],
        big[2],
        big[3],
        small[10],
    )


def solution(mesh):
    pairs = P(AXES, None, None)
    columns = P(None, None, AXES)
    rows = P(None, AXES, None)
    in_specs = (
        (pairs, P(AXES), pairs, P(), P(), columns)
        + (P(),) * 7
        + (rows, P(), columns, rows, P())
    )
    out_specs = (
        (P(None, AXES, None, None), pairs, P(), P(), columns)
        + (P(),) * 7
        + (rows, P(), columns, rows, P())
    )
    size = math.prod(mesh.shape.values())
    return jax.shard_map(
        functools.partial(body, size),
        mesh=mesh,
        in_specs=in_specs,
        out_specs=out_specs,
        check_vma=False,
    )
```

```python
import functools
import math

import jax
import jax.numpy as jnp
import numpy as np
from jax import lax
from jax.experimental import pallas as pl
from jax.experimental.pallas import tpu as pltpu
from jax.sharding import PartitionSpec as P

epsilon = 1e-05
f32 = jnp.float32
bf16 = jnp.bfloat16
AXES = ("wide", "narrow")
BLK = 256
BINS = 2 * BLK
CB = 256
PAD = 8
VMEM = 60 * 2**20
NN = (((1,), (0,)), ((), ()))
NT = (((1,), (1,)), ((), ()))
TN = (((0,), (0,)), ((), ()))
GELU_A = math.sqrt(2.0 / math.pi)
GELU_B = 0.044715


def dot(left, right, dims):
    return lax.dot_general(left, right, dims, preferred_element_type=f32)


def dot_fine(left, right, dims):
    return lax.dot_general(
        left, right, dims, precision=lax.Precision.HIGHEST, preferred_element_type=f32
    )


def split_low(table):
    high = table.astype(jnp.bfloat16)
    low = (table - high.astype(np.float32)).astype(jnp.bfloat16)
    return np.concatenate([high, high, low], axis=1)


def spectrum_tables():
    t = np.arange(BLK, dtype=np.float64)[None, :]
    k = np.arange(BLK, dtype=np.float64)[:, None]
    angle = 2.0 * np.pi * ((k * t) % BINS) / BINS
    forward = np.concatenate([np.cos(angle), -np.sin(angle)], axis=0)
    forward[BLK] = np.where(np.arange(BLK) % 2 == 0, 1.0, -1.0)
    weight = np.full((BINS, 1), 2.0 / BINS)
    weight[0] = 1.0 / BINS
    weight[BLK] = 1.0 / BINS
    inverse = (forward * weight).T
    return forward.astype(np.float32), inverse.astype(np.float32)


FORWARD, INVERSE = spectrum_tables()


def transform(table, values):
    return dot(table, values.astype(bf16), NN)


def transform_fine(table, values):
    high = values.astype(bf16)
    low = (values - high.astype(f32)).astype(bf16)
    return dot(table, jnp.concatenate([high, low, high], axis=0), NN)


def fold(values):
    rows, cols = values.shape
    return jnp.sum(values.reshape(rows // 8, 8, cols), axis=0)


def loop_rows(total, step, body, init):
    def run(index, carry):
        return body(pl.multiple_of(index * step, step), carry)

    return lax.fori_loop(0, total // step, run, init)


def row_mask(start, rows, cols):
    return start + lax.broadcasted_iota(jnp.int32, (rows, cols), 0)


def earlier(ref, lead, start, rows, cols, split):
    ext = ref[lead + (pl.ds(start, rows + PAD), slice(None))]
    t = row_mask(start, rows, cols)
    one = jnp.where(t != split, pltpu.roll(ext, 1, 0)[PAD:], 0.0)
    two = jnp.where((t != split) & (t != split + 1), pltpu.roll(ext, 2, 0)[PAD:], 0.0)
    return ext[PAD:], one, two


def later(ref, lead, start, rows, cols, split):
    ext = ref[lead + (pl.ds(start, rows + PAD), slice(None))]
    total = rows + PAD
    t = row_mask(start, rows, cols)
    one = jnp.where(t + 1 != split, pltpu.roll(ext, total - 1, 0)[:rows], 0.0)
    two = jnp.where(
        (t + 2 != split) & (t + 1 != split), pltpu.roll(ext, total - 2, 0)[:rows], 0.0
    )
    return ext[:rows], one, two


def norm_parts(values):
    average = jnp.mean(values, axis=-1, keepdims=True)
    centered = values - average
    variance = jnp.mean(centered * centered, axis=-1, keepdims=True)
    rstd = lax.rsqrt(variance + epsilon)
    return centered * rstd, rstd


def part_place(part, boundary):
    block = jnp.where(part <= boundary, part, part - 1)
    return pl.multiple_of(block * BLK, BLK)


def part_keep(part, boundary, split, start):
    t = row_mask(start, BLK, CB)
    front = jnp.where(part <= boundary, 1, 0)
    return jnp.where(t < split, 1, 0) == front


def load_part(ref, part, parts, boundary, split):
    start = part_place(part, boundary)
    return jnp.where(part_keep(part, boundary, split, start), ref[pl.ds(start, BLK), :], 0.0)


def store_part(ref, part, boundary, split, values):
    start = part_place(part, boundary)
    keep = part_keep(part, boundary, split, start)
    ref[pl.ds(start, BLK), :] = jnp.where(keep, values, ref[pl.ds(start, BLK), :])


def first_row(shape):
    return lax.broadcasted_iota(jnp.int32, shape, 0) == 0


def sum_terms(terms):
    total = terms[0]
    for term in terms[1:]:
        total = total + term
    return total


def mixer_forward_kernel(
    split_ref,
    state_ref,
    norm_ref,
    chan_ref,
    win_ref,
    khat_ref,
    fwd_ref,
    inv_ref,
    wout_ref,
    middle_ref,
    second_ref,
    normed_ref,
    biased_ref,
    conv_ref,
    scale_ref,
    val_ref,
    query_ref,
    prod_ref,
    spec_ref,
    res_ref,
):
    step = pl.program_id(0)
    length, width = state_ref.shape
    split = split_ref[0]
    boundary = split // BLK
    parts = length // BLK + 1

    @pl.when(step == 0)
    def _():
        def norm(row, carry):
            hat, _ = norm_parts(state_ref[pl.ds(row, 64), :])
            normed_ref[pl.ds(row, 64), :] = (hat * norm_ref[0:1, :] + norm_ref[1:2, :]).astype(bf16)
            return carry

        loop_rows(length, 64, norm, 0)
        val_ref[0:PAD, :] = jnp.zeros((PAD, CB), f32)

    biased_ref[:, 0:PAD, :] = jnp.zeros((3, PAD, CB), f32)
    for stream in range(3):
        biased = dot(normed_ref[...], win_ref[stream], NT) + chan_ref[stream : stream + 1, :]
        biased_ref[stream, PAD:, :] = biased

    rows = 32

    def shorten(row, carry):
        out = []
        for stream in range(3):
            now, one, two = earlier(biased_ref, (stream,), row, rows, CB, split)
            out.append(
                chan_ref[3 + stream : 4 + stream, :] * now
                + chan_ref[6 + stream : 7 + stream, :] * one
                + chan_ref[9 + stream : 10 + stream, :] * two
            )
        query_ref[pl.ds(row, rows), :] = out[0]
        val_ref[pl.ds(row + PAD, rows), :] = out[2]
        prod_ref[pl.ds(row, rows), :] = out[1] * out[2]
        return carry

    loop_rows(length, rows, shorten, 0)

    def condition(row, total):
        now, one, two = earlier(val_ref, (), row, rows, CB, split)
        cond = chan_ref[12:13, :] * now + chan_ref[13:14, :] * one + chan_ref[14:15, :] * two
        return total + fold(cond * cond)

    squares = loop_rows(length, rows, condition, jnp.zeros((8, CB), f32))
    scale = jnp.sqrt(jnp.sum(squares, axis=0, keepdims=True) * (1.0 / length) + epsilon)
    scale_ref[...] = jnp.broadcast_to(scale, (8, CB))

    for part in range(parts):
        spec_ref[part] = transform_fine(
            fwd_ref[...], load_part(prod_ref, part, parts, boundary, split)
        )

    def pairs_into(part, bound):
        low = 0 if part <= bound else bound + 1
        return [(part - source, source) for source in range(low, part + 1)]

    for bound in range(parts - 1):

        @pl.when(boundary == bound)
        def _():
            def multiply(row, carry):
                k_re = [khat_ref[m, pl.ds(row, 8), :] for m in range(parts - 1)]
                k_im = [khat_ref[m, pl.ds(row + BLK, 8), :] for m in range(parts - 1)]
                s_re = [spec_ref[v, pl.ds(row, 8), :] for v in range(parts)]
                s_im = [spec_ref[v, pl.ds(row + BLK, 8), :] for v in range(parts)]
                for part in range(parts):
                    pairs = pairs_into(part, bound)
                    res_ref[part, pl.ds(row, 8), :] = sum_terms(
                        [k_re[m] * s_re[v] - k_im[m] * s_im[v] for m, v in pairs]
                    )
                    res_ref[part, pl.ds(row + BLK, 8), :] = sum_terms(
                        [k_re[m] * s_im[v] + k_im[m] * s_re[v] for m, v in pairs]
                    )
                return carry

            loop_rows(BLK, 8, multiply, 0)
            top = first_row((8, CB))
            for part in range(parts):
                pairs = pairs_into(part, bound)
                for base in (0, BLK):
                    real = sum_terms(
                        [khat_ref[m, base : base + 8, :] * spec_ref[v, base : base + 8, :] for m, v in pairs]
                    )
                    res_ref[part, base : base + 8, :] = jnp.where(
                        top, real, res_ref[part, base : base + 8, :]
                    )

    for part in range(parts):
        store_part(conv_ref, part, boundary, split, transform_fine(inv_ref[...], res_ref[part]))

    mixed = (query_ref[...] * scale * conv_ref[...]).astype(bf16)
    update = dot(mixed, wout_ref[...], NN)

    @pl.when(step == 0)
    def _():
        middle_ref[...] = update

    @pl.when(step > 0)
    def _():
        middle_ref[...] += update

    @pl.when(step == pl.num_programs(0) - 1)
    def _():
        def finish(row, carry):
            here = pl.ds(row, 64)
            middle = state_ref[here, :] + middle_ref[here, :] + norm_ref[4:5, :]
            middle_ref[here, :] = middle
            hat, _ = norm_parts(middle)
            second_ref[here, :] = (hat * norm_ref[2:3, :] + norm_ref[3:4, :]).astype(bf16)
            return carry

        loop_rows(length, 64, finish, 0)


def whole_block(shape):
    return pl.BlockSpec(shape, lambda *index: (0,) * len(shape))


def fixed_block(shape):
    return pl.BlockSpec(shape, lambda *index: (0,) * len(shape), pipeline_mode=pl.Buffered(1))


def mixer_forward(after, split, state, norm_pack, chan_pack, w_in, khat, w_out):
    length, width = state.shape
    steps = width // CB
    parts = length // BLK + 1
    forward = jnp.asarray(split_low(FORWARD))
    inverse = jnp.asarray(split_low(INVERSE))
    return call_after(
        after,
        mixer_forward_kernel,
        grid=(steps,),
        in_specs=[
            pl.BlockSpec(memory_space=pltpu.SMEM),
            fixed_block((length, width)),
            fixed_block(norm_pack.shape),
            pl.BlockSpec((16, CB), lambda i: (0, i)),
            pl.BlockSpec((3, CB, width), lambda i: (0, i, 0)),
            pl.BlockSpec((parts - 1, BINS, CB), lambda i: (0, 0, i)),
            fixed_block(forward.shape),
            fixed_block(inverse.shape),
            pl.BlockSpec((CB, width), lambda i: (i, 0)),
        ],
        out_specs=[
            whole_block((length, width)),
            whole_block((length, width)),
            whole_block((length, width)),
            pl.BlockSpec((3, length + PAD, CB), lambda i: (0, 0, i)),
            pl.BlockSpec((length, CB), lambda i: (0, i)),
            pl.BlockSpec((8, CB), lambda i: (0, i)),
        ],
        out_shape=[
            jax.ShapeDtypeStruct((length, width), f32),
            jax.ShapeDtypeStruct((length, width), bf16),
            jax.ShapeDtypeStruct((length, width), bf16),
            jax.ShapeDtypeStruct((3, length + PAD, width), f32),
            jax.ShapeDtypeStruct((length, width), f32),
            jax.ShapeDtypeStruct((8, width), f32),
        ],
        scratch_shapes=[
            pltpu.VMEM((length + PAD, CB), f32),
            pltpu.VMEM((length, CB), f32),
            pltpu.VMEM((length, CB), f32),
            pltpu.VMEM((parts, BINS, CB), f32),
            pltpu.VMEM((parts, BINS, CB), f32),
        ],
        compiler_params=pltpu.CompilerParams(vmem_limit_bytes=VMEM),
        cost_estimate=cost(20e9, 40 * 2**20),
        name="mixer_forward",
    )(split, state, norm_pack, chan_pack, w_in.reshape(3, width, width), khat, forward, inverse, w_out)


PARTS = 2


def call_after(after, kernel, in_specs, **options):
    count = len(after)

    def run(*refs):
        kernel(*refs[count:])

    call = pl.pallas_call(
        run, in_specs=[pl.BlockSpec(memory_space=pl.ANY)] * count + in_specs, **options
    )
    return functools.partial(call, *after)


def cost(flops, moved):
    return pl.CostEstimate(flops=int(flops), bytes_accessed=int(moved), transcendentals=0)


def flat(block):
    return block.reshape(-1, block.shape[-1])


def load_weights(masks, taken, me_ref, refs, up_ref, down_ref, sems):
    moves = []
    size, piece = down_ref.shape[0] // len(taken), down_ref.shape[1]
    for array, own in zip(refs, masks):
        for slot, mask in enumerate(own):
            device = slot if mask is None else me_ref[0] ^ mask
            for part, source in enumerate(taken):
                start = 3 * piece * source
                targets = [
                    up_ref.at[2 * (size * part + device)],
                    up_ref.at[2 * (size * part + device) + 1],
                    down_ref.at[size * part + device],
                ]
                for place, target in enumerate(targets):
                    rows = slice(start + place * piece, start + (place + 1) * piece)
                    moves.append(
                        pltpu.make_async_copy(array.at[slot, rows, :], target, sems.at[len(moves)])
                    )
    for move in moves:
        move.start()
    return moves


def weight_blocks(up_ref, down_ref, parts, inner, count, step):
    size = down_ref.shape[0] // parts
    part, block = step // inner, step % inner
    base = block * count
    return (
        flat(up_ref[pl.ds(2 * size * part + base, count)]),
        flat(up_ref[pl.ds(2 * size * part + size + base, count)]),
        flat(down_ref[pl.ds(size * part + base, count)]),
    )


def gated_forward_kernel(first, masks, taken, block, me_ref, second_ref, middle_ref, norm_ref, *refs):
    step = pl.program_id(0)
    length = second_ref.shape[0]
    rows = 256
    if masks:
        gate_ref, value_ref, out_ref, up_ref, down_ref, sems = refs[len(masks) :]

        @pl.when(step == 0)
        def _():
            moves = load_weights(masks, taken, me_ref, refs[: len(masks)], up_ref, down_ref, sems)
            for move in moves:
                move.wait()

    else:
        up_ref, down_ref, gate_ref, value_ref, out_ref = refs
    count = block // down_ref.shape[1]
    parts = len(taken)
    gate_w, value_w, down_w = weight_blocks(
        up_ref, down_ref, parts, pl.num_programs(0) // parts, count, step
    )

    @pl.when(step == 0)
    def _():
        if first:
            out_ref[...] = middle_ref[...] + norm_ref[5:6, :]
        else:
            out_ref[...] = middle_ref[...]

    for row in range(0, length, rows):
        here = slice(row, row + rows)
        gate = dot(second_ref[here, :], gate_w, NT)
        value = dot(second_ref[here, :], value_w, NT)
        gate_ref[here, :] = gate.astype(bf16)
        value_ref[here, :] = value.astype(bf16)
        bent = jnp.tanh(GELU_A * gate * (1.0 + GELU_B * gate * gate))
        hidden = (0.5 * gate * (1.0 + bent) * value).astype(bf16)
        out_ref[here, :] += dot(hidden, down_w, NN)


def pieces_of(weight, group):
    grouped = weight.reshape(-1, PARTS, group // PARTS, weight.shape[-1])
    return [grouped[:, part] for part in range(PARTS)]


def weight_operands(weights, parts):
    anywhere = pl.BlockSpec(memory_space=pl.ANY)
    if isinstance(weights, dict):
        arrays = [piece for piece, _ in weights["pieces"]]
        masks = [own for _, own in weights["pieces"]]
        size = sum(len(own) for own in masks)
        width = arrays[0].shape[2]
        piece = weights["rows"]
        scratch = [
            pltpu.VMEM((2 * size * parts, piece, width), bf16),
            pltpu.VMEM((size * parts, piece, width), bf16),
            pltpu.SemaphoreType.DMA((3 * size * parts,)),
        ]
        return arrays, [anywhere] * len(arrays), masks, scratch, piece
    return list(weights), [fixed_block(part.shape) for part in weights], None, [], weights[1].shape[1]


def gated_forward(after, me, second, weights, before, norm_pack, hidden, first, taken=(0,), block=768):
    length, width = second.shape
    steps = hidden // block
    arrays, specs, masks, scratch, _ = weight_operands(weights, len(taken))
    return call_after(
        after,
        functools.partial(gated_forward_kernel, first, masks, taken, block),
        grid=(steps,),
        in_specs=[
            pl.BlockSpec(memory_space=pltpu.SMEM),
            fixed_block((length, width)),
            fixed_block((length, width)),
            fixed_block(norm_pack.shape),
        ]
        + specs,
        out_specs=[
            pl.BlockSpec((length, block), lambda i: (0, i)),
            pl.BlockSpec((length, block), lambda i: (0, i)),
            whole_block((length, width)),
        ],
        out_shape=[
            jax.ShapeDtypeStruct((length, hidden), bf16),
            jax.ShapeDtypeStruct((length, hidden), bf16),
            jax.ShapeDtypeStruct((length, width), f32),
        ],
        scratch_shapes=scratch,
        compiler_params=pltpu.CompilerParams(vmem_limit_bytes=VMEM),
        cost_estimate=cost(6 * length * width * hidden, 20 * 2**20),
        name="gated_forward",
    )(me, second, before, norm_pack, *arrays)


def norm_backward(values, grad_out, gain):
    hat, rstd = norm_parts(values)
    grad_hat = grad_out * gain
    mean_one = jnp.mean(grad_hat, axis=-1, keepdims=True)
    mean_two = jnp.mean(grad_hat * hat, axis=-1, keepdims=True)
    return rstd * (grad_hat - mean_one - hat * mean_two), grad_out * hat


def gated_backward_kernel(
    first,
    last,
    masks,
    own_order,
    taken,
    block,
    me_ref,
    grad_ref,
    before_ref,
    second_ref,
    middle_ref,
    norm_ref,
    gate_ref,
    value_ref,
    *refs,
):
    step = pl.program_id(0)
    steps = pl.num_programs(0)
    length, width = grad_ref.shape
    rows = 256
    slots = bool(masks)
    if slots:
        pieces, refs = refs[: len(masks)], refs[len(masks) :]
    else:
        up_ref, down_ref = refs[:2]
        refs = refs[2:]
    one_ref, two_ref, out_ref, small_ref, glow_ref, hidden_ref, dgate_ref, dvalue_ref, stage_ref, sems = refs[:10]
    if slots:
        up_ref, down_ref, load_sems = refs[10:]
    piece = down_ref.shape[1]
    count = block // piece
    side = step % 2

    @pl.when(step == 0)
    def _():
        moves = []
        if slots:
            moves = load_weights(masks, taken, me_ref, pieces, up_ref, down_ref, load_sems)
        glow_ref[...] = grad_ref[...].astype(bf16)
        if first:
            out_ref[...] = jnp.zeros_like(out_ref)
        else:
            out_ref[...] = before_ref[...]
        for move in moves:
            move.wait()

    parts = len(taken)
    inner = steps // parts
    gate_w, value_w, down_w = weight_blocks(up_ref, down_ref, parts, inner, count, step)

    def copies(at_step, kind, item):
        source = stage_ref.at[at_step % 2, kind, pl.ds(item * piece, piece), :]
        half = at_step % inner * count + item
        start = at_step // inner * 3 * piece
        if not slots:
            if kind == 2:
                return source, [(None, two_ref.at[half])]
            return source, [(None, one_ref.at[half + kind * inner * count])]
        if kind == 2:
            device = half
            rows_at = pl.ds(start + 2 * piece, piece)
        else:
            device = (half >> 1) + kind * (inner * count >> 1)
            rows_at = pl.ds(start + (half & 1) * piece, piece)
        if not own_order:
            return source, [(None, one_ref.at[device, rows_at, :])]
        mask = device ^ me_ref[0]
        place = mask >> 1
        core = mask & 1
        return source, [
            (core == 0, one_ref.at[place, rows_at, :]),
            (core == 1, two_ref.at[place, rows_at, :]),
        ]

    def send(kind):
        def go(item, carry):
            source, targets = copies(step, kind, item)
            for condition, target in targets:
                move = pltpu.make_async_copy(source, target, sems.at[side, kind, item])
                if condition is None:
                    move.start()
                else:
                    pl.when(condition)(move.start)
            return carry

        lax.fori_loop(0, count, go, 0)

    def drain(at_step):
        def go(item, carry):
            for kind in range(3):
                source, targets = copies(at_step, kind, item)
                pltpu.make_async_copy(
                    source, targets[0][1], sems.at[at_step % 2, kind, item]
                ).wait()
            return carry

        lax.fori_loop(0, count, go, 0)

    for row in range(0, length, rows):
        here = slice(row, row + rows)
        grad_hidden = dot(glow_ref[here, :], down_w, NT)
        gate = gate_ref[here, :].astype(f32)
        value = value_ref[here, :].astype(f32)
        square = gate * gate
        bent = jnp.tanh(GELU_A * gate * (1.0 + GELU_B * square))
        half = 0.5 * (1.0 + bent)
        unit = half * gate
        slope = half + 0.5 * gate * (1.0 - bent * bent) * (GELU_A * (1.0 + 3.0 * GELU_B * square))
        hidden_ref[here, :] = (unit * value).astype(bf16)
        dgate = (grad_hidden * value * slope).astype(bf16)
        dvalue = (grad_hidden * unit).astype(bf16)
        dgate_ref[here, :] = dgate
        dvalue_ref[here, :] = dvalue
        out_ref[here, :] += dot(dgate, gate_w, NN) + dot(dvalue, value_w, NN)

    @pl.when(step > 1)
    def _():
        drain(step - 2)

    stage_ref[side, 0] = dot(dgate_ref[...], second_ref[...], TN).astype(bf16)
    send(0)
    stage_ref[side, 1] = dot(dvalue_ref[...], second_ref[...], TN).astype(bf16)
    send(1)
    stage_ref[side, 2] = dot(hidden_ref[...], glow_ref[...], TN).astype(bf16)
    send(2)

    @pl.when(step == steps - 1)
    def _():
        if not last:
            small_ref[...] = jnp.zeros_like(small_ref)
        else:

            def finish(row, carry):
                here = pl.ds(row, 32)
                grad_out = out_ref[here, :]
                grad = grad_ref[here, :]
                change, gain_rows = norm_backward(middle_ref[here, :], grad_out, norm_ref[2:3, :])
                total = grad + change
                out_ref[here, :] = total
                return (
                    carry[0] + fold(gain_rows),
                    carry[1] + fold(grad_out),
                    carry[2] + fold(total),
                    carry[3] + fold(grad),
                )

            zero = jnp.zeros((8, width), f32)
            sums = loop_rows(length, 32, finish, (zero, zero, zero, zero))
            small_ref[...] = jnp.concatenate(
                [jnp.sum(part, axis=0, keepdims=True) for part in sums]
                + [jnp.zeros((4, width), f32)],
                axis=0,
            )

        @pl.when(steps > 1)
        def _():
            drain(step - 1)

        drain(step)


def gated_backward(after,
    me, grad, before, second, middle, norm_pack, gate, value, weights, first, last, own_order, taken=(0,), block=768
):
    length, width = second.shape
    parts = len(taken)
    inner = gate.shape[1] // block
    start = 0
    if isinstance(weights, dict):
        start = taken[0] * inner // PARTS
        inner = parts * inner // PARTS
    hidden = inner * block
    arrays, specs, masks, scratch, piece = weight_operands(weights, parts)
    count = block // piece
    column = pl.BlockSpec((length, block), lambda i: (0, i + start))
    anywhere = pl.BlockSpec(memory_space=pl.ANY)
    if masks:
        size = sum(len(own) for own in masks)
        places = [jax.ShapeDtypeStruct((size // 2, 3 * piece * parts, width), bf16)] * 2
        if not own_order:
            places = [
                jax.ShapeDtypeStruct((size, 3 * piece * parts, width), bf16),
                jax.ShapeDtypeStruct((16, width), bf16),
            ]
    else:
        places = [jax.ShapeDtypeStruct(array.shape, bf16) for array in arrays]
    return call_after(
        after,
        functools.partial(
            gated_backward_kernel, first, last, masks, own_order, taken, block
        ),
        grid=(inner,),
        in_specs=[
            pl.BlockSpec(memory_space=pltpu.SMEM),
            fixed_block((length, width)),
            fixed_block(before.shape),
            fixed_block((length, width)),
            fixed_block((length, width)),
            fixed_block(norm_pack.shape),
            column,
            column,
        ]
        + specs,
        out_specs=[anywhere, anywhere, whole_block((length, width)), whole_block((8, width))],
        out_shape=places
        + [
            jax.ShapeDtypeStruct((length, width), f32),
            jax.ShapeDtypeStruct((8, width), f32),
        ],
        scratch_shapes=[
            pltpu.VMEM((length, width), bf16),
            pltpu.VMEM((length, block), bf16),
            pltpu.VMEM((length, block), bf16),
            pltpu.VMEM((length, block), bf16),
            pltpu.VMEM((2, 3, block, width), bf16),
            pltpu.SemaphoreType.DMA((2, 3, count)),
        ]
        + scratch,
        compiler_params=pltpu.CompilerParams(vmem_limit_bytes=VMEM),
        cost_estimate=cost(12 * length * width * hidden, 20 * 2**20),
        name="gated_backward",
    )(me, grad, before, second, middle, norm_pack, gate, value, *arrays)


def mixer_backward_kernel(
    first,
    last,
    split_ref,
    grad_ref,
    before_ref,
    normed_ref,
    chan_ref,
    biased_ref,
    conv_ref,
    scale_ref,
    khat_ref,
    fwd_ref,
    inv_ref,
    wout_ref,
    win_ref,
    kernel_ref,
    inner_t_ref,
    slope_ref,
    features_t_ref,
    freq_out_ref,
    inner_before_ref,
    win_g_ref,
    wout_g_ref,
    chan_g_ref,
    inner_g_ref,
    freq_g_ref,
    out_ref,
    mlow_ref,
    kern_g_ref,
    key_ref,
    val_ref,
    prod_ref,
    dconv_ref,
    mixed_ref,
    cond_ref,
    dpad_ref,
    low_ref,
    spec_ref,
    dspec_ref,
    res_ref,
    gram_ref,
):
    step = pl.program_id(0)
    length, width = grad_ref.shape
    split = split_ref[0]
    boundary = split // BLK
    parts = length // BLK + 1
    rows = 32

    @pl.when(step == 0)
    def _():
        mlow_ref[...] = grad_ref[...].astype(bf16)
        val_ref[0:PAD, :] = jnp.zeros((PAD, CB), f32)
        cond_ref[length:, :] = jnp.zeros((PAD, CB), f32)
        dpad_ref[:, length:, :] = jnp.zeros((3, PAD, CB), f32)

    dconv_ref[...] = dot(mlow_ref[...], wout_ref[...], NT)
    scale = scale_ref[0:1, :]

    def gate(row, total):
        here = pl.ds(row, rows)
        out = []
        for stream in range(3):
            now, one, two = earlier(biased_ref, (stream,), row, rows, CB, split)
            out.append(
                chan_ref[3 + stream : 4 + stream, :] * now
                + chan_ref[6 + stream : 7 + stream, :] * one
                + chan_ref[9 + stream : 10 + stream, :] * two
            )
        query, key, value = out
        key_ref[here, :] = key
        val_ref[pl.ds(row + PAD, rows), :] = value
        prod_ref[here, :] = key * value
        grad = dconv_ref[here, :]
        conv = conv_ref[here, :]
        mixed_ref[here, :] = (query * scale * conv).astype(bf16)
        dpad_ref[0, here, :] = grad * scale * conv
        through = grad * query
        dconv_ref[here, :] = through * scale
        return total + fold(through * conv)

    scale_sum = loop_rows(length, rows, gate, jnp.zeros((8, CB), f32))
    grad_scale = jnp.sum(scale_sum, axis=0, keepdims=True)
    factor = grad_scale / (scale * float(length))

    def condition(row, carry):
        now, one, two = earlier(val_ref, (), row, rows, CB, split)
        cond_ref[pl.ds(row, rows), :] = (
            chan_ref[12:13, :] * now + chan_ref[13:14, :] * one + chan_ref[14:15, :] * two
        )
        return carry

    loop_rows(length, rows, condition, 0)

    for part in range(parts):
        spec_ref[part] = transform(fwd_ref[...], load_part(prod_ref, part, parts, boundary, split))
        dspec_ref[part] = transform(fwd_ref[...], load_part(dconv_ref, part, parts, boundary, split))

    def pairs_from(source, bound):
        high = bound if source <= bound else parts - 1
        return [(part - source, part) for part in range(source, high + 1)]

    def pairs_apart(lag, bound):
        found = []
        for source in range(parts - lag):
            if (source <= bound) == (source + lag <= bound):
                found.append((source, source + lag))
        return found

    odd_sign = jnp.where(lax.broadcasted_iota(jnp.int32, (8, CB), 0) % 2 == 0, 1.0, -1.0)

    def chain(grams):
        return [
            grams[lag] + odd_sign * grams[lag + 1] if lag + 1 < parts - 1 else grams[lag]
            for lag in range(parts - 1)
        ]

    def or_zero(terms):
        return sum_terms(terms) if terms else jnp.zeros((8, CB), f32)

    for bound in range(parts - 1):

        @pl.when(boundary == bound)
        def _():
            def multiply(row, carry):
                k_re = [khat_ref[m, pl.ds(row, 8), :] for m in range(parts - 1)]
                k_im = [khat_ref[m, pl.ds(row + BLK, 8), :] for m in range(parts - 1)]
                e_re = [dspec_ref[v, pl.ds(row, 8), :] for v in range(parts)]
                e_im = [dspec_ref[v, pl.ds(row + BLK, 8), :] for v in range(parts)]
                for source in range(parts):
                    pairs = pairs_from(source, bound)
                    res_ref[source, pl.ds(row, 8), :] = sum_terms(
                        [k_re[m] * e_re[v] + k_im[m] * e_im[v] for m, v in pairs]
                    )
                    res_ref[source, pl.ds(row + BLK, 8), :] = sum_terms(
                        [k_re[m] * e_im[v] - k_im[m] * e_re[v] for m, v in pairs]
                    )
                s_re = [spec_ref[v, pl.ds(row, 8), :] for v in range(parts)]
                s_im = [spec_ref[v, pl.ds(row + BLK, 8), :] for v in range(parts)]
                real, imag = [], []
                for lag in range(parts - 1):
                    pairs = pairs_apart(lag, bound)
                    real.append(
                        or_zero([s_re[j] * e_re[i] + s_im[j] * e_im[i] for j, i in pairs])
                    )
                    imag.append(
                        or_zero([s_re[j] * e_im[i] - s_im[j] * e_re[i] for j, i in pairs])
                    )
                for lag, (one, two) in enumerate(zip(chain(real), chain(imag))):
                    gram_ref[lag, pl.ds(row, 8), :] = one
                    gram_ref[lag, pl.ds(row + BLK, 8), :] = two
                return carry

            loop_rows(BLK, 8, multiply, 0)
            top = first_row((8, CB))
            for base in (0, BLK):
                tile = slice(base, base + 8)
                for source in range(parts):
                    real = sum_terms(
                        [khat_ref[m, tile, :] * dspec_ref[v, tile, :] for m, v in pairs_from(source, bound)]
                    )
                    res_ref[source, tile, :] = jnp.where(top, real, res_ref[source, tile, :])
                grams = [
                    or_zero([spec_ref[j, tile, :] * dspec_ref[i, tile, :] for j, i in pairs_apart(lag, bound)])
                    for lag in range(parts - 1)
                ]
                for lag, real in enumerate(chain(grams)):
                    gram_ref[lag, tile, :] = jnp.where(top, real, gram_ref[lag, tile, :])

    for part in range(parts):
        store_part(prod_ref, part, boundary, split, transform(inv_ref[...], res_ref[part]))
    for lag in range(parts - 1):
        kern_g_ref[lag * BLK : (lag + 1) * BLK, :] = transform(inv_ref[...], gram_ref[lag])

    def spread(row, carry):
        here = pl.ds(row, rows)
        change = prod_ref[here, :]
        value = val_ref[pl.ds(row + PAD, rows), :]
        dpad_ref[1, here, :] = change * value
        now, one, two = later(cond_ref, (), row, rows, CB, split)
        from_cond = chan_ref[12:13, :] * now + chan_ref[13:14, :] * one + chan_ref[14:15, :] * two
        dpad_ref[2, here, :] = change * key_ref[here, :] + factor * from_cond
        return (
            carry[0] + fold(value * now),
            carry[1] + fold(value * one),
            carry[2] + fold(value * two),
        )

    zero = jnp.zeros((8, CB), f32)
    cond_sums = loop_rows(length, rows, spread, (zero, zero, zero))
    sums = [None] * 12
    for stream in range(3):

        def back(row, carry, stream=stream):
            now, one, two = later(dpad_ref, (stream,), row, rows, CB, split)
            biased = biased_ref[stream, pl.ds(row + PAD, rows), :]
            change = (
                chan_ref[3 + stream : 4 + stream, :] * now
                + chan_ref[6 + stream : 7 + stream, :] * one
                + chan_ref[9 + stream : 10 + stream, :] * two
            )
            low_ref[stream, pl.ds(row, rows), :] = change.astype(bf16)
            return (
                carry[0] + fold(change),
                carry[1] + fold(biased * now),
                carry[2] + fold(biased * one),
                carry[3] + fold(biased * two),
            )

        got = loop_rows(length, rows, back, (zero, zero, zero, zero))
        for index in range(4):
            sums[3 * index + stream] = got[index]
    decay = chan_ref[15:16, :]
    level = jnp.sqrt(2.0 * decay)
    lead = 0.5 / decay

    def profile(row, total):
        here = pl.ds(row, rows)
        position = row_mask(row, rows, CB).astype(f32)
        change = kern_g_ref[here, :]
        kern_g_ref[here, :] = change * (jnp.exp(-position * decay) * level)
        return total + fold(change * kernel_ref[here, :] * (lead - position))

    decay_sum = loop_rows(length, rows, profile, zero)
    chan_g_ref[0:16, :] = jnp.concatenate(
        [jnp.sum(part, axis=0, keepdims=True) for part in sums]
        + [factor * jnp.sum(part, axis=0, keepdims=True) for part in cond_sums]
        + [jnp.sum(decay_sum, axis=0, keepdims=True)],
        axis=0,
    )
    chan_g_ref[16:, :] = dot_fine(inner_t_ref[...], kern_g_ref[...], NN)
    inner_g = dot_fine(kern_g_ref[...], freq_out_ref[...], NT)

    @pl.when(step == 0)
    def _():
        if first:
            inner_g_ref[...] = inner_g
        else:
            inner_g_ref[...] = inner_before_ref[...] + inner_g

    @pl.when(step > 0)
    def _():
        inner_g_ref[...] += inner_g

    wout_g_ref[...] = dot(mixed_ref[...], mlow_ref[...], TN).astype(bf16)
    for stream in range(3):
        win_g_ref[stream] = dot(low_ref[stream], normed_ref[...], TN).astype(bf16)
    update = sum_terms([dot(low_ref[stream], win_ref[stream], NN) for stream in range(3)])

    @pl.when(step == 0)
    def _():
        if first:
            out_ref[...] = update
        else:
            out_ref[...] = before_ref[...] + update

    @pl.when(step > 0)
    def _():
        out_ref[...] += update

    if not last:
        freq_g_ref[...] = jnp.zeros_like(freq_g_ref)
        return

    @pl.when(step == pl.num_programs(0) - 1)
    def _():
        phase_g = inner_g_ref[...] * slope_ref[...]
        freq_g_ref[0 : phase_g.shape[1], :] = dot_fine(features_t_ref[...], phase_g, NN)
        freq_g_ref[phase_g.shape[1] :, :] = fold(phase_g)
def mixer_backward(after, start, steps, split, grad, before, normed, chan_pack, biased, conv, scale, khat, w_out, w_in, filtered, freq_out, inner_before):
    length, width = grad.shape
    last = (start + steps) * CB == width
    parts = length // BLK + 1
    forward = jnp.asarray(FORWARD, bf16)
    inverse = jnp.asarray(INVERSE, bf16)
    kernel, inner_t, slope, features_t = filtered
    hidden = freq_out.shape[0]
    full = fixed_block((length, width))
    tall = pltpu.VMEM((length, CB), f32)
    tall_pad = pltpu.VMEM((length + PAD, CB), f32)
    spectrum = pltpu.VMEM((parts, BINS, CB), f32)
    return call_after(
        after,
        functools.partial(mixer_backward_kernel, start == 0, last),
        grid=(steps,),
        in_specs=[
            pl.BlockSpec(memory_space=pltpu.SMEM),
            full,
            fixed_block(before.shape),
            full,
            pl.BlockSpec((16, CB), lambda i: (0, i + start)),
            pl.BlockSpec((3, length + PAD, CB), lambda i: (0, 0, i + start)),
            pl.BlockSpec((length, CB), lambda i: (0, i + start)),
            pl.BlockSpec((8, CB), lambda i: (0, i + start)),
            pl.BlockSpec((parts - 1, BINS, CB), lambda i: (0, 0, i + start)),
            fixed_block(forward.shape),
            fixed_block(inverse.shape),
            pl.BlockSpec((CB, width), lambda i: (i + start, 0)),
            pl.BlockSpec((3, CB, width), lambda i: (0, i + start, 0)),
            pl.BlockSpec((length, CB), lambda i: (0, i + start)),
            fixed_block(inner_t.shape),
            fixed_block(slope.shape),
            fixed_block(features_t.shape),
            pl.BlockSpec((freq_out.shape[0], CB), lambda i: (0, i + start)),
            fixed_block(inner_before.shape),
        ],
        out_specs=[
            pl.BlockSpec((3, CB, width), lambda i: (0, i, 0)),
            pl.BlockSpec((CB, width), lambda i: (i, 0)),
            pl.BlockSpec((16 + hidden, CB), lambda i: (0, i)),
            whole_block((length, hidden)),
            whole_block((hidden + 8, hidden)),
            whole_block((length, width)),
        ],
        out_shape=[
            jax.ShapeDtypeStruct((3, steps * CB, width), bf16),
            jax.ShapeDtypeStruct((steps * CB, width), bf16),
            jax.ShapeDtypeStruct((16 + hidden, steps * CB), f32),
            jax.ShapeDtypeStruct((length, hidden), f32),
            jax.ShapeDtypeStruct((hidden + 8, hidden), f32),
            jax.ShapeDtypeStruct((length, width), f32),
        ],
        scratch_shapes=[
            pltpu.VMEM((length, width), bf16),
            tall,
            tall,
            tall_pad,
            tall,
            tall,
            pltpu.VMEM((length, CB), bf16),
            tall_pad,
            pltpu.VMEM((3, length + PAD, CB), f32),
            pltpu.VMEM((3, length, CB), bf16),
            spectrum,
            spectrum,
            spectrum,
            pltpu.VMEM((parts - 1, BINS, CB), f32),
        ],
        compiler_params=pltpu.CompilerParams(vmem_limit_bytes=VMEM),
        cost_estimate=cost(12e9 * steps, 14 * 2**20 * steps),
        name="mixer_backward",
    )(
        split,
        grad,
        before,
        normed,
        chan_pack,
        biased,
        conv,
        scale,
        khat,
        forward,
        inverse,
        w_out,
        w_in.reshape(3, width, width),
        kernel,
        inner_t,
        slope,
        features_t,
        freq_out,
        inner_before,
    )


def norm_finish_kernel(acc_ref, state_ref, grad_ref, norm_ref, out_ref, small_ref):
    length, width = state_ref.shape

    def finish(row, carry):
        here = pl.ds(row, 32)
        grad_out = acc_ref[here, :]
        change, gain_rows = norm_backward(state_ref[here, :], grad_out, norm_ref[0:1, :])
        out_ref[here, :] = grad_ref[here, :] + change
        return carry[0] + fold(gain_rows), carry[1] + fold(grad_out)

    @pl.when(pl.program_id(0) == 0)
    def _():
        small_ref[...] = jnp.zeros_like(small_ref)

    zero = jnp.zeros((8, width), f32)
    got = loop_rows(length, 32, finish, (zero, zero))
    small_ref[...] += jnp.concatenate(
        [jnp.sum(part, axis=0, keepdims=True) for part in got] + [jnp.zeros((6, width), f32)], axis=0
    )


def norm_finish(after, acc, state, grad, norm_pack, block=256):
    length, width = state.shape
    tile = pl.BlockSpec((block, width), lambda i: (i, 0))
    return call_after(
        after,
        norm_finish_kernel,
        grid=(length // block,),
        in_specs=[tile, tile, tile, whole_block(norm_pack.shape)],
        out_specs=[tile, whole_block((8, width))],
        out_shape=[
            jax.ShapeDtypeStruct((length, width), f32),
            jax.ShapeDtypeStruct((8, width), f32),
        ],
        compiler_params=pltpu.CompilerParams(vmem_limit_bytes=VMEM),
        cost_estimate=cost(3e9, 16 * 2**20),
        name="norm_finish",
    )(acc, state, grad, norm_pack)


def filter_features(length, count):
    half = count // 2
    positions = np.arange(length, dtype=np.float64)[:, None]
    harmonics = np.arange(1, half + 1, dtype=np.float64)[None, :]
    angles = 2.0 * np.pi * ((positions * harmonics) % length) / length
    return np.concatenate([np.sin(angles), np.cos(angles)], axis=1).astype(np.float32)


def highest(left, right, dims):
    return lax.dot_general(left, right, dims, precision=lax.Precision.HIGHEST)


def filter_kernel_body(inner_ref, out_ref, chan_ref, fwd_ref, kernel_ref, khat_ref):
    length = inner_ref.shape[0]
    decay = chan_ref[15:16, :]
    level = jnp.sqrt(2.0 * decay)
    sign = jnp.where(lax.broadcasted_iota(jnp.int32, (BINS, CB), 0) % 2 == 0, 1.0, -1.0)
    before = None
    for block in range(length // BLK):
        here = slice(block * BLK, (block + 1) * BLK)
        profile = dot_fine(inner_ref[here, :], out_ref[...], NN)
        position = row_mask(block * BLK, BLK, CB).astype(f32)
        kernel = profile * (jnp.exp(-position * decay) * level)
        kernel_ref[here, :] = kernel
        spectrum = transform_fine(fwd_ref[...], kernel)
        khat_ref[block] = spectrum if before is None else spectrum + sign * before
        before = spectrum


def filter_forward(length, chan_pack, freq_in, freq_bias, freq_out):
    table = filter_features(length, freq_in.shape[0])
    features = jnp.asarray(table)
    phase = highest(features, freq_in, NN) + freq_bias
    inner = jnp.sin(phase)
    width = freq_out.shape[1]
    hidden = inner.shape[1]
    forward = jnp.asarray(split_low(FORWARD))
    blocks = length // BLK
    kernel, khat = pl.pallas_call(
        filter_kernel_body,
        grid=(width // CB,),
        in_specs=[
            fixed_block((length, hidden)),
            pl.BlockSpec((hidden, CB), lambda i: (0, i)),
            pl.BlockSpec((16, CB), lambda i: (0, i)),
            fixed_block(forward.shape),
        ],
        out_specs=[
            pl.BlockSpec((length, CB), lambda i: (0, i)),
            pl.BlockSpec((blocks, BINS, CB), lambda i: (0, 0, i)),
        ],
        out_shape=[
            jax.ShapeDtypeStruct((length, width), f32),
            jax.ShapeDtypeStruct((blocks, BINS, width), f32),
        ],
        compiler_params=pltpu.CompilerParams(vmem_limit_bytes=VMEM),
        cost_estimate=cost(6e9, 10 * 2**20),
        name="filter_forward",
    )(inner, freq_out, chan_pack, forward)
    return khat, (kernel, inner.T, jnp.cos(phase), jnp.asarray(table.T.copy()))


def cube_orders(size):
    bits = [1 << place for place in range(1, size.bit_length() - 1)]
    if len(bits) < 2:
        return [bits + [1], bits + [1]]
    return [bits + [1], bits[:-2] + [bits[-1], bits[-2]] + [1]]


def slot_table(order, size):
    table = np.zeros(size, np.int32)
    for slot in range(size):
        mask = sum(bit for place, bit in enumerate(order) if slot >> place & 1)
        table[mask] = slot
    return table


def swap(values, bit, size):
    return lax.ppermute(values, AXES, [(index, index ^ bit) for index in range(size)])


def cube_gather(block, order, size, me):
    held = block[None]
    for bit in order:
        held = jnp.concatenate([held, swap(held, bit, size)], axis=0)
    places = jnp.asarray(slot_table(order, size))[jnp.arange(size, dtype=jnp.int32) ^ me]
    return jnp.take(held, places, axis=0)


def cube_scatter(blocks, order, size, me):
    masks = np.zeros(size, np.int32)
    masks[slot_table(order, size)] = np.arange(size)
    held = jnp.take(blocks, jnp.asarray(masks) ^ me, axis=0)
    for place in reversed(range(len(order))):
        half = 1 << place
        got = swap(held[half:], order[place], size)
        held = held[:half].astype(f32) + got.astype(f32)
        if place:
            held = held.astype(bf16)
    return held[0]


def cube_sum(values, size):
    for place in range(size.bit_length() - 1):
        values = values + swap(values, 1 << place, size)
    return values


def halves(rows):
    if rows < 32:
        return rows // 2
    return (rows // 2 + 15) // 16 * 16


def gather_rows(block, size, me):
    cut = halves(block.shape[0])
    orders = cube_orders(size)
    one = cube_gather(block[:cut], orders[0], size, me)
    two = cube_gather(block[cut:], orders[1], size, me)
    return jnp.concatenate([one, two], axis=1)


def scatter_rows(blocks, size, me):
    cut = halves(blocks.shape[1])
    orders = cube_orders(size)
    one = cube_scatter(blocks[:, :cut], orders[0], size, me)
    two = cube_scatter(blocks[:, cut:], orders[1], size, me)
    return jnp.concatenate([one, two], axis=0)


def hold(value, *others):
    for other in others:
        value = value + (other[(0,) * other.ndim] * 0).astype(value.dtype)
    return value


def hold_place(value, *others):
    if not others:
        return value
    anywhere = pl.BlockSpec(memory_space=pl.ANY)

    def nothing(*refs):
        pass

    return pl.pallas_call(
        nothing,
        in_specs=[anywhere] * (1 + len(others)),
        out_specs=anywhere,
        out_shape=jax.ShapeDtypeStruct(value.shape, value.dtype),
        input_output_aliases={0: 0},
        cost_estimate=cost(0, 0),
        name="hold_place",
    )(value, *others)


def gather_steps(block, after, clock, done):
    size = 32
    block = hold(block, *after)
    came = [swap(block, bit, size) for bit in (2, 4, 6)]
    yield [block]
    line = hold(jnp.stack([block] + came), *clock)
    others = [swap(line, bit, size) for bit in (8, 16, 24)]
    own = swap(line, 1, size)
    yield [line]
    others = [hold_place(other, *clock) for other in others]
    pieces = []
    for bit, piece in zip((0, 8, 16, 24), [line] + others):
        masks = tuple(bit + place for place in (0, 2, 4, 6))
        pieces.append((piece, masks))
        other = swap(piece, 1, size) if bit else own
        pieces.append((other, tuple(mask + 1 for mask in masks)))
    yield others
    done(pieces)


def place_kernel(masks, cuts, me_ref, *refs):
    pieces = refs[: len(masks)]
    targets = refs[len(masks) : len(masks) + len(cuts)]
    held, in_sems, out_sems = refs[-3:]
    loads = []
    slot = 0
    for index, (piece, own) in enumerate(zip(pieces, masks)):
        load = pltpu.make_async_copy(piece, held.at[slot : slot + len(own)], in_sems.at[index])
        load.start()
        loads.append((load, slot, own))
        slot += len(own)
    moves = []
    for load, slot, own in loads:
        load.wait()
        for place, mask in enumerate(own):
            device = me_ref[0] ^ mask
            start = 0
            for target, rows in zip(targets, cuts):
                move = pltpu.make_async_copy(
                    held.at[slot + place, start : start + rows, :],
                    target.at[device],
                    out_sems.at[len(moves)],
                )
                move.start()
                moves.append(move)
                start += rows
    for move in moves:
        move.wait()


def place_pieces(pieces, cuts, me):
    arrays = [piece for piece, _ in pieces]
    masks = [own for _, own in pieces]
    size = sum(len(own) for own in masks)
    width = arrays[0].shape[-1]
    anywhere = pl.BlockSpec(memory_space=pl.ANY)
    return pl.pallas_call(
        functools.partial(place_kernel, masks, cuts),
        in_specs=[pl.BlockSpec(memory_space=pltpu.SMEM)] + [anywhere] * len(arrays),
        out_specs=[anywhere] * len(cuts),
        out_shape=[jax.ShapeDtypeStruct((size, rows, width), bf16) for rows in cuts],
        scratch_shapes=[
            pltpu.VMEM((size, sum(cuts), width), bf16),
            pltpu.SemaphoreType.DMA((len(masks),)),
            pltpu.SemaphoreType.DMA((size * len(cuts),)),
        ],
        compiler_params=pltpu.CompilerParams(vmem_limit_bytes=VMEM),
        cost_estimate=cost(0, 2 * sum(cuts) * size * width * 2),
        name="place_pieces",
    )(me, *arrays)


def scatter_steps(keep, send, clock, done):
    size = 32
    shape = (4, 4) + keep.shape[1:]
    keep = keep.reshape(shape)
    got = swap(send, 1, size).reshape(shape)
    yield [send]

    def both(group):
        return keep[group].astype(f32) + got[group].astype(f32)

    out = [hold(both(group), *clock).astype(bf16) for group in (3, 1, 2)]
    came = [swap(piece, bit, size) for piece, bit in zip(out, (24, 8, 16))]
    yield out
    line = hold(sum_terms([both(0)] + [piece.astype(f32) for piece in came]), *clock)
    low = [line[place].astype(bf16) for place in (1, 2, 3)]
    came = [swap(piece, 2 * place + 2, size) for place, piece in enumerate(low)]
    yield low
    done(hold(sum_terms([line[0]] + [piece.astype(f32) for piece in came]), *clock))


def sum_steps(values, size, me, done, after=()):
    halved = values.reshape((2, -1) + values.shape[1:])
    core = me % 2
    send = jnp.take(halved, 1 - core, axis=0, mode="clip")
    part = jnp.take(halved, core, axis=0, mode="clip") + swap(send, 1, size)
    yield [send]
    part = hold(part, *after)
    for place in reversed(range(1, size.bit_length() - 1)):
        came = swap(part, 1 << place, size)
        yield [part]
        part = part + came
    other = swap(part, 1, size)
    yield [part]
    done(jnp.concatenate([jnp.where(core == 0, part, other), jnp.where(core == 0, other, part)], axis=0))


def body(
    size,
    tokens,
    split_point,
    cotangent,
    norm_gain,
    norm_shift,
    in_weight,
    in_bias,
    short_taps,
    cond_taps,
    decay_rate,
    freq_in,
    freq_bias,
    freq_out,
    out_weight,
    out_bias,
    up_weight,
    down_weight,
    down_bias,
):
    layers = in_weight.shape[0]
    length, width = tokens.shape[1:]
    me = lax.axis_index(AXES)
    split = split_point.astype(jnp.int32)
    state = tokens[0].astype(f32)
    in_rows = in_weight.shape[2]
    out_rows = out_weight.shape[1]

    packs = []
    for layer in range(layers):
        norm_pack = jnp.concatenate(
            [
                jnp.stack([norm_gain[layer, 0], norm_shift[layer, 0]]),
                jnp.stack([norm_gain[layer, 1], norm_shift[layer, 1]]),
                out_bias[layer][None],
                down_bias[layer][None],
                jnp.zeros((2, width), f32),
            ]
        )
        chan_pack = jnp.concatenate(
            [
                in_bias[layer].reshape(3, width),
                short_taps[layer].reshape(9, width),
                cond_taps[layer],
                decay_rate[layer][None],
            ]
        )
        packs.append((norm_pack, chan_pack))

    mine = me.astype(jnp.int32)[None]
    up_rows = up_weight.shape[2]
    down_rows = down_weight.shape[1]
    special = size == 32
    clock = []
    mixer_w = [None] * layers
    gated_w = [[None] * PARTS for _ in range(layers)]
    hidden = size * down_rows // PARTS

    def mixer_block(layer):
        return jnp.concatenate([in_weight[layer].T, out_weight[layer]], axis=0)

    def mixer_weights(layer, rows):
        mixer_w[layer] = (
            rows[:, :in_rows].reshape(3 * width, width),
            rows[:, in_rows:].reshape(width, width),
        )

    def gather_mixer(layer, after):
        def done(pieces):
            (rows,) = place_pieces(pieces, (in_rows + out_rows,), mine)
            mixer_weights(layer, rows)

        return gather_steps(mixer_block(layer), after, clock, done)

    def gated_weights(layer, pieces):
        gated_w[layer] = {"pieces": pieces, "rows": down_rows // PARTS}

    def gather_gated(layer, after):
        return gather_steps(all_parts(layer), after, clock, functools.partial(gated_weights, layer))

    def whole_gather(block, *after):
        return lax.all_gather(hold(block, *after), AXES, axis=0)

    def all_parts(layer):
        halved = up_weight[layer].T.reshape(2, PARTS, -1, width)
        own = down_weight[layer].reshape(PARTS, -1, width)
        rows = []
        for part in range(PARTS):
            rows += [halved[0, part], halved[1, part], own[part]]
        return jnp.concatenate(rows, axis=0)

    def go(*names):
        sent = []
        for name in names:
            sent.extend(next(steps[name], ()))
        return sent

    filters = [None] * layers

    def make_filter(layer, *after):
        filters[layer] = filter_forward(
            length,
            packs[layer][1],
            hold(freq_in[layer], *after),
            freq_bias[layer],
            freq_out[layer],
        )

    for layer in range(layers):
        make_filter(layer)
    steps = {}
    if special:
        steps[0, "mixer"] = gather_mixer(0, ())
    else:
        for layer in range(layers):
            mixer_weights(layer, gather_rows(mixer_block(layer), size, me))
            gated_block = jnp.concatenate([up_weight[layer].T, down_weight[layer]], axis=0)
            gated_rows = gather_rows(gated_block, size, me)
            ups = pieces_of(gated_rows[:, :up_rows].reshape(-1, width), 96)
            downs = pieces_of(gated_rows[:, up_rows:].reshape(-1, width), 96)
            gated_w[layer] = list(zip(ups, downs))

    saved = []
    outputs = []
    for layer in range(layers):
        norm_pack, chan_pack = packs[layer]
        waits = []
        ahead = (layer + 1, "mixer"), (layer + 1, "gated")
        more = special and layer + 1 < layers
        gated, ahead = (layer, "gated"), (layer + 1, "mixer")
        if special:
            if layer == 0:
                go((0, "mixer"))
                line = go((0, "mixer"))
                steps[gated] = gather_gated(0, line)
                go(gated)
                clock[:] = go((0, "mixer"))[:1]
            else:
                go((layer, "mixer"))
            waits = go(gated)
            if more:
                steps[ahead] = gather_mixer(layer + 1, waits)
                go(ahead)
            go((layer, "mixer"))
        w_in, w_out = mixer_w[layer]
        middle, second, normed, biased, conv, scale = mixer_forward(
            waits, split, state, norm_pack, chan_pack, w_in, filters[layer][0], w_out
        )
        waits = ()
        clock[:] = [middle]
        waits = []
        if special:
            go(gated)
            if more:
                waits = go(ahead)
                steps[layer + 1, "gated"] = gather_gated(layer + 1, [middle])
                go((layer + 1, "gated"))
            go(gated)
        total = middle
        kept = []
        if special:
            gate, value, total = gated_forward(
                waits,
                mine,
                second,
                gated_w[layer],
                total,
                norm_pack,
                PARTS * hidden,
                True,
                tuple(range(PARTS)),
            )
            clock[:] = [total]
            kept = [(gate, value)]
        else:
            for part in range(PARTS):
                gate, value, total = gated_forward(
                    [], mine, second, gated_w[layer][part], total, norm_pack, hidden, part == 0
                )
                kept.append((gate, value))
        saved.append((state, normed, biased, conv, scale, middle, second, kept))
        outputs.append(total)
        state = total

    gradient = cotangent[0].astype(f32)
    big = [None] * layers
    small = [None] * layers
    moving = {}

    def forward_on(*names):
        sent = []
        for name in names:
            if name in moving:
                sent.extend(next(moving[name], ()))
        return sent

    def whole_scatter(values):
        return lax.psum_scatter(values, AXES, scatter_dimension=0)

    nothing = jnp.zeros((8, width), f32)
    for layer in reversed(range(layers)):
        w_in, w_out = mixer_w[layer]
        norm_pack, chan_pack = packs[layer]
        state_in, normed, biased, conv, scale, middle, second, kept = saved[layer]
        passed = nothing
        gated_g = []
        by_steps = special and layer == 0
        owned = [None] * PARTS
        calls = [(part,) for part in range(PARTS)]
        if special and not by_steps:
            calls = [tuple(range(PARTS))]
        for index, taken in enumerate(calls):
            waits = []
            if by_steps:
                waits = forward_on("mixer", "part0")
            elif layer == layers - 1 and index == 0:
                waits = [state]
            if special:
                gate, value = kept[0]
                own = gated_w[layer]
            else:
                gate, value = kept[index]
                own = gated_w[layer][index]
            one, two, passed, sums_two = gated_backward(
                waits,
                mine,
                gradient,
                passed,
                second,
                middle,
                norm_pack,
                gate,
                value,
                own,
                index == 0,
                index == len(calls) - 1,
                by_steps,
                taken,
            )
            clock[:] = [sums_two]
            gated_g.append((one, two))
            if by_steps:
                moving[f"part{index}"] = scatter_steps(
                    one, two, clock, functools.partial(owned.__setitem__, index)
                )
        if special and not by_steps:
            rows = whole_scatter(gated_g[0][0])
            owned = [rows[part * rows.shape[0] // PARTS :][: rows.shape[0] // PARTS] for part in range(PARTS)]
        grad_middle = passed
        passed, inner_g = nothing, nothing
        found = []
        splits = [1] * (width // CB) if by_steps else [width // CB]
        start = 0
        for index, count in enumerate(splits):
            waits = []
            if by_steps:
                names = [("mixer", "part0", "part1"), (), ("part0", "part1")]
                waits = forward_on(*names[min(index, 2)])
            *got, inner_g, freq_g, passed = mixer_backward(
                waits,
                start,
                count,
                split,
                grad_middle,
                passed,
                normed,
                chan_pack,
                biased,
                conv,
                scale,
                filters[layer][0],
                w_out,
                w_in,
                filters[layer][1],
                freq_out[layer],
                inner_g,
            )
            clock[:] = [freq_g]
            found.append(got)
            start += count
        in_g = jnp.concatenate([got[0] for got in found], axis=1)
        out_g = jnp.concatenate([got[1] for got in found], axis=0)
        chan_g = jnp.concatenate([got[2] for got in found], axis=1)
        mixer_g = jnp.concatenate(
            [in_g.reshape(size, in_rows, width), out_g.reshape(size, out_rows, width)], axis=1
        )

        mixer_own = [None]
        waits = []
        if special:
            order = jnp.arange(size // 2, dtype=jnp.int32) * 2 ^ me
            if by_steps:
                forward_on("part0")
                order = hold(order, *forward_on("part1"))
            keep, send = [
                mixer_g.at[places].get(mode="promise_in_bounds") for places in (order, order ^ 1)
            ]
            while forward_on("mixer"):
                pass
            waits = [send]
            moving["mixer"] = scatter_steps(
                keep, send, clock, functools.partial(mixer_own.__setitem__, 0)
            )
        else:
            up_g = jnp.stack([one for one, _ in gated_g], axis=1).reshape(size, -1, width)
            down_g = jnp.stack([two for _, two in gated_g], axis=1).reshape(size, -1, width)
            owned = (scatter_rows(up_g, size, me), scatter_rows(down_g, size, me))
            mixer_own[0] = scatter_rows(mixer_g, size, me)
        gradient, sums_one = norm_finish(waits, passed, state_in, grad_middle, norm_pack)
        small[layer] = (chan_g, freq_g, sums_one, sums_two)
        big[layer] = (owned, mixer_own)

    def lines_of(values):
        return -(-values.size // (8 * width)) * 8

    def lined(values):
        lines = lines_of(values)
        flat_values = jnp.pad(values.reshape(-1), (0, lines * width - values.size))
        return flat_values.reshape(lines, width)

    vector = jnp.concatenate([lined(piece) for pieces in small for piece in pieces], axis=0)
    vector = jnp.pad(vector, ((0, -vector.shape[0] % 16), (0, 0)))
    if special:
        vector = hold(vector, send)
    summed = [None]
    sent = []
    moving["small"] = sum_steps(vector, size, me, functools.partial(summed.__setitem__, 0), sent)
    forward_on("mixer", "small")
    sent.extend(forward_on("mixer"))
    clock[:] = sent[:1]
    while forward_on("mixer", "small", "part1", "part0"):
        pass
    vector = summed[0]
    count = sum(lines_of(piece) for piece in small[0])
    vector = vector[: layers * count].reshape(layers, count, width)
    found = []
    start = 0
    for piece in small[0]:
        lines = lines_of(piece)
        part = vector[:, start : start + lines]
        if piece.shape[1] != width:
            part = part.reshape(layers, -1)[:, : piece.size]
        found.append(part.reshape((layers,) + piece.shape))
        start += lines
    chan_g, freq_g, sums_one, sums_two = found
    count = freq_in.shape[1]
    small = [
        jnp.stack([sums_one[:, 0], sums_two[:, 0]], axis=1),
        jnp.stack([sums_one[:, 1], sums_two[:, 1]], axis=1),
        chan_g[:, 0:3].reshape(layers, 3 * width),
        chan_g[:, 3:12].reshape(layers, 3, 3 * width),
        chan_g[:, 12:15],
        chan_g[:, 15],
        freq_g[:, :count],
        jnp.sum(freq_g[:, count:], axis=1),
        chan_g[:, 16:],
        sums_two[:, 2],
        sums_two[:, 3],
    ]

    for layer in range(layers):
        owned, mixer_own = big[layer]
        if special:
            piece = down_rows // PARTS
            up_own = jnp.concatenate(
                [part[at * piece : (at + 1) * piece] for at in range(2) for part in owned], axis=0
            ).astype(f32)
            down_own = jnp.concatenate([part[2 * piece :] for part in owned], axis=0).astype(f32)
        else:
            up_own, down_own = owned
        mixer_rows = mixer_own[0].astype(f32)
        big[layer] = (mixer_rows[:in_rows].T, mixer_rows[in_rows:], up_own.T, down_own)
    big = [jnp.stack([big[layer][index] for layer in range(layers)]) for index in range(4)]
    return (
        jnp.stack(outputs)[:, None],
        gradient[None],
        small[0],
        small[1],
        big[0],
        small[2],
        small[3],
        small[4],
        small[5],
        small[6],
        small[7],
        small[8],
        big[1],
        small[9],
        big[2],
        big[3],
        small[10],
    )


def solution(mesh):
    pairs = P(AXES, None, None)
    columns = P(None, None, AXES)
    rows = P(None, AXES, None)
    in_specs = (
        (pairs, P(AXES), pairs, P(), P(), columns)
        + (P(),) * 7
        + (rows, P(), columns, rows, P())
    )
    out_specs = (
        (P(None, AXES, None, None), pairs, P(), P(), columns)
        + (P(),) * 7
        + (rows, P(), columns, rows, P())
    )
    size = math.prod(mesh.shape.values())
    return jax.shard_map(
        functools.partial(body, size),
        mesh=mesh,
        in_specs=in_specs,
        out_specs=out_specs,
        check_vma=False,
    )
```

```python
import functools
import math

import jax
import jax.numpy as jnp
import numpy as np
from jax import lax
from jax.experimental import pallas as pl
from jax.experimental.pallas import tpu as pltpu
from jax.sharding import PartitionSpec as P

epsilon = 1e-05
f32 = jnp.float32
bf16 = jnp.bfloat16
AXES = ("wide", "narrow")
BLK = 256
BINS = 2 * BLK
CB = 256
PAD = 8
VMEM = 60 * 2**20
NN = (((1,), (0,)), ((), ()))
NT = (((1,), (1,)), ((), ()))
TN = (((0,), (0,)), ((), ()))
GELU_A = math.sqrt(2.0 / math.pi)
GELU_B = 0.044715


def dot(left, right, dims):
    return lax.dot_general(left, right, dims, preferred_element_type=f32)


def dot_fine(left, right, dims):
    return lax.dot_general(
        left, right, dims, precision=lax.Precision.HIGHEST, preferred_element_type=f32
    )


def split_low(table):
    high = table.astype(jnp.bfloat16)
    low = (table - high.astype(np.float32)).astype(jnp.bfloat16)
    return np.concatenate([high, high, low], axis=1)


def spectrum_tables():
    t = np.arange(BLK, dtype=np.float64)[None, :]
    k = np.arange(BLK, dtype=np.float64)[:, None]
    angle = 2.0 * np.pi * ((k * t) % BINS) / BINS
    forward = np.concatenate([np.cos(angle), -np.sin(angle)], axis=0)
    forward[BLK] = np.where(np.arange(BLK) % 2 == 0, 1.0, -1.0)
    weight = np.full((BINS, 1), 2.0 / BINS)
    weight[0] = 1.0 / BINS
    weight[BLK] = 1.0 / BINS
    inverse = (forward * weight).T
    return forward.astype(np.float32), inverse.astype(np.float32)


FORWARD, INVERSE = spectrum_tables()


def transform(table, values):
    return dot(table, values.astype(bf16), NN)


def transform_fine(table, values):
    high = values.astype(bf16)
    low = (values - high.astype(f32)).astype(bf16)
    return dot(table, jnp.concatenate([high, low, high], axis=0), NN)


def fold(values):
    rows, cols = values.shape
    return jnp.sum(values.reshape(rows // 8, 8, cols), axis=0)


def loop_rows(total, step, body, init):
    def run(index, carry):
        return body(pl.multiple_of(index * step, step), carry)

    return lax.fori_loop(0, total // step, run, init)


def row_mask(start, rows, cols):
    return start + lax.broadcasted_iota(jnp.int32, (rows, cols), 0)


def earlier(ref, lead, start, rows, cols, split):
    ext = ref[lead + (pl.ds(start, rows + PAD), slice(None))]
    t = row_mask(start, rows, cols)
    one = jnp.where(t != split, pltpu.roll(ext, 1, 0)[PAD:], 0.0)
    two = jnp.where((t != split) & (t != split + 1), pltpu.roll(ext, 2, 0)[PAD:], 0.0)
    return ext[PAD:], one, two


def later(ref, lead, start, rows, cols, split):
    ext = ref[lead + (pl.ds(start, rows + PAD), slice(None))]
    total = rows + PAD
    t = row_mask(start, rows, cols)
    one = jnp.where(t + 1 != split, pltpu.roll(ext, total - 1, 0)[:rows], 0.0)
    two = jnp.where(
        (t + 2 != split) & (t + 1 != split), pltpu.roll(ext, total - 2, 0)[:rows], 0.0
    )
    return ext[:rows], one, two


def norm_parts(values):
    average = jnp.mean(values, axis=-1, keepdims=True)
    centered = values - average
    variance = jnp.mean(centered * centered, axis=-1, keepdims=True)
    rstd = lax.rsqrt(variance + epsilon)
    return centered * rstd, rstd


def part_place(part, boundary):
    block = jnp.where(part <= boundary, part, part - 1)
    return pl.multiple_of(block * BLK, BLK)


def part_keep(part, boundary, split, start):
    t = row_mask(start, BLK, CB)
    front = jnp.where(part <= boundary, 1, 0)
    return jnp.where(t < split, 1, 0) == front


def load_part(ref, part, parts, boundary, split):
    start = part_place(part, boundary)
    return jnp.where(part_keep(part, boundary, split, start), ref[pl.ds(start, BLK), :], 0.0)


def store_part(ref, part, boundary, split, values):
    start = part_place(part, boundary)
    keep = part_keep(part, boundary, split, start)
    ref[pl.ds(start, BLK), :] = jnp.where(keep, values, ref[pl.ds(start, BLK), :])


def first_row(shape):
    return lax.broadcasted_iota(jnp.int32, shape, 0) == 0


def sum_terms(terms):
    total = terms[0]
    for term in terms[1:]:
        total = total + term
    return total


def mixer_forward_kernel(
    split_ref,
    state_ref,
    norm_ref,
    chan_ref,
    win_ref,
    khat_ref,
    fwd_ref,
    inv_ref,
    wout_ref,
    middle_ref,
    second_ref,
    normed_ref,
    biased_ref,
    conv_ref,
    scale_ref,
    val_ref,
    query_ref,
    prod_ref,
    spec_ref,
    res_ref,
):
    step = pl.program_id(0)
    length, width = state_ref.shape
    split = split_ref[0]
    boundary = split // BLK
    parts = length // BLK + 1

    @pl.when(step == 0)
    def _():
        def norm(row, carry):
            hat, _ = norm_parts(state_ref[pl.ds(row, 256), :].astype(f32))
            normed_ref[pl.ds(row, 256), :] = (hat * norm_ref[0:1, :] + norm_ref[1:2, :]).astype(bf16)
            return carry

        loop_rows(length, 256, norm, 0)
        val_ref[0:PAD, :] = jnp.zeros((PAD, CB), f32)

    biased_ref[:, 0:PAD, :] = jnp.zeros((3, PAD, CB), f32)
    for stream in range(3):
        biased = dot(normed_ref[...], win_ref[stream], NT) + chan_ref[stream : stream + 1, :]
        biased_ref[stream, PAD:, :] = biased

    rows = 64

    def shorten(row, carry):
        out = []
        for stream in range(3):
            now, one, two = earlier(biased_ref, (stream,), row, rows, CB, split)
            out.append(
                chan_ref[3 + stream : 4 + stream, :] * now
                + chan_ref[6 + stream : 7 + stream, :] * one
                + chan_ref[9 + stream : 10 + stream, :] * two
            )
        query_ref[pl.ds(row, rows), :] = out[0]
        val_ref[pl.ds(row + PAD, rows), :] = out[2]
        prod_ref[pl.ds(row, rows), :] = out[1] * out[2]
        return carry

    loop_rows(length, rows, shorten, 0)

    def condition(row, total):
        now, one, two = earlier(val_ref, (), row, rows, CB, split)
        cond = chan_ref[12:13, :] * now + chan_ref[13:14, :] * one + chan_ref[14:15, :] * two
        return total + fold(cond * cond)

    squares = loop_rows(length, rows, condition, jnp.zeros((8, CB), f32))
    scale = jnp.sqrt(jnp.sum(squares, axis=0, keepdims=True) * (1.0 / length) + epsilon)
    scale_ref[...] = jnp.broadcast_to(scale, (8, CB))

    for part in range(parts):
        spec_ref[part] = transform_fine(
            fwd_ref[...], load_part(prod_ref, part, parts, boundary, split)
        )

    def pairs_into(part, bound):
        low = 0 if part <= bound else bound + 1
        return [(part - source, source) for source in range(low, part + 1)]

    for bound in range(parts - 1):

        @pl.when(boundary == bound)
        def _():
            def multiply(row, carry):
                k_re = [khat_ref[m, pl.ds(row, 8), :] for m in range(parts - 1)]
                k_im = [khat_ref[m, pl.ds(row + BLK, 8), :] for m in range(parts - 1)]
                s_re = [spec_ref[v, pl.ds(row, 8), :] for v in range(parts)]
                s_im = [spec_ref[v, pl.ds(row + BLK, 8), :] for v in range(parts)]
                for part in range(parts):
                    pairs = pairs_into(part, bound)
                    res_ref[part, pl.ds(row, 8), :] = sum_terms(
                        [k_re[m] * s_re[v] - k_im[m] * s_im[v] for m, v in pairs]
                    )
                    res_ref[part, pl.ds(row + BLK, 8), :] = sum_terms(
                        [k_re[m] * s_im[v] + k_im[m] * s_re[v] for m, v in pairs]
                    )
                return carry

            loop_rows(BLK, 8, multiply, 0)
            top = first_row((8, CB))
            for part in range(parts):
                pairs = pairs_into(part, bound)
                for base in (0, BLK):
                    real = sum_terms(
                        [khat_ref[m, base : base + 8, :] * spec_ref[v, base : base + 8, :] for m, v in pairs]
                    )
                    res_ref[part, base : base + 8, :] = jnp.where(
                        top, real, res_ref[part, base : base + 8, :]
                    )

    for part in range(parts):
        store_part(conv_ref, part, boundary, split, transform_fine(inv_ref[...], res_ref[part]))

    mixed = (query_ref[...] * scale * conv_ref[...]).astype(bf16)
    update = dot(mixed, wout_ref[...], NN)

    @pl.when(step == 0)
    def _():
        middle_ref[...] = update

    @pl.when(step > 0)
    def _():
        middle_ref[...] += update

    @pl.when(step == pl.num_programs(0) - 1)
    def _():
        def finish(row, carry):
            here = pl.ds(row, 256)
            middle = state_ref[here, :].astype(f32) + middle_ref[here, :] + norm_ref[4:5, :]
            middle_ref[here, :] = middle
            hat, _ = norm_parts(middle)
            second_ref[here, :] = (hat * norm_ref[2:3, :] + norm_ref[3:4, :]).astype(bf16)
            return carry

        loop_rows(length, 256, finish, 0)


def whole_block(shape):
    return pl.BlockSpec(shape, lambda *index: (0,) * len(shape))


def fixed_block(shape):
    return pl.BlockSpec(shape, lambda *index: (0,) * len(shape), pipeline_mode=pl.Buffered(1))


def mixer_forward(after, split, state, norm_pack, chan_pack, w_in, khat, w_out):
    length, width = state.shape
    steps = width // CB
    parts = length // BLK + 1
    forward = jnp.asarray(split_low(FORWARD))
    inverse = jnp.asarray(split_low(INVERSE))
    return call_after(
        after,
        mixer_forward_kernel,
        grid=(steps,),
        in_specs=[
            pl.BlockSpec(memory_space=pltpu.SMEM),
            fixed_block((length, width)),
            fixed_block(norm_pack.shape),
            pl.BlockSpec((16, CB), lambda i: (0, i)),
            pl.BlockSpec((3, CB, width), lambda i: (0, i, 0)),
            pl.BlockSpec((parts - 1, BINS, CB), lambda i: (0, 0, i)),
            fixed_block(forward.shape),
            fixed_block(inverse.shape),
            pl.BlockSpec((CB, width), lambda i: (i, 0)),
        ],
        out_specs=[
            whole_block((length, width)),
            whole_block((length, width)),
            whole_block((length, width)),
            pl.BlockSpec((3, length + PAD, CB), lambda i: (0, 0, i)),
            pl.BlockSpec((length, CB), lambda i: (0, i)),
            pl.BlockSpec((8, CB), lambda i: (0, i)),
        ],
        out_shape=[
            jax.ShapeDtypeStruct((length, width), f32),
            jax.ShapeDtypeStruct((length, width), bf16),
            jax.ShapeDtypeStruct((length, width), bf16),
            jax.ShapeDtypeStruct((3, length + PAD, width), f32),
            jax.ShapeDtypeStruct((length, width), f32),
            jax.ShapeDtypeStruct((8, width), f32),
        ],
        scratch_shapes=[
            pltpu.VMEM((length + PAD, CB), f32),
            pltpu.VMEM((length, CB), f32),
            pltpu.VMEM((length, CB), f32),
            pltpu.VMEM((parts, BINS, CB), f32),
            pltpu.VMEM((parts, BINS, CB), f32),
        ],
        compiler_params=pltpu.CompilerParams(vmem_limit_bytes=VMEM),
        cost_estimate=cost(20e9, 40 * 2**20),
        name="mixer_forward",
    )(split, state, norm_pack, chan_pack, w_in.reshape(3, width, width), khat, forward, inverse, w_out)


PARTS = 2


def call_after(after, kernel, in_specs, **options):
    count = len(after)

    def run(*refs):
        kernel(*refs[count:])

    call = pl.pallas_call(
        run, in_specs=[pl.BlockSpec(memory_space=pl.ANY)] * count + in_specs, **options
    )
    return functools.partial(call, *after)


def cost(flops, moved):
    return pl.CostEstimate(flops=int(flops), bytes_accessed=int(moved), transcendentals=0)


def flat(block):
    return block.reshape(-1, block.shape[-1])


def load_weights(masks, taken, me_ref, refs, up_ref, down_ref, sems):
    size, piece = down_ref.shape[0] // len(taken), down_ref.shape[1]
    found = []
    count = 0
    for part, source in enumerate(taken):
        moves = []
        start = 3 * piece * source
        for array, own in zip(refs, masks):
            for slot, mask in enumerate(own):
                device = slot if mask is None else me_ref[0] ^ mask
                targets = [
                    up_ref.at[2 * (size * part + device)],
                    up_ref.at[2 * (size * part + device) + 1],
                    down_ref.at[size * part + device],
                ]
                for place, target in enumerate(targets):
                    rows = slice(start + place * piece, start + (place + 1) * piece)
                    moves.append(
                        pltpu.make_async_copy(array.at[slot, rows, :], target, sems.at[count])
                    )
                    count += 1
        found.append(moves)
    return found


def wait_weights(step, inner, found):
    for part, moves in enumerate(found):

        @pl.when(step == part * inner)
        def _():
            for move in moves:
                move.wait()


def weight_blocks(up_ref, down_ref, parts, inner, count, step):
    size = down_ref.shape[0] // parts
    part, block = step // inner, step % inner
    base = block * count
    return (
        flat(up_ref[pl.ds(2 * size * part + base, count)]),
        flat(up_ref[pl.ds(2 * size * part + size + base, count)]),
        flat(down_ref[pl.ds(size * part + base, count)]),
    )


def gated_forward_kernel(first, masks, taken, block, me_ref, second_ref, middle_ref, norm_ref, *refs):
    step = pl.program_id(0)
    length = second_ref.shape[0]
    rows = 256
    if masks:
        gate_ref, value_ref, out_ref, up_ref, down_ref, sems = refs[len(masks) :]

        @pl.when(step == 0)
        def _():
            for moves in load_weights(masks, taken, me_ref, refs[: len(masks)], up_ref, down_ref, sems):
                for move in moves:
                    move.start()

        wait_weights(
            step,
            pl.num_programs(0) // len(taken),
            load_weights(masks, taken, me_ref, refs[: len(masks)], up_ref, down_ref, sems),
        )

    else:
        up_ref, down_ref, gate_ref, value_ref, out_ref = refs
    count = block // down_ref.shape[1]
    parts = len(taken)
    gate_w, value_w, down_w = weight_blocks(
        up_ref, down_ref, parts, pl.num_programs(0) // parts, count, step
    )

    @pl.when(step == 0)
    def _():
        if first:
            out_ref[...] = middle_ref[...] + norm_ref[5:6, :]
        else:
            out_ref[...] = middle_ref[...]

    for row in range(0, length, rows):
        here = slice(row, row + rows)
        gate = dot(second_ref[here, :], gate_w, NT)
        value = dot(second_ref[here, :], value_w, NT)
        gate_ref[here, :] = gate.astype(bf16)
        value_ref[here, :] = value.astype(bf16)
        bent = jnp.tanh(GELU_A * gate * (1.0 + GELU_B * gate * gate))
        hidden = (0.5 * gate * (1.0 + bent) * value).astype(bf16)
        out_ref[here, :] += dot(hidden, down_w, NN)


def pieces_of(weight, group):
    grouped = weight.reshape(-1, PARTS, group // PARTS, weight.shape[-1])
    return [grouped[:, part] for part in range(PARTS)]


def weight_operands(weights, parts):
    anywhere = pl.BlockSpec(memory_space=pl.ANY)
    if isinstance(weights, dict):
        arrays = [piece for piece, _ in weights["pieces"]]
        masks = [own for _, own in weights["pieces"]]
        size = sum(len(own) for own in masks)
        width = arrays[0].shape[2]
        piece = weights["rows"]
        scratch = [
            pltpu.VMEM((2 * size * parts, piece, width), bf16),
            pltpu.VMEM((size * parts, piece, width), bf16),
            pltpu.SemaphoreType.DMA((3 * size * parts,)),
        ]
        return arrays, [anywhere] * len(arrays), masks, scratch, piece
    return list(weights), [fixed_block(part.shape) for part in weights], None, [], weights[1].shape[1]


def gated_forward(after, me, second, weights, before, norm_pack, hidden, first, taken=(0,), block=768):
    length, width = second.shape
    steps = hidden // block
    arrays, specs, masks, scratch, _ = weight_operands(weights, len(taken))
    return call_after(
        after,
        functools.partial(gated_forward_kernel, first, masks, taken, block),
        grid=(steps,),
        in_specs=[
            pl.BlockSpec(memory_space=pltpu.SMEM),
            fixed_block((length, width)),
            fixed_block((length, width)),
            fixed_block(norm_pack.shape),
        ]
        + specs,
        out_specs=[
            pl.BlockSpec((length, block), lambda i: (0, i)),
            pl.BlockSpec((length, block), lambda i: (0, i)),
            whole_block((length, width)),
        ],
        out_shape=[
            jax.ShapeDtypeStruct((length, hidden), bf16),
            jax.ShapeDtypeStruct((length, hidden), bf16),
            jax.ShapeDtypeStruct((length, width), f32),
        ],
        scratch_shapes=scratch,
        compiler_params=pltpu.CompilerParams(vmem_limit_bytes=VMEM),
        cost_estimate=cost(6 * length * width * hidden, 20 * 2**20),
        name="gated_forward",
    )(me, second, before, norm_pack, *arrays)


def norm_backward(values, grad_out, gain):
    hat, rstd = norm_parts(values)
    grad_hat = grad_out * gain
    mean_one = jnp.mean(grad_hat, axis=-1, keepdims=True)
    mean_two = jnp.mean(grad_hat * hat, axis=-1, keepdims=True)
    return rstd * (grad_hat - mean_one - hat * mean_two), grad_out * hat


def gated_backward_kernel(
    first,
    last,
    masks,
    own_order,
    taken,
    block,
    me_ref,
    glow_ref,
    grad_ref,
    before_ref,
    second_ref,
    middle_ref,
    norm_ref,
    gate_ref,
    value_ref,
    *refs,
):
    step = pl.program_id(0)
    steps = pl.num_programs(0)
    length, width = glow_ref.shape
    rows = 256
    slots = bool(masks)
    if slots:
        pieces, refs = refs[: len(masks)], refs[len(masks) :]
    else:
        up_ref, down_ref = refs[:2]
        refs = refs[2:]
    one_ref, two_ref, out_ref, mlow_ref, small_ref, hidden_ref, dgate_ref, dvalue_ref, stage_ref, sems = refs[:10]
    if slots:
        up_ref, down_ref, load_sems = refs[10:]
    piece = down_ref.shape[1]
    count = block // piece
    side = step % 2

    @pl.when(step == 0)
    def _():
        if slots:
            for moves in load_weights(masks, taken, me_ref, pieces, up_ref, down_ref, load_sems):
                for move in moves:
                    move.start()
        if first:
            out_ref[...] = jnp.zeros_like(out_ref)
        else:
            out_ref[...] = before_ref[...]

    parts = len(taken)
    inner = steps // parts
    if slots:
        wait_weights(step, inner, load_weights(masks, taken, me_ref, pieces, up_ref, down_ref, load_sems))
    gate_w, value_w, down_w = weight_blocks(up_ref, down_ref, parts, inner, count, step)

    def copies(at_step, kind):
        group = 2 if slots and kind < 2 else 1
        span = group * piece
        base = at_step % inner * count // group
        start = at_step // inner * 3 * piece
        found = []
        for item in range(count // group):
            source = stage_ref.at[at_step % 2, kind, item * span : (item + 1) * span, :]
            sem = sems.at[at_step % 2, kind, item]
            if not slots:
                place = base + item + (kind * inner * count if kind < 2 else 0)
                found.append((source, sem, [(None, (two_ref if kind == 2 else one_ref).at[place])]))
                continue
            device = base + item + (kind * inner * count // 2 if kind < 2 else 0)
            rows_at = pl.ds(start + (2 * piece if kind == 2 else 0), span)
            if not own_order:
                found.append((source, sem, [(None, one_ref.at[device, rows_at, :])]))
                continue
            mask = device ^ me_ref[0]
            place = mask >> 1
            core = mask & 1
            targets = [
                (core == 0, one_ref.at[place, rows_at, :]),
                (core == 1, two_ref.at[place, rows_at, :]),
            ]
            found.append((source, sem, targets))
        return found

    def send(kind):
        for source, sem, targets in copies(step, kind):
            for condition, target in targets:
                move = pltpu.make_async_copy(source, target, sem)
                if condition is None:
                    move.start()
                else:
                    pl.when(condition)(move.start)

    def drain(at_step):
        for kind in range(3):
            for source, sem, targets in copies(at_step, kind):
                pltpu.make_async_copy(source, targets[0][1], sem).wait()

    for row in range(0, length, rows):
        here = slice(row, row + rows)
        grad_hidden = dot(glow_ref[here, :], down_w, NT)
        gate = gate_ref[here, :].astype(f32)
        value = value_ref[here, :].astype(f32)
        square = gate * gate
        bent = jnp.tanh(GELU_A * gate * (1.0 + GELU_B * square))
        half = 0.5 * (1.0 + bent)
        unit = half * gate
        slope = half + 0.5 * gate * (1.0 - bent * bent) * (GELU_A * (1.0 + 3.0 * GELU_B * square))
        hidden_ref[here, :] = (unit * value).astype(bf16)
        dgate = (grad_hidden * value * slope).astype(bf16)
        dvalue = (grad_hidden * unit).astype(bf16)
        dgate_ref[here, :] = dgate
        dvalue_ref[here, :] = dvalue
        out_ref[here, :] += dot(dgate, gate_w, NN) + dot(dvalue, value_w, NN)

    @pl.when(step > 1)
    def _():
        drain(step - 2)

    stage_ref[side, 0] = dot(dgate_ref[...], second_ref[...], TN).astype(bf16)
    send(0)
    stage_ref[side, 1] = dot(dvalue_ref[...], second_ref[...], TN).astype(bf16)
    send(1)
    stage_ref[side, 2] = dot(hidden_ref[...], glow_ref[...], TN).astype(bf16)
    send(2)

    @pl.when(step == steps - 1)
    def _():
        if not last:
            small_ref[...] = jnp.zeros_like(small_ref)
            mlow_ref[...] = jnp.zeros_like(mlow_ref)
        else:

            def finish(row, carry):
                here = pl.ds(row, 128)
                grad_out = out_ref[here, :]
                grad = grad_ref[here, :].astype(f32)
                change, gain_rows = norm_backward(middle_ref[here, :], grad_out, norm_ref[2:3, :])
                total = grad + change
                out_ref[here, :] = total
                mlow_ref[here, :] = total.astype(bf16)
                return (
                    carry[0] + fold(gain_rows),
                    carry[1] + fold(grad_out),
                    carry[2] + fold(total),
                    carry[3] + fold(grad),
                )

            zero = jnp.zeros((8, width), f32)
            sums = loop_rows(length, 128, finish, (zero, zero, zero, zero))
            small_ref[...] = jnp.concatenate(
                [jnp.sum(part, axis=0, keepdims=True) for part in sums]
                + [jnp.zeros((4, width), f32)],
                axis=0,
            )

        @pl.when(steps > 1)
        def _():
            drain(step - 1)

        drain(step)


def gated_backward(after,
    me, glow, grad, before, second, middle, norm_pack, gate, value, weights, first, last, own_order, taken=(0,), block=768
):
    length, width = second.shape
    parts = len(taken)
    inner = gate.shape[1] // block
    start = 0
    if isinstance(weights, dict):
        start = taken[0] * inner // PARTS
        inner = parts * inner // PARTS
    hidden = inner * block
    arrays, specs, masks, scratch, piece = weight_operands(weights, parts)
    count = block // piece
    column = pl.BlockSpec((length, block), lambda i: (0, i + start))
    anywhere = pl.BlockSpec(memory_space=pl.ANY)
    if masks:
        size = sum(len(own) for own in masks)
        places = [jax.ShapeDtypeStruct((size // 2, 3 * piece * parts, width), bf16)] * 2
        if not own_order:
            places = [
                jax.ShapeDtypeStruct((size, 3 * piece * parts, width), bf16),
                jax.ShapeDtypeStruct((16, width), bf16),
            ]
    else:
        places = [jax.ShapeDtypeStruct(array.shape, bf16) for array in arrays]
    return call_after(
        after,
        functools.partial(
            gated_backward_kernel, first, last, masks, own_order, taken, block
        ),
        grid=(inner,),
        in_specs=[
            pl.BlockSpec(memory_space=pltpu.SMEM),
            fixed_block((length, width)),
            fixed_block(grad.shape),
            fixed_block(before.shape),
            fixed_block((length, width)),
            fixed_block(middle.shape),
            fixed_block(norm_pack.shape),
            column,
            column,
        ]
        + specs,
        out_specs=[
            anywhere,
            anywhere,
            whole_block((length, width)),
            whole_block((length if last else 16, width)),
            whole_block((8, width)),
        ],
        out_shape=places
        + [
            jax.ShapeDtypeStruct((length, width), f32),
            jax.ShapeDtypeStruct((length if last else 16, width), bf16),
            jax.ShapeDtypeStruct((8, width), f32),
        ],
        scratch_shapes=[
            pltpu.VMEM((length, block), bf16),
            pltpu.VMEM((length, block), bf16),
            pltpu.VMEM((length, block), bf16),
            pltpu.VMEM((2, 3, block, width), bf16),
            pltpu.SemaphoreType.DMA((2, 3, count)),
        ]
        + scratch,
        compiler_params=pltpu.CompilerParams(vmem_limit_bytes=VMEM),
        cost_estimate=cost(12 * length * width * hidden, 20 * 2**20),
        name="gated_backward",
    )(me, glow, grad, before, second, middle, norm_pack, gate, value, *arrays)


def mixer_backward_kernel(
    first,
    last,
    split_ref,
    mlow_ref,
    normed_ref,
    chan_ref,
    biased_ref,
    conv_ref,
    scale_ref,
    khat_ref,
    fwd_ref,
    inv_ref,
    wout_ref,
    kernel_ref,
    inner_t_ref,
    slope_ref,
    features_t_ref,
    freq_out_ref,
    inner_before_ref,
    win_g_ref,
    wout_g_ref,
    chan_g_ref,
    inner_g_ref,
    freq_g_ref,
    low_ref,
    kern_g_ref,
    key_ref,
    val_ref,
    prod_ref,
    dconv_ref,
    mixed_ref,
    cond_ref,
    dpad_ref,
    spec_ref,
    dspec_ref,
    res_ref,
    gram_ref,
):
    step = pl.program_id(0)
    length, width = mlow_ref.shape
    split = split_ref[0]
    boundary = split // BLK
    parts = length // BLK + 1
    rows = 64

    @pl.when(step == 0)
    def _():
        val_ref[0:PAD, :] = jnp.zeros((PAD, CB), f32)
        cond_ref[length:, :] = jnp.zeros((PAD, CB), f32)
        dpad_ref[:, length:, :] = jnp.zeros((3, PAD, CB), f32)

    dconv_ref[...] = dot(mlow_ref[...], wout_ref[...], NT)
    scale = scale_ref[0:1, :]

    def gate(row, total):
        here = pl.ds(row, rows)
        out = []
        for stream in range(3):
            now, one, two = earlier(biased_ref, (stream,), row, rows, CB, split)
            out.append(
                chan_ref[3 + stream : 4 + stream, :] * now
                + chan_ref[6 + stream : 7 + stream, :] * one
                + chan_ref[9 + stream : 10 + stream, :] * two
            )
        query, key, value = out
        key_ref[here, :] = key
        val_ref[pl.ds(row + PAD, rows), :] = value
        prod_ref[here, :] = key * value
        grad = dconv_ref[here, :]
        conv = conv_ref[here, :]
        mixed_ref[here, :] = (query * scale * conv).astype(bf16)
        dpad_ref[0, here, :] = grad * scale * conv
        through = grad * query
        dconv_ref[here, :] = through * scale
        return total + fold(through * conv)

    scale_sum = loop_rows(length, rows, gate, jnp.zeros((8, CB), f32))
    grad_scale = jnp.sum(scale_sum, axis=0, keepdims=True)
    factor = grad_scale / (scale * float(length))

    def condition(row, carry):
        now, one, two = earlier(val_ref, (), row, rows, CB, split)
        cond_ref[pl.ds(row, rows), :] = (
            chan_ref[12:13, :] * now + chan_ref[13:14, :] * one + chan_ref[14:15, :] * two
        )
        return carry

    loop_rows(length, rows, condition, 0)

    for part in range(parts):
        spec_ref[part] = transform(fwd_ref[...], load_part(prod_ref, part, parts, boundary, split))
        dspec_ref[part] = transform(fwd_ref[...], load_part(dconv_ref, part, parts, boundary, split))

    def pairs_from(source, bound):
        high = bound if source <= bound else parts - 1
        return [(part - source, part) for part in range(source, high + 1)]

    def pairs_apart(lag, bound):
        found = []
        for source in range(parts - lag):
            if (source <= bound) == (source + lag <= bound):
                found.append((source, source + lag))
        return found

    odd_sign = jnp.where(lax.broadcasted_iota(jnp.int32, (8, CB), 0) % 2 == 0, 1.0, -1.0)

    def chain(grams):
        return [
            grams[lag] + odd_sign * grams[lag + 1] if lag + 1 < parts - 1 else grams[lag]
            for lag in range(parts - 1)
        ]

    def or_zero(terms):
        return sum_terms(terms) if terms else jnp.zeros((8, CB), f32)

    for bound in range(parts - 1):

        @pl.when(boundary == bound)
        def _():
            def multiply(row, carry):
                k_re = [khat_ref[m, pl.ds(row, 8), :] for m in range(parts - 1)]
                k_im = [khat_ref[m, pl.ds(row + BLK, 8), :] for m in range(parts - 1)]
                e_re = [dspec_ref[v, pl.ds(row, 8), :] for v in range(parts)]
                e_im = [dspec_ref[v, pl.ds(row + BLK, 8), :] for v in range(parts)]
                for source in range(parts):
                    pairs = pairs_from(source, bound)
                    res_ref[source, pl.ds(row, 8), :] = sum_terms(
                        [k_re[m] * e_re[v] + k_im[m] * e_im[v] for m, v in pairs]
                    )
                    res_ref[source, pl.ds(row + BLK, 8), :] = sum_terms(
                        [k_re[m] * e_im[v] - k_im[m] * e_re[v] for m, v in pairs]
                    )
                s_re = [spec_ref[v, pl.ds(row, 8), :] for v in range(parts)]
                s_im = [spec_ref[v, pl.ds(row + BLK, 8), :] for v in range(parts)]
                real, imag = [], []
                for lag in range(parts - 1):
                    pairs = pairs_apart(lag, bound)
                    real.append(
                        or_zero([s_re[j] * e_re[i] + s_im[j] * e_im[i] for j, i in pairs])
                    )
                    imag.append(
                        or_zero([s_re[j] * e_im[i] - s_im[j] * e_re[i] for j, i in pairs])
                    )
                for lag, (one, two) in enumerate(zip(chain(real), chain(imag))):
                    gram_ref[lag, pl.ds(row, 8), :] = one
                    gram_ref[lag, pl.ds(row + BLK, 8), :] = two
                return carry

            loop_rows(BLK, 8, multiply, 0)
            top = first_row((8, CB))
            for base in (0, BLK):
                tile = slice(base, base + 8)
                for source in range(parts):
                    real = sum_terms(
                        [khat_ref[m, tile, :] * dspec_ref[v, tile, :] for m, v in pairs_from(source, bound)]
                    )
                    res_ref[source, tile, :] = jnp.where(top, real, res_ref[source, tile, :])
                grams = [
                    or_zero([spec_ref[j, tile, :] * dspec_ref[i, tile, :] for j, i in pairs_apart(lag, bound)])
                    for lag in range(parts - 1)
                ]
                for lag, real in enumerate(chain(grams)):
                    gram_ref[lag, tile, :] = jnp.where(top, real, gram_ref[lag, tile, :])

    for part in range(parts):
        store_part(prod_ref, part, boundary, split, transform(inv_ref[...], res_ref[part]))
    for lag in range(parts - 1):
        kern_g_ref[lag * BLK : (lag + 1) * BLK, :] = transform(inv_ref[...], gram_ref[lag])

    def spread(row, carry):
        here = pl.ds(row, rows)
        change = prod_ref[here, :]
        value = val_ref[pl.ds(row + PAD, rows), :]
        dpad_ref[1, here, :] = change * value
        now, one, two = later(cond_ref, (), row, rows, CB, split)
        from_cond = chan_ref[12:13, :] * now + chan_ref[13:14, :] * one + chan_ref[14:15, :] * two
        dpad_ref[2, here, :] = change * key_ref[here, :] + factor * from_cond
        return (
            carry[0] + fold(value * now),
            carry[1] + fold(value * one),
            carry[2] + fold(value * two),
        )

    zero = jnp.zeros((8, CB), f32)
    cond_sums = loop_rows(length, rows, spread, (zero, zero, zero))
    sums = [None] * 12
    for stream in range(3):

        def back(row, carry, stream=stream):
            now, one, two = later(dpad_ref, (stream,), row, rows, CB, split)
            biased = biased_ref[stream, pl.ds(row + PAD, rows), :]
            change = (
                chan_ref[3 + stream : 4 + stream, :] * now
                + chan_ref[6 + stream : 7 + stream, :] * one
                + chan_ref[9 + stream : 10 + stream, :] * two
            )
            low_ref[stream, pl.ds(row, rows), :] = change.astype(bf16)
            return (
                carry[0] + fold(change),
                carry[1] + fold(biased * now),
                carry[2] + fold(biased * one),
                carry[3] + fold(biased * two),
            )

        got = loop_rows(length, rows, back, (zero, zero, zero, zero))
        for index in range(4):
            sums[3 * index + stream] = got[index]
    decay = chan_ref[15:16, :]
    level = jnp.sqrt(2.0 * decay)
    lead = 0.5 / decay

    def profile(row, total):
        here = pl.ds(row, rows)
        position = row_mask(row, rows, CB).astype(f32)
        change = kern_g_ref[here, :]
        kern_g_ref[here, :] = change * (jnp.exp(-position * decay) * level)
        return total + fold(change * kernel_ref[here, :] * (lead - position))

    decay_sum = loop_rows(length, rows, profile, zero)
    chan_g_ref[0:16, :] = jnp.concatenate(
        [jnp.sum(part, axis=0, keepdims=True) for part in sums]
        + [factor * jnp.sum(part, axis=0, keepdims=True) for part in cond_sums]
        + [jnp.sum(decay_sum, axis=0, keepdims=True)],
        axis=0,
    )
    chan_g_ref[16:, :] = dot_fine(inner_t_ref[...], kern_g_ref[...], NN)
    inner_g = dot_fine(kern_g_ref[...], freq_out_ref[...], NT)

    @pl.when(step == 0)
    def _():
        if first:
            inner_g_ref[...] = inner_g
        else:
            inner_g_ref[...] = inner_before_ref[...] + inner_g

    @pl.when(step > 0)
    def _():
        inner_g_ref[...] += inner_g

    wout_g_ref[...] = dot(mixed_ref[...], mlow_ref[...], TN).astype(bf16)
    for stream in range(3):
        win_g_ref[stream] = dot(low_ref[stream], normed_ref[...], TN).astype(bf16)
    if not last:
        freq_g_ref[...] = jnp.zeros_like(freq_g_ref)
        return

    @pl.when(step == pl.num_programs(0) - 1)
    def _():
        phase_g = inner_g_ref[...] * slope_ref[...]
        freq_g_ref[0 : phase_g.shape[1], :] = dot_fine(features_t_ref[...], phase_g, NN)
        freq_g_ref[phase_g.shape[1] :, :] = fold(phase_g)
def mixer_backward(after, start, steps, split, mlow, normed, chan_pack, biased, conv, scale, khat, w_out, filtered, freq_out, inner_before):
    length, width = mlow.shape
    last = (start + steps) * CB == width
    parts = length // BLK + 1
    forward = jnp.asarray(FORWARD, bf16)
    inverse = jnp.asarray(INVERSE, bf16)
    kernel, inner_t, slope, features_t = filtered
    hidden = freq_out.shape[0]
    full = fixed_block((length, width))
    tall = pltpu.VMEM((length, CB), f32)
    tall_pad = pltpu.VMEM((length + PAD, CB), f32)
    spectrum = pltpu.VMEM((parts, BINS, CB), f32)
    return call_after(
        after,
        functools.partial(mixer_backward_kernel, start == 0, last),
        grid=(steps,),
        in_specs=[
            pl.BlockSpec(memory_space=pltpu.SMEM),
            full,
            full,
            pl.BlockSpec((16, CB), lambda i: (0, i + start)),
            pl.BlockSpec((3, length + PAD, CB), lambda i: (0, 0, i + start)),
            pl.BlockSpec((length, CB), lambda i: (0, i + start)),
            pl.BlockSpec((8, CB), lambda i: (0, i + start)),
            pl.BlockSpec((parts - 1, BINS, CB), lambda i: (0, 0, i + start)),
            fixed_block(forward.shape),
            fixed_block(inverse.shape),
            pl.BlockSpec((CB, width), lambda i: (i + start, 0)),
            pl.BlockSpec((length, CB), lambda i: (0, i + start)),
            fixed_block(inner_t.shape),
            fixed_block(slope.shape),
            fixed_block(features_t.shape),
            pl.BlockSpec((freq_out.shape[0], CB), lambda i: (0, i + start)),
            fixed_block(inner_before.shape),
        ],
        out_specs=[
            pl.BlockSpec((3, CB, width), lambda i: (0, i, 0)),
            pl.BlockSpec((CB, width), lambda i: (i, 0)),
            pl.BlockSpec((16 + hidden, CB), lambda i: (0, i)),
            whole_block((length, hidden)),
            whole_block((hidden + 8, hidden)),
            pl.BlockSpec((3, length, CB), lambda i: (0, 0, i)),
        ],
        out_shape=[
            jax.ShapeDtypeStruct((3, steps * CB, width), bf16),
            jax.ShapeDtypeStruct((steps * CB, width), bf16),
            jax.ShapeDtypeStruct((16 + hidden, steps * CB), f32),
            jax.ShapeDtypeStruct((length, hidden), f32),
            jax.ShapeDtypeStruct((hidden + 8, hidden), f32),
            jax.ShapeDtypeStruct((3, length, steps * CB), bf16),
        ],
        scratch_shapes=[
            tall,
            tall,
            tall_pad,
            tall,
            tall,
            pltpu.VMEM((length, CB), bf16),
            tall_pad,
            pltpu.VMEM((3, length + PAD, CB), f32),
            spectrum,
            spectrum,
            spectrum,
            pltpu.VMEM((parts - 1, BINS, CB), f32),
        ],
        compiler_params=pltpu.CompilerParams(vmem_limit_bytes=VMEM),
        cost_estimate=cost(12e9 * steps, 14 * 2**20 * steps),
        name="mixer_backward",
    )(
        split,
        mlow,
        normed,
        chan_pack,
        biased,
        conv,
        scale,
        khat,
        forward,
        inverse,
        w_out,
        kernel,
        inner_t,
        slope,
        features_t,
        freq_out,
        inner_before,
    )


def norm_finish_kernel(state_ref, grad_ref, norm_ref, win_ref, *refs):
    *low_refs, out_ref, low_out_ref, small_ref = refs
    rows, width = state_ref.shape
    update = None
    start = 0
    for low_ref in low_refs:
        count = low_ref.shape[2]
        for stream in range(3):
            term = dot(low_ref[stream], win_ref[stream, start : start + count, :], NN)
            update = term if update is None else update + term
        start += count
    change, gain_rows = norm_backward(state_ref[...].astype(f32), update, norm_ref[0:1, :])
    total = grad_ref[...] + change
    out_ref[...] = total
    low_out_ref[...] = total.astype(bf16)

    @pl.when(pl.program_id(0) == 0)
    def _():
        small_ref[...] = jnp.zeros_like(small_ref)

    sums = [jnp.sum(part, axis=0, keepdims=True) for part in (gain_rows, update)]
    small_ref[...] += jnp.concatenate(sums + [jnp.zeros((6, width), f32)], axis=0)


def norm_finish(after, lows, w_in, state, grad, norm_pack, block=256):
    length, width = state.shape
    tile = pl.BlockSpec((block, width), lambda i: (i, 0))
    return call_after(
        after,
        norm_finish_kernel,
        grid=(length // block,),
        in_specs=[tile, tile, whole_block(norm_pack.shape), fixed_block((3, width, width))]
        + [pl.BlockSpec((3, block, low.shape[2]), lambda i: (0, i, 0)) for low in lows],
        out_specs=[tile, tile, whole_block((8, width))],
        out_shape=[
            jax.ShapeDtypeStruct((length, width), f32),
            jax.ShapeDtypeStruct((length, width), bf16),
            jax.ShapeDtypeStruct((8, width), f32),
        ],
        compiler_params=pltpu.CompilerParams(vmem_limit_bytes=VMEM),
        cost_estimate=cost(6 * length * width * width, 20 * 2**20),
        name="norm_finish",
    )(state, grad, norm_pack, w_in.reshape(3, width, width), *lows)


def filter_features(length, count):
    half = count // 2
    positions = np.arange(length, dtype=np.float64)[:, None]
    harmonics = np.arange(1, half + 1, dtype=np.float64)[None, :]
    angles = 2.0 * np.pi * ((positions * harmonics) % length) / length
    return np.concatenate([np.sin(angles), np.cos(angles)], axis=1).astype(np.float32)


def highest(left, right, dims):
    return lax.dot_general(left, right, dims, precision=lax.Precision.HIGHEST)


def filter_kernel_body(inner_ref, out_ref, chan_ref, fwd_ref, kernel_ref, khat_ref):
    length = inner_ref.shape[0]
    decay = chan_ref[15:16, :]
    level = jnp.sqrt(2.0 * decay)
    sign = jnp.where(lax.broadcasted_iota(jnp.int32, (BINS, CB), 0) % 2 == 0, 1.0, -1.0)
    before = None
    for block in range(length // BLK):
        here = slice(block * BLK, (block + 1) * BLK)
        profile = dot_fine(inner_ref[here, :], out_ref[...], NN)
        position = row_mask(block * BLK, BLK, CB).astype(f32)
        kernel = profile * (jnp.exp(-position * decay) * level)
        kernel_ref[here, :] = kernel
        spectrum = transform_fine(fwd_ref[...], kernel)
        khat_ref[block] = spectrum if before is None else spectrum + sign * before
        before = spectrum


def filter_forward(length, chan_pack, freq_in, freq_bias, freq_out):
    table = filter_features(length, freq_in.shape[0])
    features = jnp.asarray(table)
    phase = highest(features, freq_in, NN) + freq_bias
    inner = jnp.sin(phase)
    width = freq_out.shape[1]
    hidden = inner.shape[1]
    forward = jnp.asarray(split_low(FORWARD))
    blocks = length // BLK
    kernel, khat = pl.pallas_call(
        filter_kernel_body,
        grid=(width // CB,),
        in_specs=[
            fixed_block((length, hidden)),
            pl.BlockSpec((hidden, CB), lambda i: (0, i)),
            pl.BlockSpec((16, CB), lambda i: (0, i)),
            fixed_block(forward.shape),
        ],
        out_specs=[
            pl.BlockSpec((length, CB), lambda i: (0, i)),
            pl.BlockSpec((blocks, BINS, CB), lambda i: (0, 0, i)),
        ],
        out_shape=[
            jax.ShapeDtypeStruct((length, width), f32),
            jax.ShapeDtypeStruct((blocks, BINS, width), f32),
        ],
        compiler_params=pltpu.CompilerParams(vmem_limit_bytes=VMEM),
        cost_estimate=cost(6e9, 10 * 2**20),
        name="filter_forward",
    )(inner, freq_out, chan_pack, forward)
    return khat, (kernel, inner.T, jnp.cos(phase), jnp.asarray(table.T.copy()))


def cube_orders(size):
    bits = [1 << place for place in range(1, size.bit_length() - 1)]
    if len(bits) < 2:
        return [bits + [1], bits + [1]]
    return [bits + [1], bits[:-2] + [bits[-1], bits[-2]] + [1]]


def slot_table(order, size):
    table = np.zeros(size, np.int32)
    for slot in range(size):
        mask = sum(bit for place, bit in enumerate(order) if slot >> place & 1)
        table[mask] = slot
    return table


def swap(values, bit, size):
    return lax.ppermute(values, AXES, [(index, index ^ bit) for index in range(size)])


def cube_gather(block, order, size, me):
    held = block[None]
    for bit in order:
        held = jnp.concatenate([held, swap(held, bit, size)], axis=0)
    places = jnp.asarray(slot_table(order, size))[jnp.arange(size, dtype=jnp.int32) ^ me]
    return jnp.take(held, places, axis=0)


def cube_scatter(blocks, order, size, me):
    masks = np.zeros(size, np.int32)
    masks[slot_table(order, size)] = np.arange(size)
    held = jnp.take(blocks, jnp.asarray(masks) ^ me, axis=0)
    for place in reversed(range(len(order))):
        half = 1 << place
        got = swap(held[half:], order[place], size)
        held = held[:half].astype(f32) + got.astype(f32)
        if place:
            held = held.astype(bf16)
    return held[0]


def cube_sum(values, size):
    for place in range(size.bit_length() - 1):
        values = values + swap(values, 1 << place, size)
    return values


def halves(rows):
    if rows < 32:
        return rows // 2
    return (rows // 2 + 15) // 16 * 16


def gather_rows(block, size, me):
    cut = halves(block.shape[0])
    orders = cube_orders(size)
    one = cube_gather(block[:cut], orders[0], size, me)
    two = cube_gather(block[cut:], orders[1], size, me)
    return jnp.concatenate([one, two], axis=1)


def scatter_rows(blocks, size, me):
    cut = halves(blocks.shape[1])
    orders = cube_orders(size)
    one = cube_scatter(blocks[:, :cut], orders[0], size, me)
    two = cube_scatter(blocks[:, cut:], orders[1], size, me)
    return jnp.concatenate([one, two], axis=0)


def hold(value, *others):
    for other in others:
        value = value + (other[(0,) * other.ndim] * 0).astype(value.dtype)
    return value


def hold_place(value, *others):
    if not others:
        return value
    anywhere = pl.BlockSpec(memory_space=pl.ANY)

    def nothing(*refs):
        pass

    return pl.pallas_call(
        nothing,
        in_specs=[anywhere] * (1 + len(others)),
        out_specs=anywhere,
        out_shape=jax.ShapeDtypeStruct(value.shape, value.dtype),
        input_output_aliases={0: 0},
        cost_estimate=cost(0, 0),
        name="hold_place",
    )(value, *others)


def gather_steps(block, after, clock, done):
    size = 32
    block = hold(block, *after)
    came = [swap(block, bit, size) for bit in (2, 4, 6)]
    yield [block]
    line = hold(jnp.stack([block] + came), *clock)
    others = [swap(line, bit, size) for bit in (8, 16, 24)]
    own = swap(line, 1, size)
    yield [line]
    others = [hold_place(other, *clock) for other in others]
    pieces = []
    for bit, piece in zip((0, 8, 16, 24), [line] + others):
        masks = tuple(bit + place for place in (0, 2, 4, 6))
        pieces.append((piece, masks))
        other = swap(piece, 1, size) if bit else own
        pieces.append((other, tuple(mask + 1 for mask in masks)))
    yield others
    done(pieces)


def place_kernel(masks, cuts, me_ref, *refs):
    pieces = refs[: len(masks)]
    targets = refs[len(masks) : len(masks) + len(cuts)]
    held, in_sems, out_sems = refs[-3:]
    loads = []
    slot = 0
    for index, (piece, own) in enumerate(zip(pieces, masks)):
        load = pltpu.make_async_copy(piece, held.at[slot : slot + len(own)], in_sems.at[index])
        load.start()
        loads.append((load, slot, own))
        slot += len(own)
    moves = []
    for load, slot, own in loads:
        load.wait()
        for place, mask in enumerate(own):
            device = me_ref[0] ^ mask
            start = 0
            for target, rows in zip(targets, cuts):
                move = pltpu.make_async_copy(
                    held.at[slot + place, start : start + rows, :],
                    target.at[device],
                    out_sems.at[len(moves)],
                )
                move.start()
                moves.append(move)
                start += rows
    for move in moves:
        move.wait()


def place_pieces(pieces, cuts, me):
    arrays = [piece for piece, _ in pieces]
    masks = [own for _, own in pieces]
    size = sum(len(own) for own in masks)
    width = arrays[0].shape[-1]
    anywhere = pl.BlockSpec(memory_space=pl.ANY)
    return pl.pallas_call(
        functools.partial(place_kernel, masks, cuts),
        in_specs=[pl.BlockSpec(memory_space=pltpu.SMEM)] + [anywhere] * len(arrays),
        out_specs=[anywhere] * len(cuts),
        out_shape=[jax.ShapeDtypeStruct((size, rows, width), bf16) for rows in cuts],
        scratch_shapes=[
            pltpu.VMEM((size, sum(cuts), width), bf16),
            pltpu.SemaphoreType.DMA((len(masks),)),
            pltpu.SemaphoreType.DMA((size * len(cuts),)),
        ],
        compiler_params=pltpu.CompilerParams(vmem_limit_bytes=VMEM),
        cost_estimate=cost(0, 2 * sum(cuts) * size * width * 2),
        name="place_pieces",
    )(me, *arrays)


def scatter_steps(keep, send, clock, done):
    size = 32
    shape = (4, 4) + keep.shape[1:]
    keep = keep.reshape(shape)
    got = swap(send, 1, size).reshape(shape)
    yield [send]

    def both(group):
        return keep[group].astype(f32) + got[group].astype(f32)

    out = [hold(both(group), *clock).astype(bf16) for group in (3, 1, 2)]
    came = [swap(piece, bit, size) for piece, bit in zip(out, (24, 8, 16))]
    yield out
    line = hold(sum_terms([both(0)] + [piece.astype(f32) for piece in came]), *clock)
    low = [line[place].astype(bf16) for place in (1, 2, 3)]
    came = [swap(piece, 2 * place + 2, size) for place, piece in enumerate(low)]
    yield low
    done(hold(sum_terms([line[0]] + [piece.astype(f32) for piece in came]), *clock))


def sum_steps(values, size, me, done, after=()):
    halved = values.reshape((2, -1) + values.shape[1:])
    core = me % 2
    send = jnp.take(halved, 1 - core, axis=0, mode="clip")
    part = jnp.take(halved, core, axis=0, mode="clip") + swap(send, 1, size)
    yield [send]
    part = hold(part, *after)
    for place in reversed(range(1, size.bit_length() - 1)):
        came = swap(part, 1 << place, size)
        yield [part]
        part = part + came
    other = swap(part, 1, size)
    yield [part]
    done(jnp.concatenate([jnp.where(core == 0, part, other), jnp.where(core == 0, other, part)], axis=0))


def body(
    size,
    tokens,
    split_point,
    cotangent,
    norm_gain,
    norm_shift,
    in_weight,
    in_bias,
    short_taps,
    cond_taps,
    decay_rate,
    freq_in,
    freq_bias,
    freq_out,
    out_weight,
    out_bias,
    up_weight,
    down_weight,
    down_bias,
):
    layers = in_weight.shape[0]
    length, width = tokens.shape[1:]
    me = lax.axis_index(AXES)
    split = split_point.astype(jnp.int32)
    state = tokens[0]
    in_rows = in_weight.shape[2]
    out_rows = out_weight.shape[1]

    packs = []
    for layer in range(layers):
        norm_pack = jnp.concatenate(
            [
                jnp.stack([norm_gain[layer, 0], norm_shift[layer, 0]]),
                jnp.stack([norm_gain[layer, 1], norm_shift[layer, 1]]),
                out_bias[layer][None],
                down_bias[layer][None],
                jnp.zeros((2, width), f32),
            ]
        )
        chan_pack = jnp.concatenate(
            [
                in_bias[layer].reshape(3, width),
                short_taps[layer].reshape(9, width),
                cond_taps[layer],
                decay_rate[layer][None],
            ]
        )
        packs.append((norm_pack, chan_pack))

    mine = me.astype(jnp.int32)[None]
    up_rows = up_weight.shape[2]
    down_rows = down_weight.shape[1]
    special = size == 32
    clock = []
    mixer_w = [None] * layers
    gated_w = [[None] * PARTS for _ in range(layers)]
    hidden = size * down_rows // PARTS

    def mixer_block(layer):
        return jnp.concatenate([in_weight[layer].T, out_weight[layer]], axis=0)

    def mixer_weights(layer, rows):
        mixer_w[layer] = (
            rows[:, :in_rows].reshape(3 * width, width),
            rows[:, in_rows:].reshape(width, width),
        )

    def gather_mixer(layer, after):
        def done(pieces):
            (rows,) = place_pieces(pieces, (in_rows + out_rows,), mine)
            mixer_weights(layer, rows)

        return gather_steps(mixer_block(layer), after, clock, done)

    def gated_weights(layer, pieces):
        gated_w[layer] = {"pieces": pieces, "rows": down_rows // PARTS}

    def gather_gated(layer, after):
        return gather_steps(all_parts(layer), after, clock, functools.partial(gated_weights, layer))

    def whole_gather(block, *after):
        return lax.all_gather(hold(block, *after), AXES, axis=0)

    def all_parts(layer):
        halved = up_weight[layer].T.reshape(2, PARTS, -1, width)
        own = down_weight[layer].reshape(PARTS, -1, width)
        rows = []
        for part in range(PARTS):
            rows += [halved[0, part], halved[1, part], own[part]]
        return jnp.concatenate(rows, axis=0)

    def go(*names):
        sent = []
        for name in names:
            sent.extend(next(steps[name], ()))
        return sent

    filters = [None] * layers

    def make_filter(layer, *after):
        filters[layer] = filter_forward(
            length,
            packs[layer][1],
            hold(freq_in[layer], *after),
            freq_bias[layer],
            freq_out[layer],
        )

    for layer in range(layers):
        make_filter(layer)
    steps = {}
    if special:
        rows = whole_gather(jnp.concatenate([all_parts(0), mixer_block(0)], axis=0))
        gated_weights(0, [(rows, (None,) * size)])
        mixer_weights(0, rows[:, -in_rows - out_rows :])
    else:
        for layer in range(layers):
            mixer_weights(layer, gather_rows(mixer_block(layer), size, me))
            gated_block = jnp.concatenate([up_weight[layer].T, down_weight[layer]], axis=0)
            gated_rows = gather_rows(gated_block, size, me)
            ups = pieces_of(gated_rows[:, :up_rows].reshape(-1, width), 96)
            downs = pieces_of(gated_rows[:, up_rows:].reshape(-1, width), 96)
            gated_w[layer] = list(zip(ups, downs))

    saved = []
    outputs = []
    for layer in range(layers):
        norm_pack, chan_pack = packs[layer]
        waits = []
        ahead = (layer + 1, "mixer"), (layer + 1, "gated")
        more = special and layer + 1 < layers
        ahead = (layer + 1, "mixer"), (layer + 1, "gated")
        if more:
            steps[ahead[0]] = gather_mixer(layer + 1, [filters[layer][0]])
            go(ahead[0])
            steps[ahead[1]] = gather_gated(layer + 1, [mixer_w[layer][1]])
            go(ahead[1])
            clock[:] = [mixer_w[layer][1]]
            waits = go(ahead[0])
        w_in, w_out = mixer_w[layer]
        middle, second, normed, biased, conv, scale = mixer_forward(
            waits, split, state, norm_pack, chan_pack, w_in, filters[layer][0], w_out
        )
        waits = ()
        clock[:] = [middle]
        waits = []
        if more:
            go(ahead[0])
            go(ahead[0])
            waits = go(ahead[1])
        elif special:
            go((layer, "gated"))
            go((layer, "gated"))
        total = middle
        kept = []
        if special:
            gate, value, total = gated_forward(
                waits,
                mine,
                second,
                gated_w[layer],
                total,
                norm_pack,
                PARTS * hidden,
                True,
                tuple(range(PARTS)),
            )
            clock[:] = [total]
            kept = [(gate, value)]
        else:
            for part in range(PARTS):
                gate, value, total = gated_forward(
                    [], mine, second, gated_w[layer][part], total, norm_pack, hidden, part == 0
                )
                kept.append((gate, value))
        saved.append((state, normed, biased, conv, scale, middle, second, kept))
        outputs.append(total)
        state = total

    gradient = glow = cotangent[0]
    big = [None] * layers
    small = [None] * layers
    moving = {}

    def forward_on(*names):
        sent = []
        for name in names:
            if name in moving:
                sent.extend(next(moving[name], ()))
        return sent

    def whole_scatter(values):
        return lax.psum_scatter(values, AXES, scatter_dimension=0)

    early = []
    nothing = jnp.zeros((8, width), f32)
    for layer in reversed(range(layers)):
        w_in, w_out = mixer_w[layer]
        norm_pack, chan_pack = packs[layer]
        state_in, normed, biased, conv, scale, middle, second, kept = saved[layer]
        passed = nothing
        gated_g = []
        by_steps = special and layer == 0
        owned = [None] * PARTS
        calls = [(part,) for part in range(PARTS)]
        if special and not by_steps:
            calls = [tuple(range(PARTS))]
        for index, taken in enumerate(calls):
            waits = []
            if by_steps:
                waits = forward_on("mixer", "part0")
            elif layer == layers - 1 and index == 0:
                waits = [state]
            if special:
                gate, value = kept[0]
                own = gated_w[layer]
            else:
                gate, value = kept[index]
                own = gated_w[layer][index]
            final = index == len(calls) - 1
            one, two, passed, mlow, sums_two = gated_backward(
                waits,
                mine,
                glow,
                gradient if final else nothing,
                passed,
                second,
                middle if final else nothing,
                norm_pack,
                gate,
                value,
                own,
                index == 0,
                final,
                by_steps,
                taken,
            )
            clock[:] = [sums_two]
            gated_g.append((one, two))
            if by_steps:
                moving[f"part{index}"] = scatter_steps(
                    one, two, clock, functools.partial(owned.__setitem__, index)
                )
        if special and not by_steps:
            rows = whole_scatter(gated_g[0][0])
            early.append(rows)
            owned = [rows[part * rows.shape[0] // PARTS :][: rows.shape[0] // PARTS] for part in range(PARTS)]
        grad_middle = passed
        inner_g = nothing
        lows = []
        found = []
        splits = [1] * (width // CB) if by_steps else [width // CB]
        start = 0
        for index, count in enumerate(splits):
            waits = []
            if by_steps:
                names = [("part0", "part1"), ("mixer", "part1"), ("part0",)]
                waits = forward_on(*names[min(index, 2)])
                if index == 1:
                    waits += early
            *got, inner_g, freq_g, low = mixer_backward(
                waits,
                start,
                count,
                split,
                mlow,
                normed,
                chan_pack,
                biased,
                conv,
                scale,
                filters[layer][0],
                w_out,
                filters[layer][1],
                freq_out[layer],
                inner_g,
            )
            lows.append(low)
            clock[:] = [freq_g]
            found.append(got)
            start += count
        in_g = jnp.concatenate([got[0] for got in found], axis=1)
        out_g = jnp.concatenate([got[1] for got in found], axis=0)
        chan_g = jnp.concatenate([got[2] for got in found], axis=1)
        mixer_g = jnp.concatenate(
            [in_g.reshape(size, in_rows, width), out_g.reshape(size, out_rows, width)], axis=1
        )

        mixer_own = [None]
        waits = []
        if special:
            order = jnp.arange(size // 2, dtype=jnp.int32) * 2 ^ me
            keep, send = [
                mixer_g.at[places].get(mode="promise_in_bounds") for places in (order, order ^ 1)
            ]
            while forward_on("mixer"):
                pass
            waits = [send, keep]
            moving["mixer"] = scatter_steps(
                keep, send, clock, functools.partial(mixer_own.__setitem__, 0)
            )
        else:
            up_g = jnp.stack([one for one, _ in gated_g], axis=1).reshape(size, -1, width)
            down_g = jnp.stack([two for _, two in gated_g], axis=1).reshape(size, -1, width)
            owned = (scatter_rows(up_g, size, me), scatter_rows(down_g, size, me))
            mixer_own[0] = scatter_rows(mixer_g, size, me)
        gradient, glow, sums_one = norm_finish(
            waits, lows, w_in, state_in, grad_middle, norm_pack
        )
        small[layer] = (chan_g, freq_g, sums_one, sums_two)
        big[layer] = (owned, mixer_own)

    def lines_of(values):
        return -(-values.size // (8 * width)) * 8

    def lined(values):
        lines = lines_of(values)
        flat_values = jnp.pad(values.reshape(-1), (0, lines * width - values.size))
        return flat_values.reshape(lines, width)

    vector = jnp.concatenate([lined(piece) for pieces in small for piece in pieces], axis=0)
    vector = jnp.pad(vector, ((0, -vector.shape[0] % 16), (0, 0)))
    if special:
        vector = hold(vector, send)
    summed = [None]
    sent = []
    moving["small"] = sum_steps(vector, size, me, functools.partial(summed.__setitem__, 0), sent)
    forward_on("mixer", "small")
    sent.extend(forward_on("mixer"))
    clock[:] = sent[:1]
    while forward_on("mixer", "small", "part1", "part0"):
        pass
    vector = summed[0]
    count = sum(lines_of(piece) for piece in small[0])
    vector = vector[: layers * count].reshape(layers, count, width)
    found = []
    start = 0
    for piece in small[0]:
        lines = lines_of(piece)
        part = vector[:, start : start + lines]
        if piece.shape[1] != width:
            part = part.reshape(layers, -1)[:, : piece.size]
        found.append(part.reshape((layers,) + piece.shape))
        start += lines
    chan_g, freq_g, sums_one, sums_two = found
    count = freq_in.shape[1]
    small = [
        jnp.stack([sums_one[:, 0], sums_two[:, 0]], axis=1),
        jnp.stack([sums_one[:, 1], sums_two[:, 1]], axis=1),
        chan_g[:, 0:3].reshape(layers, 3 * width),
        chan_g[:, 3:12].reshape(layers, 3, 3 * width),
        chan_g[:, 12:15],
        chan_g[:, 15],
        freq_g[:, :count],
        jnp.sum(freq_g[:, count:], axis=1),
        chan_g[:, 16:],
        sums_two[:, 2],
        sums_two[:, 3],
    ]

    for layer in range(layers):
        owned, mixer_own = big[layer]
        if special:
            piece = down_rows // PARTS
            up_own = jnp.concatenate(
                [part[at * piece : (at + 1) * piece] for at in range(2) for part in owned], axis=0
            ).astype(f32)
            down_own = jnp.concatenate([part[2 * piece :] for part in owned], axis=0).astype(f32)
        else:
            up_own, down_own = owned
        mixer_rows = mixer_own[0].astype(f32)
        big[layer] = (mixer_rows[:in_rows].T, mixer_rows[in_rows:], up_own.T, down_own)
    big = [jnp.stack([big[layer][index] for layer in range(layers)]) for index in range(4)]
    return (
        jnp.stack(outputs)[:, None],
        gradient[None],
        small[0],
        small[1],
        big[0],
        small[2],
        small[3],
        small[4],
        small[5],
        small[6],
        small[7],
        small[8],
        big[1],
        small[9],
        big[2],
        big[3],
        small[10],
    )


def solution(mesh):
    pairs = P(AXES, None, None)
    columns = P(None, None, AXES)
    rows = P(None, AXES, None)
    in_specs = (
        (pairs, P(AXES), pairs, P(), P(), columns)
        + (P(),) * 7
        + (rows, P(), columns, rows, P())
    )
    out_specs = (
        (P(None, AXES, None, None), pairs, P(), P(), columns)
        + (P(),) * 7
        + (rows, P(), columns, rows, P())
    )
    size = math.prod(mesh.shape.values())
    return jax.shard_map(
        functools.partial(body, size),
        mesh=mesh,
        in_specs=in_specs,
        out_specs=out_specs,
        check_vma=False,
    )
```

```python
import functools
import math

import jax
import jax.numpy as jnp
import numpy as np
from jax import lax
from jax.experimental import pallas as pl
from jax.experimental.pallas import tpu as pltpu
from jax.sharding import PartitionSpec as P

epsilon = 1e-05
f32 = jnp.float32
bf16 = jnp.bfloat16
AXES = ("wide", "narrow")
BLK = 256
BINS = 2 * BLK
CB = 256
PAD = 8
VMEM = 60 * 2**20
NN = (((1,), (0,)), ((), ()))
NT = (((1,), (1,)), ((), ()))
TN = (((0,), (0,)), ((), ()))
GELU_A = math.sqrt(2.0 / math.pi)
GELU_B = 0.044715


def dot(left, right, dims):
    return lax.dot_general(left, right, dims, preferred_element_type=f32)


def dot_fine(left, right, dims):
    return lax.dot_general(
        left, right, dims, precision=lax.Precision.HIGHEST, preferred_element_type=f32
    )


def split_low(table):
    high = table.astype(jnp.bfloat16)
    low = (table - high.astype(np.float32)).astype(jnp.bfloat16)
    return np.concatenate([high, high, low], axis=1)


def spectrum_tables():
    t = np.arange(BLK, dtype=np.float64)[None, :]
    k = np.arange(BLK, dtype=np.float64)[:, None]
    angle = 2.0 * np.pi * ((k * t) % BINS) / BINS
    forward = np.concatenate([np.cos(angle), -np.sin(angle)], axis=0)
    forward[BLK] = np.where(np.arange(BLK) % 2 == 0, 1.0, -1.0)
    weight = np.full((BINS, 1), 2.0 / BINS)
    weight[0] = 1.0 / BINS
    weight[BLK] = 1.0 / BINS
    inverse = (forward * weight).T
    return forward.astype(np.float32), inverse.astype(np.float32)


FORWARD, INVERSE = spectrum_tables()


def transform(table, values):
    return dot(table, values.astype(bf16), NN)


def transform_fine(table, values):
    high = values.astype(bf16)
    low = (values - high.astype(f32)).astype(bf16)
    return dot(table, jnp.concatenate([high, low, high], axis=0), NN)


def fold(values):
    rows, cols = values.shape
    return jnp.sum(values.reshape(rows // 8, 8, cols), axis=0)


def loop_rows(total, step, body, init):
    def run(index, carry):
        return body(pl.multiple_of(index * step, step), carry)

    return lax.fori_loop(0, total // step, run, init)


def row_mask(start, rows, cols):
    return start + lax.broadcasted_iota(jnp.int32, (rows, cols), 0)


def earlier(ref, lead, start, rows, cols, split):
    ext = ref[lead + (pl.ds(start, rows + PAD), slice(None))]
    t = row_mask(start, rows, cols)
    one = jnp.where(t != split, pltpu.roll(ext, 1, 0)[PAD:], 0.0)
    two = jnp.where((t != split) & (t != split + 1), pltpu.roll(ext, 2, 0)[PAD:], 0.0)
    return ext[PAD:], one, two


def later(ref, lead, start, rows, cols, split):
    ext = ref[lead + (pl.ds(start, rows + PAD), slice(None))]
    total = rows + PAD
    t = row_mask(start, rows, cols)
    one = jnp.where(t + 1 != split, pltpu.roll(ext, total - 1, 0)[:rows], 0.0)
    two = jnp.where(
        (t + 2 != split) & (t + 1 != split), pltpu.roll(ext, total - 2, 0)[:rows], 0.0
    )
    return ext[:rows], one, two


def norm_parts(values):
    average = jnp.mean(values, axis=-1, keepdims=True)
    centered = values - average
    variance = jnp.mean(centered * centered, axis=-1, keepdims=True)
    rstd = lax.rsqrt(variance + epsilon)
    return centered * rstd, rstd


def part_place(part, boundary):
    block = jnp.where(part <= boundary, part, part - 1)
    return pl.multiple_of(block * BLK, BLK)


def part_keep(part, boundary, split, start):
    t = row_mask(start, BLK, CB)
    front = jnp.where(part <= boundary, 1, 0)
    return jnp.where(t < split, 1, 0) == front


def load_part(ref, part, parts, boundary, split):
    start = part_place(part, boundary)
    return jnp.where(part_keep(part, boundary, split, start), ref[pl.ds(start, BLK), :], 0.0)


def store_part(ref, part, boundary, split, values):
    start = part_place(part, boundary)
    keep = part_keep(part, boundary, split, start)
    ref[pl.ds(start, BLK), :] = jnp.where(keep, values, ref[pl.ds(start, BLK), :])


def first_row(shape):
    return lax.broadcasted_iota(jnp.int32, shape, 0) == 0


def sum_terms(terms):
    total = terms[0]
    for term in terms[1:]:
        total = total + term
    return total


def mixer_forward_kernel(
    split_ref,
    state_ref,
    norm_ref,
    chan_ref,
    win_ref,
    khat_ref,
    fwd_ref,
    inv_ref,
    wout_ref,
    middle_ref,
    second_ref,
    normed_ref,
    biased_ref,
    conv_ref,
    scale_ref,
    val_ref,
    query_ref,
    prod_ref,
    spec_ref,
    res_ref,
):
    step = pl.program_id(0)
    length, width = state_ref.shape
    split = split_ref[0]
    boundary = split // BLK
    parts = length // BLK + 1

    @pl.when(step == 0)
    def _():
        def norm(row, carry):
            hat, _ = norm_parts(state_ref[pl.ds(row, 256), :].astype(f32))
            normed_ref[pl.ds(row, 256), :] = (hat * norm_ref[0:1, :] + norm_ref[1:2, :]).astype(bf16)
            return carry

        loop_rows(length, 256, norm, 0)
        val_ref[0:PAD, :] = jnp.zeros((PAD, CB), f32)

    biased_ref[:, 0:PAD, :] = jnp.zeros((3, PAD, CB), f32)
    for stream in range(3):
        biased = dot(normed_ref[...], win_ref[stream], NT) + chan_ref[stream : stream + 1, :]
        biased_ref[stream, PAD:, :] = biased

    rows = 64

    def shorten(row, carry):
        out = []
        for stream in range(3):
            now, one, two = earlier(biased_ref, (stream,), row, rows, CB, split)
            out.append(
                chan_ref[3 + stream : 4 + stream, :] * now
                + chan_ref[6 + stream : 7 + stream, :] * one
                + chan_ref[9 + stream : 10 + stream, :] * two
            )
        query_ref[pl.ds(row, rows), :] = out[0]
        val_ref[pl.ds(row + PAD, rows), :] = out[2]
        prod_ref[pl.ds(row, rows), :] = out[1] * out[2]
        return carry

    loop_rows(length, rows, shorten, 0)

    def condition(row, total):
        now, one, two = earlier(val_ref, (), row, rows, CB, split)
        cond = chan_ref[12:13, :] * now + chan_ref[13:14, :] * one + chan_ref[14:15, :] * two
        return total + fold(cond * cond)

    squares = loop_rows(length, rows, condition, jnp.zeros((8, CB), f32))
    scale = jnp.sqrt(jnp.sum(squares, axis=0, keepdims=True) * (1.0 / length) + epsilon)
    scale_ref[...] = jnp.broadcast_to(scale, (8, CB))

    for part in range(parts):
        spec_ref[part] = transform_fine(
            fwd_ref[...], load_part(prod_ref, part, parts, boundary, split)
        )

    def pairs_into(part, bound):
        low = 0 if part <= bound else bound + 1
        return [(part - source, source) for source in range(low, part + 1)]

    for bound in range(parts - 1):

        @pl.when(boundary == bound)
        def _():
            def multiply(row, carry):
                k_re = [khat_ref[m, pl.ds(row, 8), :] for m in range(parts - 1)]
                k_im = [khat_ref[m, pl.ds(row + BLK, 8), :] for m in range(parts - 1)]
                s_re = [spec_ref[v, pl.ds(row, 8), :] for v in range(parts)]
                s_im = [spec_ref[v, pl.ds(row + BLK, 8), :] for v in range(parts)]
                for part in range(parts):
                    pairs = pairs_into(part, bound)
                    res_ref[part, pl.ds(row, 8), :] = sum_terms(
                        [k_re[m] * s_re[v] - k_im[m] * s_im[v] for m, v in pairs]
                    )
                    res_ref[part, pl.ds(row + BLK, 8), :] = sum_terms(
                        [k_re[m] * s_im[v] + k_im[m] * s_re[v] for m, v in pairs]
                    )
                return carry

            loop_rows(BLK, 8, multiply, 0)
            top = first_row((8, CB))
            for part in range(parts):
                pairs = pairs_into(part, bound)
                for base in (0, BLK):
                    real = sum_terms(
                        [khat_ref[m, base : base + 8, :] * spec_ref[v, base : base + 8, :] for m, v in pairs]
                    )
                    res_ref[part, base : base + 8, :] = jnp.where(
                        top, real, res_ref[part, base : base + 8, :]
                    )

    for part in range(parts):
        store_part(conv_ref, part, boundary, split, transform_fine(inv_ref[...], res_ref[part]))

    mixed = (query_ref[...] * scale * conv_ref[...]).astype(bf16)
    update = dot(mixed, wout_ref[...], NN)

    @pl.when(step == 0)
    def _():
        middle_ref[...] = update

    @pl.when(step > 0)
    def _():
        middle_ref[...] += update

    @pl.when(step == pl.num_programs(0) - 1)
    def _():
        def finish(row, carry):
            here = pl.ds(row, 256)
            middle = state_ref[here, :].astype(f32) + middle_ref[here, :] + norm_ref[4:5, :]
            middle_ref[here, :] = middle
            hat, _ = norm_parts(middle)
            second_ref[here, :] = (hat * norm_ref[2:3, :] + norm_ref[3:4, :]).astype(bf16)
            return carry

        loop_rows(length, 256, finish, 0)


def whole_block(shape):
    return pl.BlockSpec(shape, lambda *index: (0,) * len(shape))


def fixed_block(shape):
    return pl.BlockSpec(shape, lambda *index: (0,) * len(shape), pipeline_mode=pl.Buffered(1))


def mixer_forward(after, split, state, norm_pack, chan_pack, w_in, khat, w_out):
    length, width = state.shape
    steps = width // CB
    parts = length // BLK + 1
    forward = jnp.asarray(split_low(FORWARD))
    inverse = jnp.asarray(split_low(INVERSE))
    return call_after(
        after,
        mixer_forward_kernel,
        grid=(steps,),
        in_specs=[
            pl.BlockSpec(memory_space=pltpu.SMEM),
            fixed_block((length, width)),
            fixed_block(norm_pack.shape),
            pl.BlockSpec((16, CB), lambda i: (0, i)),
            pl.BlockSpec((3, CB, width), lambda i: (0, i, 0)),
            pl.BlockSpec((parts - 1, BINS, CB), lambda i: (0, 0, i)),
            fixed_block(forward.shape),
            fixed_block(inverse.shape),
            pl.BlockSpec((CB, width), lambda i: (i, 0)),
        ],
        out_specs=[
            whole_block((length, width)),
            whole_block((length, width)),
            whole_block((length, width)),
            pl.BlockSpec((3, length + PAD, CB), lambda i: (0, 0, i)),
            pl.BlockSpec((length, CB), lambda i: (0, i)),
            pl.BlockSpec((8, CB), lambda i: (0, i)),
        ],
        out_shape=[
            jax.ShapeDtypeStruct((length, width), f32),
            jax.ShapeDtypeStruct((length, width), bf16),
            jax.ShapeDtypeStruct((length, width), bf16),
            jax.ShapeDtypeStruct((3, length + PAD, width), f32),
            jax.ShapeDtypeStruct((length, width), f32),
            jax.ShapeDtypeStruct((8, width), f32),
        ],
        scratch_shapes=[
            pltpu.VMEM((length + PAD, CB), f32),
            pltpu.VMEM((length, CB), f32),
            pltpu.VMEM((length, CB), f32),
            pltpu.VMEM((parts, BINS, CB), f32),
            pltpu.VMEM((parts, BINS, CB), f32),
        ],
        compiler_params=pltpu.CompilerParams(vmem_limit_bytes=VMEM),
        cost_estimate=cost(20e9, 40 * 2**20),
        name="mixer_forward",
    )(split, state, norm_pack, chan_pack, w_in.reshape(3, width, width), khat, forward, inverse, w_out)


PARTS = 2


def call_after(after, kernel, in_specs, **options):
    count = len(after)

    def run(*refs):
        kernel(*refs[count:])

    call = pl.pallas_call(
        run, in_specs=[pl.BlockSpec(memory_space=pl.ANY)] * count + in_specs, **options
    )
    return functools.partial(call, *after)


def cost(flops, moved):
    return pl.CostEstimate(flops=int(flops), bytes_accessed=int(moved), transcendentals=0)


def flat(block):
    return block.reshape(-1, block.shape[-1])


def load_weights(masks, taken, me_ref, refs, up_ref, down_ref, sems):
    size, piece = down_ref.shape[0] // len(taken), down_ref.shape[1]
    found = []
    count = 0
    for part, source in enumerate(taken):
        moves = []
        start = 3 * piece * source
        for array, own in zip(refs, masks):
            for slot, mask in enumerate(own):
                device = slot if mask is None else me_ref[0] ^ mask
                targets = [
                    up_ref.at[2 * (size * part + device)],
                    up_ref.at[2 * (size * part + device) + 1],
                    down_ref.at[size * part + device],
                ]
                for place, target in enumerate(targets):
                    rows = slice(start + place * piece, start + (place + 1) * piece)
                    moves.append(
                        pltpu.make_async_copy(array.at[slot, rows, :], target, sems.at[count])
                    )
                    count += 1
        found.append(moves)
    return found


def wait_weights(step, inner, found):
    for part, moves in enumerate(found):

        @pl.when(step == part * inner)
        def _():
            for move in moves:
                move.wait()


def weight_blocks(up_ref, down_ref, parts, inner, count, step):
    size = down_ref.shape[0] // parts
    part, block = step // inner, step % inner
    base = block * count
    return (
        flat(up_ref[pl.ds(2 * size * part + base, count)]),
        flat(up_ref[pl.ds(2 * size * part + size + base, count)]),
        flat(down_ref[pl.ds(size * part + base, count)]),
    )


def gated_forward_kernel(first, masks, taken, block, me_ref, second_ref, middle_ref, norm_ref, *refs):
    step = pl.program_id(0)
    length = second_ref.shape[0]
    rows = 256
    if masks:
        gate_ref, value_ref, out_ref, up_ref, down_ref, sems = refs[len(masks) :]

        @pl.when(step == 0)
        def _():
            for moves in load_weights(masks, taken, me_ref, refs[: len(masks)], up_ref, down_ref, sems):
                for move in moves:
                    move.start()

        wait_weights(
            step,
            pl.num_programs(0) // len(taken),
            load_weights(masks, taken, me_ref, refs[: len(masks)], up_ref, down_ref, sems),
        )

    else:
        up_ref, down_ref, gate_ref, value_ref, out_ref = refs
    count = block // down_ref.shape[1]
    parts = len(taken)
    gate_w, value_w, down_w = weight_blocks(
        up_ref, down_ref, parts, pl.num_programs(0) // parts, count, step
    )

    @pl.when(step == 0)
    def _():
        if first:
            out_ref[...] = middle_ref[...] + norm_ref[5:6, :]
        else:
            out_ref[...] = middle_ref[...]

    for row in range(0, length, rows):
        here = slice(row, row + rows)
        gate = dot(second_ref[here, :], gate_w, NT)
        value = dot(second_ref[here, :], value_w, NT)
        gate_ref[here, :] = gate.astype(bf16)
        value_ref[here, :] = value.astype(bf16)
        bent = jnp.tanh(GELU_A * gate * (1.0 + GELU_B * gate * gate))
        hidden = (0.5 * gate * (1.0 + bent) * value).astype(bf16)
        out_ref[here, :] += dot(hidden, down_w, NN)


def pieces_of(weight, group):
    grouped = weight.reshape(-1, PARTS, group // PARTS, weight.shape[-1])
    return [grouped[:, part] for part in range(PARTS)]


def weight_operands(weights, parts):
    anywhere = pl.BlockSpec(memory_space=pl.ANY)
    if isinstance(weights, dict):
        arrays = [piece for piece, _ in weights["pieces"]]
        masks = [own for _, own in weights["pieces"]]
        size = sum(len(own) for own in masks)
        width = arrays[0].shape[2]
        piece = weights["rows"]
        scratch = [
            pltpu.VMEM((2 * size * parts, piece, width), bf16),
            pltpu.VMEM((size * parts, piece, width), bf16),
            pltpu.SemaphoreType.DMA((3 * size * parts,)),
        ]
        return arrays, [anywhere] * len(arrays), masks, scratch, piece
    return list(weights), [fixed_block(part.shape) for part in weights], None, [], weights[1].shape[1]


def gated_forward(after, me, second, weights, before, norm_pack, hidden, first, taken=(0,), block=768):
    length, width = second.shape
    steps = hidden // block
    arrays, specs, masks, scratch, _ = weight_operands(weights, len(taken))
    return call_after(
        after,
        functools.partial(gated_forward_kernel, first, masks, taken, block),
        grid=(steps,),
        in_specs=[
            pl.BlockSpec(memory_space=pltpu.SMEM),
            fixed_block((length, width)),
            fixed_block((length, width)),
            fixed_block(norm_pack.shape),
        ]
        + specs,
        out_specs=[
            pl.BlockSpec((length, block), lambda i: (0, i)),
            pl.BlockSpec((length, block), lambda i: (0, i)),
            whole_block((length, width)),
        ],
        out_shape=[
            jax.ShapeDtypeStruct((length, hidden), bf16),
            jax.ShapeDtypeStruct((length, hidden), bf16),
            jax.ShapeDtypeStruct((length, width), f32),
        ],
        scratch_shapes=scratch,
        compiler_params=pltpu.CompilerParams(vmem_limit_bytes=VMEM),
        cost_estimate=cost(6 * length * width * hidden, 20 * 2**20),
        name="gated_forward",
    )(me, second, before, norm_pack, *arrays)


def norm_backward(values, grad_out, gain):
    hat, rstd = norm_parts(values)
    grad_hat = grad_out * gain
    mean_one = jnp.mean(grad_hat, axis=-1, keepdims=True)
    mean_two = jnp.mean(grad_hat * hat, axis=-1, keepdims=True)
    return rstd * (grad_hat - mean_one - hat * mean_two), grad_out * hat


def gated_backward_kernel(
    first,
    last,
    masks,
    own_order,
    taken,
    block,
    me_ref,
    glow_ref,
    grad_ref,
    before_ref,
    second_ref,
    middle_ref,
    norm_ref,
    gate_ref,
    value_ref,
    *refs,
):
    step = pl.program_id(0)
    steps = pl.num_programs(0)
    length, width = glow_ref.shape
    rows = 256
    slots = bool(masks)
    if slots:
        pieces, refs = refs[: len(masks)], refs[len(masks) :]
    else:
        up_ref, down_ref = refs[:2]
        refs = refs[2:]
    one_ref, two_ref, out_ref, mlow_ref, small_ref, hidden_ref, dgate_ref, dvalue_ref, stage_ref, sems = refs[:10]
    if slots:
        up_ref, down_ref, load_sems = refs[10:]
    piece = down_ref.shape[1]
    count = block // piece
    side = step % 2

    @pl.when(step == 0)
    def _():
        if slots:
            for moves in load_weights(masks, taken, me_ref, pieces, up_ref, down_ref, load_sems):
                for move in moves:
                    move.start()
        if first:
            out_ref[...] = jnp.zeros_like(out_ref)
        else:
            out_ref[...] = before_ref[...]

    parts = len(taken)
    inner = steps // parts
    if slots:
        wait_weights(step, inner, load_weights(masks, taken, me_ref, pieces, up_ref, down_ref, load_sems))
    gate_w, value_w, down_w = weight_blocks(up_ref, down_ref, parts, inner, count, step)

    def copies(at_step, kind):
        group = 2 if slots and kind < 2 else 1
        span = group * piece
        base = at_step % inner * count // group
        start = at_step // inner * 3 * piece
        found = []
        for item in range(count // group):
            source = stage_ref.at[at_step % 2, kind, item * span : (item + 1) * span, :]
            sem = sems.at[at_step % 2, kind, item]
            if not slots:
                place = base + item + (kind * inner * count if kind < 2 else 0)
                found.append((source, sem, [(None, (two_ref if kind == 2 else one_ref).at[place])]))
                continue
            device = base + item + (kind * inner * count // 2 if kind < 2 else 0)
            rows_at = pl.ds(start + (2 * piece if kind == 2 else 0), span)
            if not own_order:
                found.append((source, sem, [(None, one_ref.at[device, rows_at, :])]))
                continue
            mask = device ^ me_ref[0]
            place = mask >> 1
            core = mask & 1
            targets = [
                (core == 0, one_ref.at[place, rows_at, :]),
                (core == 1, two_ref.at[place, rows_at, :]),
            ]
            found.append((source, sem, targets))
        return found

    def send(kind):
        for source, sem, targets in copies(step, kind):
            for condition, target in targets:
                move = pltpu.make_async_copy(source, target, sem)
                if condition is None:
                    move.start()
                else:
                    pl.when(condition)(move.start)

    def drain(at_step):
        for kind in range(3):
            for source, sem, targets in copies(at_step, kind):
                pltpu.make_async_copy(source, targets[0][1], sem).wait()

    for row in range(0, length, rows):
        here = slice(row, row + rows)
        grad_hidden = dot(glow_ref[here, :], down_w, NT)
        gate = gate_ref[here, :].astype(f32)
        value = value_ref[here, :].astype(f32)
        square = gate * gate
        bent = jnp.tanh(GELU_A * gate * (1.0 + GELU_B * square))
        half = 0.5 * (1.0 + bent)
        unit = half * gate
        slope = half + 0.5 * gate * (1.0 - bent * bent) * (GELU_A * (1.0 + 3.0 * GELU_B * square))
        hidden_ref[here, :] = (unit * value).astype(bf16)
        dgate = (grad_hidden * value * slope).astype(bf16)
        dvalue = (grad_hidden * unit).astype(bf16)
        dgate_ref[here, :] = dgate
        dvalue_ref[here, :] = dvalue
        out_ref[here, :] += dot(dgate, gate_w, NN) + dot(dvalue, value_w, NN)

    @pl.when(step > 1)
    def _():
        drain(step - 2)

    stage_ref[side, 0] = dot(dgate_ref[...], second_ref[...], TN).astype(bf16)
    send(0)
    stage_ref[side, 1] = dot(dvalue_ref[...], second_ref[...], TN).astype(bf16)
    send(1)
    stage_ref[side, 2] = dot(hidden_ref[...], glow_ref[...], TN).astype(bf16)
    send(2)

    @pl.when(step == steps - 1)
    def _():
        if not last:
            small_ref[...] = jnp.zeros_like(small_ref)
            mlow_ref[...] = jnp.zeros_like(mlow_ref)
        else:

            def finish(row, carry):
                here = pl.ds(row, 128)
                grad_out = out_ref[here, :]
                grad = grad_ref[here, :].astype(f32)
                change, gain_rows = norm_backward(middle_ref[here, :], grad_out, norm_ref[2:3, :])
                total = grad + change
                out_ref[here, :] = total
                mlow_ref[here, :] = total.astype(bf16)
                return (
                    carry[0] + fold(gain_rows),
                    carry[1] + fold(grad_out),
                    carry[2] + fold(total),
                    carry[3] + fold(grad),
                )

            zero = jnp.zeros((8, width), f32)
            sums = loop_rows(length, 128, finish, (zero, zero, zero, zero))
            small_ref[...] = jnp.concatenate(
                [jnp.sum(part, axis=0, keepdims=True) for part in sums]
                + [jnp.zeros((4, width), f32)],
                axis=0,
            )

        @pl.when(steps > 1)
        def _():
            drain(step - 1)

        drain(step)


def gated_backward(after,
    me, glow, grad, before, second, middle, norm_pack, gate, value, weights, first, last, own_order, taken=(0,), block=768
):
    length, width = second.shape
    parts = len(taken)
    inner = gate.shape[1] // block
    start = 0
    if isinstance(weights, dict):
        start = taken[0] * inner // PARTS
        inner = parts * inner // PARTS
    hidden = inner * block
    arrays, specs, masks, scratch, piece = weight_operands(weights, parts)
    count = block // piece
    column = pl.BlockSpec((length, block), lambda i: (0, i + start))
    anywhere = pl.BlockSpec(memory_space=pl.ANY)
    if masks:
        size = sum(len(own) for own in masks)
        places = [jax.ShapeDtypeStruct((size // 2, 3 * piece * parts, width), bf16)] * 2
        if not own_order:
            places = [
                jax.ShapeDtypeStruct((size, 3 * piece * parts, width), bf16),
                jax.ShapeDtypeStruct((16, width), bf16),
            ]
    else:
        places = [jax.ShapeDtypeStruct(array.shape, bf16) for array in arrays]
    return call_after(
        after,
        functools.partial(
            gated_backward_kernel, first, last, masks, own_order, taken, block
        ),
        grid=(inner,),
        in_specs=[
            pl.BlockSpec(memory_space=pltpu.SMEM),
            fixed_block((length, width)),
            fixed_block(grad.shape),
            fixed_block(before.shape),
            fixed_block((length, width)),
            fixed_block(middle.shape),
            fixed_block(norm_pack.shape),
            column,
            column,
        ]
        + specs,
        out_specs=[
            anywhere,
            anywhere,
            whole_block((length, width)),
            whole_block((length if last else 16, width)),
            whole_block((8, width)),
        ],
        out_shape=places
        + [
            jax.ShapeDtypeStruct((length, width), f32),
            jax.ShapeDtypeStruct((length if last else 16, width), bf16),
            jax.ShapeDtypeStruct((8, width), f32),
        ],
        scratch_shapes=[
            pltpu.VMEM((length, block), bf16),
            pltpu.VMEM((length, block), bf16),
            pltpu.VMEM((length, block), bf16),
            pltpu.VMEM((2, 3, block, width), bf16),
            pltpu.SemaphoreType.DMA((2, 3, count)),
        ]
        + scratch,
        compiler_params=pltpu.CompilerParams(vmem_limit_bytes=VMEM),
        cost_estimate=cost(12 * length * width * hidden, 20 * 2**20),
        name="gated_backward",
    )(me, glow, grad, before, second, middle, norm_pack, gate, value, *arrays)


def mixer_backward_kernel(
    first,
    last,
    split_ref,
    mlow_ref,
    normed_ref,
    chan_ref,
    biased_ref,
    conv_ref,
    scale_ref,
    khat_ref,
    fwd_ref,
    inv_ref,
    wout_ref,
    kernel_ref,
    inner_t_ref,
    slope_ref,
    features_t_ref,
    freq_out_ref,
    inner_before_ref,
    win_g_ref,
    wout_g_ref,
    chan_g_ref,
    inner_g_ref,
    freq_g_ref,
    low_ref,
    kern_g_ref,
    key_ref,
    val_ref,
    prod_ref,
    dconv_ref,
    mixed_ref,
    cond_ref,
    dpad_ref,
    spec_ref,
    dspec_ref,
    res_ref,
    gram_ref,
):
    step = pl.program_id(0)
    length, width = mlow_ref.shape
    split = split_ref[0]
    boundary = split // BLK
    parts = length // BLK + 1
    rows = 64

    @pl.when(step == 0)
    def _():
        val_ref[0:PAD, :] = jnp.zeros((PAD, CB), f32)
        cond_ref[length:, :] = jnp.zeros((PAD, CB), f32)
        dpad_ref[:, length:, :] = jnp.zeros((3, PAD, CB), f32)

    dconv_ref[...] = dot(mlow_ref[...], wout_ref[...], NT)
    scale = scale_ref[0:1, :]

    def gate(row, total):
        here = pl.ds(row, rows)
        out = []
        for stream in range(3):
            now, one, two = earlier(biased_ref, (stream,), row, rows, CB, split)
            out.append(
                chan_ref[3 + stream : 4 + stream, :] * now
                + chan_ref[6 + stream : 7 + stream, :] * one
                + chan_ref[9 + stream : 10 + stream, :] * two
            )
        query, key, value = out
        key_ref[here, :] = key
        val_ref[pl.ds(row + PAD, rows), :] = value
        prod_ref[here, :] = key * value
        grad = dconv_ref[here, :]
        conv = conv_ref[here, :]
        mixed_ref[here, :] = (query * scale * conv).astype(bf16)
        dpad_ref[0, here, :] = grad * scale * conv
        through = grad * query
        dconv_ref[here, :] = through * scale
        return total + fold(through * conv)

    scale_sum = loop_rows(length, rows, gate, jnp.zeros((8, CB), f32))
    grad_scale = jnp.sum(scale_sum, axis=0, keepdims=True)
    factor = grad_scale / (scale * float(length))

    def condition(row, carry):
        now, one, two = earlier(val_ref, (), row, rows, CB, split)
        cond_ref[pl.ds(row, rows), :] = (
            chan_ref[12:13, :] * now + chan_ref[13:14, :] * one + chan_ref[14:15, :] * two
        )
        return carry

    loop_rows(length, rows, condition, 0)

    for part in range(parts):
        spec_ref[part] = transform(fwd_ref[...], load_part(prod_ref, part, parts, boundary, split))
        dspec_ref[part] = transform(fwd_ref[...], load_part(dconv_ref, part, parts, boundary, split))

    def pairs_from(source, bound):
        high = bound if source <= bound else parts - 1
        return [(part - source, part) for part in range(source, high + 1)]

    def pairs_apart(lag, bound):
        found = []
        for source in range(parts - lag):
            if (source <= bound) == (source + lag <= bound):
                found.append((source, source + lag))
        return found

    odd_sign = jnp.where(lax.broadcasted_iota(jnp.int32, (8, CB), 0) % 2 == 0, 1.0, -1.0)

    def chain(grams):
        return [
            grams[lag] + odd_sign * grams[lag + 1] if lag + 1 < parts - 1 else grams[lag]
            for lag in range(parts - 1)
        ]

    def or_zero(terms):
        return sum_terms(terms) if terms else jnp.zeros((8, CB), f32)

    for bound in range(parts - 1):

        @pl.when(boundary == bound)
        def _():
            def multiply(row, carry):
                k_re = [khat_ref[m, pl.ds(row, 8), :] for m in range(parts - 1)]
                k_im = [khat_ref[m, pl.ds(row + BLK, 8), :] for m in range(parts - 1)]
                e_re = [dspec_ref[v, pl.ds(row, 8), :] for v in range(parts)]
                e_im = [dspec_ref[v, pl.ds(row + BLK, 8), :] for v in range(parts)]
                for source in range(parts):
                    pairs = pairs_from(source, bound)
                    res_ref[source, pl.ds(row, 8), :] = sum_terms(
                        [k_re[m] * e_re[v] + k_im[m] * e_im[v] for m, v in pairs]
                    )
                    res_ref[source, pl.ds(row + BLK, 8), :] = sum_terms(
                        [k_re[m] * e_im[v] - k_im[m] * e_re[v] for m, v in pairs]
                    )
                s_re = [spec_ref[v, pl.ds(row, 8), :] for v in range(parts)]
                s_im = [spec_ref[v, pl.ds(row + BLK, 8), :] for v in range(parts)]
                real, imag = [], []
                for lag in range(parts - 1):
                    pairs = pairs_apart(lag, bound)
                    real.append(
                        or_zero([s_re[j] * e_re[i] + s_im[j] * e_im[i] for j, i in pairs])
                    )
                    imag.append(
                        or_zero([s_re[j] * e_im[i] - s_im[j] * e_re[i] for j, i in pairs])
                    )
                for lag, (one, two) in enumerate(zip(chain(real), chain(imag))):
                    gram_ref[lag, pl.ds(row, 8), :] = one
                    gram_ref[lag, pl.ds(row + BLK, 8), :] = two
                return carry

            loop_rows(BLK, 8, multiply, 0)
            top = first_row((8, CB))
            for base in (0, BLK):
                tile = slice(base, base + 8)
                for source in range(parts):
                    real = sum_terms(
                        [khat_ref[m, tile, :] * dspec_ref[v, tile, :] for m, v in pairs_from(source, bound)]
                    )
                    res_ref[source, tile, :] = jnp.where(top, real, res_ref[source, tile, :])
                grams = [
                    or_zero([spec_ref[j, tile, :] * dspec_ref[i, tile, :] for j, i in pairs_apart(lag, bound)])
                    for lag in range(parts - 1)
                ]
                for lag, real in enumerate(chain(grams)):
                    gram_ref[lag, tile, :] = jnp.where(top, real, gram_ref[lag, tile, :])

    for part in range(parts):
        store_part(prod_ref, part, boundary, split, transform(inv_ref[...], res_ref[part]))
    for lag in range(parts - 1):
        kern_g_ref[lag * BLK : (lag + 1) * BLK, :] = transform(inv_ref[...], gram_ref[lag])

    def spread(row, carry):
        here = pl.ds(row, rows)
        change = prod_ref[here, :]
        value = val_ref[pl.ds(row + PAD, rows), :]
        dpad_ref[1, here, :] = change * value
        now, one, two = later(cond_ref, (), row, rows, CB, split)
        from_cond = chan_ref[12:13, :] * now + chan_ref[13:14, :] * one + chan_ref[14:15, :] * two
        dpad_ref[2, here, :] = change * key_ref[here, :] + factor * from_cond
        return (
            carry[0] + fold(value * now),
            carry[1] + fold(value * one),
            carry[2] + fold(value * two),
        )

    zero = jnp.zeros((8, CB), f32)
    cond_sums = loop_rows(length, rows, spread, (zero, zero, zero))
    sums = [None] * 12
    for stream in range(3):

        def back(row, carry, stream=stream):
            now, one, two = later(dpad_ref, (stream,), row, rows, CB, split)
            biased = biased_ref[stream, pl.ds(row + PAD, rows), :]
            change = (
                chan_ref[3 + stream : 4 + stream, :] * now
                + chan_ref[6 + stream : 7 + stream, :] * one
                + chan_ref[9 + stream : 10 + stream, :] * two
            )
            low_ref[stream, pl.ds(row, rows), :] = change.astype(bf16)
            return (
                carry[0] + fold(change),
                carry[1] + fold(biased * now),
                carry[2] + fold(biased * one),
                carry[3] + fold(biased * two),
            )

        got = loop_rows(length, rows, back, (zero, zero, zero, zero))
        for index in range(4):
            sums[3 * index + stream] = got[index]
    decay = chan_ref[15:16, :]
    level = jnp.sqrt(2.0 * decay)
    lead = 0.5 / decay

    def profile(row, total):
        here = pl.ds(row, rows)
        position = row_mask(row, rows, CB).astype(f32)
        change = kern_g_ref[here, :]
        kern_g_ref[here, :] = change * (jnp.exp(-position * decay) * level)
        return total + fold(change * kernel_ref[here, :] * (lead - position))

    decay_sum = loop_rows(length, rows, profile, zero)
    chan_g_ref[0:16, :] = jnp.concatenate(
        [jnp.sum(part, axis=0, keepdims=True) for part in sums]
        + [factor * jnp.sum(part, axis=0, keepdims=True) for part in cond_sums]
        + [jnp.sum(decay_sum, axis=0, keepdims=True)],
        axis=0,
    )
    chan_g_ref[16:, :] = dot_fine(inner_t_ref[...], kern_g_ref[...], NN)
    inner_g = dot_fine(kern_g_ref[...], freq_out_ref[...], NT)

    @pl.when(step == 0)
    def _():
        if first:
            inner_g_ref[...] = inner_g
        else:
            inner_g_ref[...] = inner_before_ref[...] + inner_g

    @pl.when(step > 0)
    def _():
        inner_g_ref[...] += inner_g

    wout_g_ref[...] = dot(mixed_ref[...], mlow_ref[...], TN).astype(bf16)
    for stream in range(3):
        win_g_ref[stream] = dot(low_ref[stream], normed_ref[...], TN).astype(bf16)
    if not last:
        freq_g_ref[...] = jnp.zeros_like(freq_g_ref)
        return

    @pl.when(step == pl.num_programs(0) - 1)
    def _():
        phase_g = inner_g_ref[...] * slope_ref[...]
        freq_g_ref[0 : phase_g.shape[1], :] = dot_fine(features_t_ref[...], phase_g, NN)
        freq_g_ref[phase_g.shape[1] :, :] = fold(phase_g)
def mixer_backward(after, start, steps, split, mlow, normed, chan_pack, biased, conv, scale, khat, w_out, filtered, freq_out, inner_before):
    length, width = mlow.shape
    last = (start + steps) * CB == width
    parts = length // BLK + 1
    forward = jnp.asarray(FORWARD, bf16)
    inverse = jnp.asarray(INVERSE, bf16)
    kernel, inner_t, slope, features_t = filtered
    hidden = freq_out.shape[0]
    full = fixed_block((length, width))
    tall = pltpu.VMEM((length, CB), f32)
    tall_pad = pltpu.VMEM((length + PAD, CB), f32)
    spectrum = pltpu.VMEM((parts, BINS, CB), f32)
    return call_after(
        after,
        functools.partial(mixer_backward_kernel, start == 0, last),
        grid=(steps,),
        in_specs=[
            pl.BlockSpec(memory_space=pltpu.SMEM),
            full,
            full,
            pl.BlockSpec((16, CB), lambda i: (0, i + start)),
            pl.BlockSpec((3, length + PAD, CB), lambda i: (0, 0, i + start)),
            pl.BlockSpec((length, CB), lambda i: (0, i + start)),
            pl.BlockSpec((8, CB), lambda i: (0, i + start)),
            pl.BlockSpec((parts - 1, BINS, CB), lambda i: (0, 0, i + start)),
            fixed_block(forward.shape),
            fixed_block(inverse.shape),
            pl.BlockSpec((CB, width), lambda i: (i + start, 0)),
            pl.BlockSpec((length, CB), lambda i: (0, i + start)),
            fixed_block(inner_t.shape),
            fixed_block(slope.shape),
            fixed_block(features_t.shape),
            pl.BlockSpec((freq_out.shape[0], CB), lambda i: (0, i + start)),
            fixed_block(inner_before.shape),
        ],
        out_specs=[
            pl.BlockSpec((3, CB, width), lambda i: (0, i, 0)),
            pl.BlockSpec((CB, width), lambda i: (i, 0)),
            pl.BlockSpec((16 + hidden, CB), lambda i: (0, i)),
            whole_block((length, hidden)),
            whole_block((hidden + 8, hidden)),
            pl.BlockSpec((3, length, CB), lambda i: (0, 0, i)),
        ],
        out_shape=[
            jax.ShapeDtypeStruct((3, steps * CB, width), bf16),
            jax.ShapeDtypeStruct((steps * CB, width), bf16),
            jax.ShapeDtypeStruct((16 + hidden, steps * CB), f32),
            jax.ShapeDtypeStruct((length, hidden), f32),
            jax.ShapeDtypeStruct((hidden + 8, hidden), f32),
            jax.ShapeDtypeStruct((3, length, steps * CB), bf16),
        ],
        scratch_shapes=[
            tall,
            tall,
            tall_pad,
            tall,
            tall,
            pltpu.VMEM((length, CB), bf16),
            tall_pad,
            pltpu.VMEM((3, length + PAD, CB), f32),
            spectrum,
            spectrum,
            spectrum,
            pltpu.VMEM((parts - 1, BINS, CB), f32),
        ],
        compiler_params=pltpu.CompilerParams(vmem_limit_bytes=VMEM),
        cost_estimate=cost(12e9 * steps, 14 * 2**20 * steps),
        name="mixer_backward",
    )(
        split,
        mlow,
        normed,
        chan_pack,
        biased,
        conv,
        scale,
        khat,
        forward,
        inverse,
        w_out,
        kernel,
        inner_t,
        slope,
        features_t,
        freq_out,
        inner_before,
    )


def norm_finish_kernel(state_ref, grad_ref, norm_ref, win_ref, *refs):
    *low_refs, out_ref, low_out_ref, small_ref = refs
    rows, width = state_ref.shape
    update = None
    start = 0
    for low_ref in low_refs:
        count = low_ref.shape[2]
        for stream in range(3):
            term = dot(low_ref[stream], win_ref[stream, start : start + count, :], NN)
            update = term if update is None else update + term
        start += count
    change, gain_rows = norm_backward(state_ref[...].astype(f32), update, norm_ref[0:1, :])
    total = grad_ref[...] + change
    out_ref[...] = total
    low_out_ref[...] = total.astype(bf16)

    @pl.when(pl.program_id(0) == 0)
    def _():
        small_ref[...] = jnp.zeros_like(small_ref)

    sums = [jnp.sum(part, axis=0, keepdims=True) for part in (gain_rows, update)]
    small_ref[...] += jnp.concatenate(sums + [jnp.zeros((6, width), f32)], axis=0)


def norm_finish(after, lows, w_in, state, grad, norm_pack, block=256):
    length, width = state.shape
    tile = pl.BlockSpec((block, width), lambda i: (i, 0))
    return call_after(
        after,
        norm_finish_kernel,
        grid=(length // block,),
        in_specs=[tile, tile, whole_block(norm_pack.shape), fixed_block((3, width, width))]
        + [pl.BlockSpec((3, block, low.shape[2]), lambda i: (0, i, 0)) for low in lows],
        out_specs=[tile, tile, whole_block((8, width))],
        out_shape=[
            jax.ShapeDtypeStruct((length, width), f32),
            jax.ShapeDtypeStruct((length, width), bf16),
            jax.ShapeDtypeStruct((8, width), f32),
        ],
        compiler_params=pltpu.CompilerParams(vmem_limit_bytes=VMEM),
        cost_estimate=cost(6 * length * width * width, 20 * 2**20),
        name="norm_finish",
    )(state, grad, norm_pack, w_in.reshape(3, width, width), *lows)


def filter_features(length, count):
    half = count // 2
    positions = np.arange(length, dtype=np.float64)[:, None]
    harmonics = np.arange(1, half + 1, dtype=np.float64)[None, :]
    angles = 2.0 * np.pi * ((positions * harmonics) % length) / length
    return np.concatenate([np.sin(angles), np.cos(angles)], axis=1).astype(np.float32)


def highest(left, right, dims):
    return lax.dot_general(left, right, dims, precision=lax.Precision.HIGHEST)


def filter_kernel_body(inner_ref, out_ref, chan_ref, fwd_ref, kernel_ref, khat_ref):
    length = inner_ref.shape[0]
    decay = chan_ref[15:16, :]
    level = jnp.sqrt(2.0 * decay)
    sign = jnp.where(lax.broadcasted_iota(jnp.int32, (BINS, CB), 0) % 2 == 0, 1.0, -1.0)
    before = None
    for block in range(length // BLK):
        here = slice(block * BLK, (block + 1) * BLK)
        profile = dot_fine(inner_ref[here, :], out_ref[...], NN)
        position = row_mask(block * BLK, BLK, CB).astype(f32)
        kernel = profile * (jnp.exp(-position * decay) * level)
        kernel_ref[here, :] = kernel
        spectrum = transform_fine(fwd_ref[...], kernel)
        khat_ref[block] = spectrum if before is None else spectrum + sign * before
        before = spectrum


def filter_forward(length, chan_pack, freq_in, freq_bias, freq_out):
    table = filter_features(length, freq_in.shape[0])
    features = jnp.asarray(table)
    phase = highest(features, freq_in, NN) + freq_bias
    inner = jnp.sin(phase)
    width = freq_out.shape[1]
    hidden = inner.shape[1]
    forward = jnp.asarray(split_low(FORWARD))
    blocks = length // BLK
    kernel, khat = pl.pallas_call(
        filter_kernel_body,
        grid=(width // CB,),
        in_specs=[
            fixed_block((length, hidden)),
            pl.BlockSpec((hidden, CB), lambda i: (0, i)),
            pl.BlockSpec((16, CB), lambda i: (0, i)),
            fixed_block(forward.shape),
        ],
        out_specs=[
            pl.BlockSpec((length, CB), lambda i: (0, i)),
            pl.BlockSpec((blocks, BINS, CB), lambda i: (0, 0, i)),
        ],
        out_shape=[
            jax.ShapeDtypeStruct((length, width), f32),
            jax.ShapeDtypeStruct((blocks, BINS, width), f32),
        ],
        compiler_params=pltpu.CompilerParams(vmem_limit_bytes=VMEM),
        cost_estimate=cost(6e9, 10 * 2**20),
        name="filter_forward",
    )(inner, freq_out, chan_pack, forward)
    return khat, (kernel, inner.T, jnp.cos(phase), jnp.asarray(table.T.copy()))


def cube_orders(size):
    bits = [1 << place for place in range(1, size.bit_length() - 1)]
    if len(bits) < 2:
        return [bits + [1], bits + [1]]
    return [bits + [1], bits[:-2] + [bits[-1], bits[-2]] + [1]]


def slot_table(order, size):
    table = np.zeros(size, np.int32)
    for slot in range(size):
        mask = sum(bit for place, bit in enumerate(order) if slot >> place & 1)
        table[mask] = slot
    return table


def swap(values, bit, size):
    return lax.ppermute(values, AXES, [(index, index ^ bit) for index in range(size)])


def cube_gather(block, order, size, me):
    held = block[None]
    for bit in order:
        held = jnp.concatenate([held, swap(held, bit, size)], axis=0)
    places = jnp.asarray(slot_table(order, size))[jnp.arange(size, dtype=jnp.int32) ^ me]
    return jnp.take(held, places, axis=0)


def cube_scatter(blocks, order, size, me):
    masks = np.zeros(size, np.int32)
    masks[slot_table(order, size)] = np.arange(size)
    held = jnp.take(blocks, jnp.asarray(masks) ^ me, axis=0)
    for place in reversed(range(len(order))):
        half = 1 << place
        got = swap(held[half:], order[place], size)
        held = held[:half].astype(f32) + got.astype(f32)
        if place:
            held = held.astype(bf16)
    return held[0]


def cube_sum(values, size):
    for place in range(size.bit_length() - 1):
        values = values + swap(values, 1 << place, size)
    return values


def halves(rows):
    if rows < 32:
        return rows // 2
    return (rows // 2 + 15) // 16 * 16


def gather_rows(block, size, me):
    cut = halves(block.shape[0])
    orders = cube_orders(size)
    one = cube_gather(block[:cut], orders[0], size, me)
    two = cube_gather(block[cut:], orders[1], size, me)
    return jnp.concatenate([one, two], axis=1)


def scatter_rows(blocks, size, me):
    cut = halves(blocks.shape[1])
    orders = cube_orders(size)
    one = cube_scatter(blocks[:, :cut], orders[0], size, me)
    two = cube_scatter(blocks[:, cut:], orders[1], size, me)
    return jnp.concatenate([one, two], axis=0)


def hold(value, *others):
    for other in others:
        value = value + (other[(0,) * other.ndim] * 0).astype(value.dtype)
    return value


def hold_place(value, *others):
    if not others:
        return value
    anywhere = pl.BlockSpec(memory_space=pl.ANY)

    def nothing(*refs):
        pass

    return pl.pallas_call(
        nothing,
        in_specs=[anywhere] * (1 + len(others)),
        out_specs=anywhere,
        out_shape=jax.ShapeDtypeStruct(value.shape, value.dtype),
        input_output_aliases={0: 0},
        cost_estimate=cost(0, 0),
        name="hold_place",
    )(value, *others)


def gather_steps(block, after, clock, done):
    size = 32
    block = hold(block, *after)
    came = [swap(block, bit, size) for bit in (2, 4, 6)]
    yield [block]
    line = hold(jnp.stack([block] + came), *clock)
    others = [swap(line, bit, size) for bit in (8, 16, 24)]
    own = swap(line, 1, size)
    yield [line]
    others = [hold_place(other, *clock) for other in others]
    pieces = []
    for bit, piece in zip((0, 8, 16, 24), [line] + others):
        masks = tuple(bit + place for place in (0, 2, 4, 6))
        pieces.append((piece, masks))
        other = swap(piece, 1, size) if bit else own
        pieces.append((other, tuple(mask + 1 for mask in masks)))
    yield others
    done(pieces)


def place_kernel(masks, cuts, me_ref, *refs):
    pieces = refs[: len(masks)]
    targets = refs[len(masks) : len(masks) + len(cuts)]
    held, in_sems, out_sems = refs[-3:]
    loads = []
    slot = 0
    for index, (piece, own) in enumerate(zip(pieces, masks)):
        load = pltpu.make_async_copy(piece, held.at[slot : slot + len(own)], in_sems.at[index])
        load.start()
        loads.append((load, slot, own))
        slot += len(own)
    moves = []
    for load, slot, own in loads:
        load.wait()
        for place, mask in enumerate(own):
            device = me_ref[0] ^ mask
            start = 0
            for target, rows in zip(targets, cuts):
                move = pltpu.make_async_copy(
                    held.at[slot + place, start : start + rows, :],
                    target.at[device],
                    out_sems.at[len(moves)],
                )
                move.start()
                moves.append(move)
                start += rows
    for move in moves:
        move.wait()


def place_pieces(pieces, cuts, me):
    arrays = [piece for piece, _ in pieces]
    masks = [own for _, own in pieces]
    size = sum(len(own) for own in masks)
    width = arrays[0].shape[-1]
    anywhere = pl.BlockSpec(memory_space=pl.ANY)
    return pl.pallas_call(
        functools.partial(place_kernel, masks, cuts),
        in_specs=[pl.BlockSpec(memory_space=pltpu.SMEM)] + [anywhere] * len(arrays),
        out_specs=[anywhere] * len(cuts),
        out_shape=[jax.ShapeDtypeStruct((size, rows, width), bf16) for rows in cuts],
        scratch_shapes=[
            pltpu.VMEM((size, sum(cuts), width), bf16),
            pltpu.SemaphoreType.DMA((len(masks),)),
            pltpu.SemaphoreType.DMA((size * len(cuts),)),
        ],
        compiler_params=pltpu.CompilerParams(vmem_limit_bytes=VMEM),
        cost_estimate=cost(0, 2 * sum(cuts) * size * width * 2),
        name="place_pieces",
    )(me, *arrays)


def scatter_steps(keep, send, clock, done):
    size = 32
    shape = (4, 4) + keep.shape[1:]
    keep = keep.reshape(shape)
    got = swap(send, 1, size).reshape(shape)
    yield [send]

    def both(group):
        return keep[group].astype(f32) + got[group].astype(f32)

    out = [hold(both(group), *clock).astype(bf16) for group in (3, 1, 2)]
    came = [swap(piece, bit, size) for piece, bit in zip(out, (24, 8, 16))]
    yield out
    line = hold(sum_terms([both(0)] + [piece.astype(f32) for piece in came]), *clock)
    low = [line[place].astype(bf16) for place in (1, 2, 3)]
    came = [swap(piece, 2 * place + 2, size) for place, piece in enumerate(low)]
    yield low
    done(hold(sum_terms([line[0]] + [piece.astype(f32) for piece in came]), *clock))


def sum_steps(values, size, me, done, after=()):
    halved = values.reshape((2, -1) + values.shape[1:])
    core = me % 2
    send = jnp.take(halved, 1 - core, axis=0, mode="clip")
    part = jnp.take(halved, core, axis=0, mode="clip") + swap(send, 1, size)
    yield [send]
    part = hold(part, *after)
    for place in range(1, size.bit_length() - 1):
        came = swap(part, 1 << place, size)
        yield [part]
        part = part + came
    other = swap(part, 1, size)
    yield [part]
    done(jnp.concatenate([jnp.where(core == 0, part, other), jnp.where(core == 0, other, part)], axis=0))


def body(
    size,
    tokens,
    split_point,
    cotangent,
    norm_gain,
    norm_shift,
    in_weight,
    in_bias,
    short_taps,
    cond_taps,
    decay_rate,
    freq_in,
    freq_bias,
    freq_out,
    out_weight,
    out_bias,
    up_weight,
    down_weight,
    down_bias,
):
    layers = in_weight.shape[0]
    length, width = tokens.shape[1:]
    me = lax.axis_index(AXES)
    split = split_point.astype(jnp.int32)
    state = tokens[0]
    in_rows = in_weight.shape[2]
    out_rows = out_weight.shape[1]

    packs = []
    for layer in range(layers):
        norm_pack = jnp.concatenate(
            [
                jnp.stack([norm_gain[layer, 0], norm_shift[layer, 0]]),
                jnp.stack([norm_gain[layer, 1], norm_shift[layer, 1]]),
                out_bias[layer][None],
                down_bias[layer][None],
                jnp.zeros((2, width), f32),
            ]
        )
        chan_pack = jnp.concatenate(
            [
                in_bias[layer].reshape(3, width),
                short_taps[layer].reshape(9, width),
                cond_taps[layer],
                decay_rate[layer][None],
            ]
        )
        packs.append((norm_pack, chan_pack))

    mine = me.astype(jnp.int32)[None]
    up_rows = up_weight.shape[2]
    down_rows = down_weight.shape[1]
    special = size == 32
    clock = []
    mixer_w = [None] * layers
    gated_w = [[None] * PARTS for _ in range(layers)]
    hidden = size * down_rows // PARTS

    def mixer_block(layer):
        return jnp.concatenate([in_weight[layer].T, out_weight[layer]], axis=0)

    def mixer_weights(layer, rows):
        mixer_w[layer] = (
            rows[:, :in_rows].reshape(3 * width, width),
            rows[:, in_rows:].reshape(width, width),
        )

    def gather_mixer(layer, after):
        def done(pieces):
            (rows,) = place_pieces(pieces, (in_rows + out_rows,), mine)
            mixer_weights(layer, rows)

        return gather_steps(mixer_block(layer), after, clock, done)

    def gated_weights(layer, pieces):
        gated_w[layer] = {"pieces": pieces, "rows": down_rows // PARTS}

    def gather_gated(layer, after):
        return gather_steps(all_parts(layer), after, clock, functools.partial(gated_weights, layer))

    def whole_gather(block, *after):
        return lax.all_gather(hold(block, *after), AXES, axis=0)

    def all_parts(layer):
        halved = up_weight[layer].T.reshape(2, PARTS, -1, width)
        own = down_weight[layer].reshape(PARTS, -1, width)
        rows = []
        for part in range(PARTS):
            rows += [halved[0, part], halved[1, part], own[part]]
        return jnp.concatenate(rows, axis=0)

    def go(*names):
        sent = []
        for name in names:
            sent.extend(next(steps[name], ()))
        return sent

    filters = [None] * layers

    def make_filter(layer, *after):
        filters[layer] = filter_forward(
            length,
            packs[layer][1],
            hold(freq_in[layer], *after),
            freq_bias[layer],
            freq_out[layer],
        )

    for layer in range(layers):
        make_filter(layer)
    steps = {}
    if special:
        rows = whole_gather(jnp.concatenate([all_parts(0), mixer_block(0)], axis=0))
        gated_weights(0, [(rows, (None,) * size)])
        mixer_weights(0, rows[:, -in_rows - out_rows :])
    else:
        for layer in range(layers):
            mixer_weights(layer, gather_rows(mixer_block(layer), size, me))
            gated_block = jnp.concatenate([up_weight[layer].T, down_weight[layer]], axis=0)
            gated_rows = gather_rows(gated_block, size, me)
            ups = pieces_of(gated_rows[:, :up_rows].reshape(-1, width), 96)
            downs = pieces_of(gated_rows[:, up_rows:].reshape(-1, width), 96)
            gated_w[layer] = list(zip(ups, downs))

    saved = []
    outputs = []
    for layer in range(layers):
        norm_pack, chan_pack = packs[layer]
        waits = []
        ahead = (layer + 1, "mixer"), (layer + 1, "gated")
        more = special and layer + 1 < layers
        ahead = (layer + 1, "mixer"), (layer + 1, "gated")
        if more:
            steps[ahead[0]] = gather_mixer(layer + 1, [filters[layer][0]])
            go(ahead[0])
            steps[ahead[1]] = gather_gated(layer + 1, [mixer_w[layer][1]])
            go(ahead[1])
            clock[:] = [mixer_w[layer][1]]
            waits = go(ahead[0])
        w_in, w_out = mixer_w[layer]
        middle, second, normed, biased, conv, scale = mixer_forward(
            waits, split, state, norm_pack, chan_pack, w_in, filters[layer][0], w_out
        )
        waits = ()
        clock[:] = [middle]
        waits = []
        if more:
            go(ahead[0])
            go(ahead[0])
            waits = go(ahead[1])
        elif special:
            go((layer, "gated"))
            go((layer, "gated"))
        total = middle
        kept = []
        if special:
            gate, value, total = gated_forward(
                waits,
                mine,
                second,
                gated_w[layer],
                total,
                norm_pack,
                PARTS * hidden,
                True,
                tuple(range(PARTS)),
            )
            clock[:] = [total]
            kept = [(gate, value)]
        else:
            for part in range(PARTS):
                gate, value, total = gated_forward(
                    [], mine, second, gated_w[layer][part], total, norm_pack, hidden, part == 0
                )
                kept.append((gate, value))
        saved.append((state, normed, biased, conv, scale, middle, second, kept))
        outputs.append(total)
        state = total

    gradient = glow = cotangent[0]
    big = [None] * layers
    small = [None] * layers
    moving = {}

    def forward_on(*names):
        sent = []
        for name in names:
            if name in moving:
                sent.extend(next(moving[name], ()))
        return sent

    def whole_scatter(values):
        return lax.psum_scatter(values, AXES, scatter_dimension=0)

    early = []
    nothing = jnp.zeros((8, width), f32)
    for layer in reversed(range(layers)):
        w_in, w_out = mixer_w[layer]
        norm_pack, chan_pack = packs[layer]
        state_in, normed, biased, conv, scale, middle, second, kept = saved[layer]
        passed = nothing
        gated_g = []
        by_steps = special and layer == 0
        owned = [None] * PARTS
        calls = [(part,) for part in range(PARTS)]
        if special and not by_steps:
            calls = [tuple(range(PARTS))]
        for index, taken in enumerate(calls):
            waits = []
            if by_steps:
                waits = forward_on("mixer", "part0")
            elif layer == layers - 1 and index == 0:
                waits = [state]
            if special:
                gate, value = kept[0]
                own = gated_w[layer]
            else:
                gate, value = kept[index]
                own = gated_w[layer][index]
            final = index == len(calls) - 1
            one, two, passed, mlow, sums_two = gated_backward(
                waits,
                mine,
                glow,
                gradient if final else nothing,
                passed,
                second,
                middle if final else nothing,
                norm_pack,
                gate,
                value,
                own,
                index == 0,
                final,
                by_steps and not final,
                taken,
            )
            clock[:] = [sums_two]
            gated_g.append((one, two))
            if by_steps and final:
                owned[index] = whole_scatter(hold_place(one, *early))
            elif by_steps:
                moving[f"part{index}"] = scatter_steps(
                    one, two, clock, functools.partial(owned.__setitem__, index)
                )
        if special and not by_steps:
            rows = whole_scatter(gated_g[0][0])
            early.append(rows)
            owned = [rows[part * rows.shape[0] // PARTS :][: rows.shape[0] // PARTS] for part in range(PARTS)]
        grad_middle = passed
        inner_g = nothing
        lows = []
        found = []
        splits = [1] * (width // CB) if by_steps else [width // CB]
        start = 0
        for index, count in enumerate(splits):
            waits = []
            if by_steps:
                names = [("part0",), ("mixer",), ("part0",)]
                waits = forward_on(*names[min(index, 2)])
                if index == 1:
                    waits += early
            *got, inner_g, freq_g, low = mixer_backward(
                waits,
                start,
                count,
                split,
                mlow,
                normed,
                chan_pack,
                biased,
                conv,
                scale,
                filters[layer][0],
                w_out,
                filters[layer][1],
                freq_out[layer],
                inner_g,
            )
            lows.append(low)
            clock[:] = [freq_g]
            found.append(got)
            start += count
        in_g = jnp.concatenate([got[0] for got in found], axis=1)
        out_g = jnp.concatenate([got[1] for got in found], axis=0)
        chan_g = jnp.concatenate([got[2] for got in found], axis=1)
        mixer_g = jnp.concatenate(
            [in_g.reshape(size, in_rows, width), out_g.reshape(size, out_rows, width)], axis=1
        )

        mixer_own = [None]
        waits = []
        if special:
            order = jnp.arange(size // 2, dtype=jnp.int32) * 2 ^ me
            keep, send = [
                mixer_g.at[places].get(mode="promise_in_bounds") for places in (order, order ^ 1)
            ]
            while forward_on("mixer"):
                pass
            waits = [send, keep]
            moving["mixer"] = scatter_steps(
                keep, send, clock, functools.partial(mixer_own.__setitem__, 0)
            )
        else:
            up_g = jnp.stack([one for one, _ in gated_g], axis=1).reshape(size, -1, width)
            down_g = jnp.stack([two for _, two in gated_g], axis=1).reshape(size, -1, width)
            owned = (scatter_rows(up_g, size, me), scatter_rows(down_g, size, me))
            mixer_own[0] = scatter_rows(mixer_g, size, me)
        gradient, glow, sums_one = norm_finish(
            waits, lows, w_in, state_in, grad_middle, norm_pack
        )
        small[layer] = (chan_g, freq_g, sums_one, sums_two)
        big[layer] = (owned, mixer_own)

    def lines_of(values):
        return -(-values.size // (8 * width)) * 8

    def lined(values):
        lines = lines_of(values)
        flat_values = jnp.pad(values.reshape(-1), (0, lines * width - values.size))
        return flat_values.reshape(lines, width)

    vector = jnp.concatenate([lined(piece) for pieces in small for piece in pieces], axis=0)
    vector = jnp.pad(vector, ((0, -vector.shape[0] % 16), (0, 0)))
    if special:
        vector = hold(vector, send)
    summed = [None]
    sent = []
    moving["small"] = sum_steps(vector, size, me, functools.partial(summed.__setitem__, 0), sent)
    forward_on("mixer", "small")
    sent.extend(forward_on("mixer"))
    clock[:] = sent[:1]
    while forward_on("mixer", "small", "part1", "part0"):
        pass
    vector = summed[0]
    count = sum(lines_of(piece) for piece in small[0])
    vector = vector[: layers * count].reshape(layers, count, width)
    found = []
    start = 0
    for piece in small[0]:
        lines = lines_of(piece)
        part = vector[:, start : start + lines]
        if piece.shape[1] != width:
            part = part.reshape(layers, -1)[:, : piece.size]
        found.append(part.reshape((layers,) + piece.shape))
        start += lines
    chan_g, freq_g, sums_one, sums_two = found
    count = freq_in.shape[1]
    small = [
        jnp.stack([sums_one[:, 0], sums_two[:, 0]], axis=1),
        jnp.stack([sums_one[:, 1], sums_two[:, 1]], axis=1),
        chan_g[:, 0:3].reshape(layers, 3 * width),
        chan_g[:, 3:12].reshape(layers, 3, 3 * width),
        chan_g[:, 12:15],
        chan_g[:, 15],
        freq_g[:, :count],
        jnp.sum(freq_g[:, count:], axis=1),
        chan_g[:, 16:],
        sums_two[:, 2],
        sums_two[:, 3],
    ]

    for layer in range(layers):
        owned, mixer_own = big[layer]
        if special:
            piece = down_rows // PARTS
            up_own = jnp.concatenate(
                [part[at * piece : (at + 1) * piece] for at in range(2) for part in owned], axis=0
            ).astype(f32)
            down_own = jnp.concatenate([part[2 * piece :] for part in owned], axis=0).astype(f32)
        else:
            up_own, down_own = owned
        mixer_rows = mixer_own[0].astype(f32)
        big[layer] = (mixer_rows[:in_rows].T, mixer_rows[in_rows:], up_own.T, down_own)
    big = [jnp.stack([big[layer][index] for layer in range(layers)]) for index in range(4)]
    return (
        jnp.stack(outputs)[:, None],
        gradient[None],
        small[0],
        small[1],
        big[0],
        small[2],
        small[3],
        small[4],
        small[5],
        small[6],
        small[7],
        small[8],
        big[1],
        small[9],
        big[2],
        big[3],
        small[10],
    )


def solution(mesh):
    pairs = P(AXES, None, None)
    columns = P(None, None, AXES)
    rows = P(None, AXES, None)
    in_specs = (
        (pairs, P(AXES), pairs, P(), P(), columns)
        + (P(),) * 7
        + (rows, P(), columns, rows, P())
    )
    out_specs = (
        (P(None, AXES, None, None), pairs, P(), P(), columns)
        + (P(),) * 7
        + (rows, P(), columns, rows, P())
    )
    size = math.prod(mesh.shape.values())
    return jax.shard_map(
        functools.partial(body, size),
        mesh=mesh,
        in_specs=in_specs,
        out_specs=out_specs,
        check_vma=False,
    )
```
